128 devices in a mesh: layer: 32 (over z, x, core), dp: 4 (over y).
Axes of the slice: x: 4, y: 4, z: 4, core: 2. Of those that a mesh axis runs over, the one named last changes fastest.
Arguments:
- images: float32 [4, 56, 56, 128], P('dp'), may hold values from -6 to 6
- kernels: bfloat16 [96, 1152, 128], P('layer'), may hold values from -0.1875 to 0.1875
- damping: float32 [96, 128], P('layer'), may hold values from 0.02 to 4
- cotangent: float32 [4, 56, 56, 128], P('dp'), may hold values from -6 to 6
Outputs:
- slab_ends: float32 [32, 4, 56, 56, 128], P('layer', 'dp')
- coarse_ends: float32 [32, 4, 56, 56, 128], P('layer', 'dp')
- adjoint_starts: float32 [32, 4, 56, 56, 128], P('layer', 'dp')
- adjoint_coarse_starts: float32 [32, 4, 56, 56, 128], P('layer', 'dp')
- gradients: float32 [96, 1152, 128], P('layer')
The draws below stay inside these ranges and needn't reach their ends.
All inputs are finite; a program needn't handle non-finite values.
Results may differ from the reference program's by a relative error of at most 0.0054.
Values sent between devices are 32-bit elements; how exact they have to be, the bound alone decides.
A program may use at most 256 MiB of HBM per device.

```python
import math
import jax
import jax.numpy as jnp
from jax import lax

C = 128
SIDE = 56
SLAB = 3
LAYERS = 96
BATCH = 4
N_LAYER = 32


def block_scale(key, shape, shards, low, top_value):
    def one(axis_at, blocks):
        heights = jax.random.uniform(jax.random.fold_in(jax.random.fold_in(key, 6), axis_at), (blocks,), jnp.float32, low / len(shards), top_value / len(shards))
        return jnp.repeat(jnp.exp(heights), shape[axis_at] // blocks).reshape((-1,) + (1,) * (len(shape) - axis_at - 1))

    loudness = one(*shards[0])
    for cut in shards[1:]:
        loudness = loudness * one(*cut)
    return loudness


def gaussian(own_key, shape, deviation, limit, split=(), kind=jnp.bfloat16):
    array = jax.random.normal(own_key, shape, jnp.float32) * deviation
    if len(split) > 0:
        array = block_scale(own_key, shape, split, -0.22, 0.18) * array
    return jnp.clip(array, min=-limit, max=limit).astype(kind)


def setup_inputs(seed: int = 0) -> dict:
    splits = jax.random.split(jax.random.key(seed), 5)
    return {
        "images": gaussian(splits[0], (BATCH, SIDE, SIDE, C), 1.0, 6.0, ((0, 4),), jnp.float32),
        "kernels": gaussian(splits[1], (LAYERS, 9 * C, C), (9 * C) ** -0.5, 0.1875, ((0, 32),)),
        "damping": jnp.clip(jnp.exp(math.log(4.0) - 5.2983174 * jax.random.uniform(splits[2], (LAYERS, C), jnp.float32) ** block_scale(splits[2], (LAYERS, C), ((0, 32),), -0.2, 0.2)), 0.02, 4.0),
        "cotangent": gaussian(splits[3], (BATCH, SIDE, SIDE, C), 1.0, 6.0, ((0, 4),), jnp.float32),
    }


STEP = 0.125


def patches(field):
    side = field.shape[1]
    padded = jnp.pad(field, ((0, 0), (1, 1), (1, 1), (0, 0)))
    pieces = [padded[:, row_off:row_off + side, col_off:col_off + side, :] for row_off in range(3) for col_off in range(3)]
    return jnp.concatenate(pieces, axis=-1).reshape(-1, 9 * field.shape[3])


def advance(current, kernel, decay):
    columns = patches(current.astype(jnp.bfloat16))
    preact = jnp.dot(columns, kernel, preferred_element_type=jnp.float32).reshape(current.shape)
    activation = jnp.tanh(preact)
    return current + STEP * (activation - decay * current), activation


def retreat(adjoint, activation, kernel_back, decay):
    scaled = (STEP * (1.0 - activation * activation) * adjoint).astype(jnp.bfloat16)
    back_term = jnp.dot(patches(scaled), kernel_back, preferred_element_type=jnp.float32).reshape(adjoint.shape)
    return adjoint - STEP * decay * adjoint + back_term, scaled


def flipped(kernel):
    channels = kernel.shape[1]
    blocks = kernel.reshape(9, channels, channels)[::-1]
    return jnp.swapaxes(blocks, 1, 2).reshape(9 * channels, channels)


def coarse(kernel, decay, layers):
    channels = kernel.shape[1]
    tap_sum = jnp.sum(kernel.astype(jnp.float32).reshape(9, channels, channels), axis=0)
    return jnp.diag(1.0 - layers * STEP * decay) + layers * STEP * tap_sum


def transform(current, matrix):
    flattened = current.reshape(-1, matrix.shape[0])
    return jnp.dot(flattened, matrix, precision=lax.Precision.HIGHEST, preferred_element_type=jnp.float32).reshape(current.shape)


def sweep(current, kernel_set, decay_set):
    for layer_id in range(kernel_set.shape[0]):
        current, _ = advance(current, kernel_set[layer_id], decay_set[layer_id])
    return current


def sweep_back(adjoint, act_set, back_set, decay_set):
    for layer_id in reversed(range(act_set.shape[0])):
        adjoint, _ = retreat(adjoint, act_set[layer_id], back_set[layer_id], decay_set[layer_id])
    return adjoint


def reference(images, kernels, damping, cotangent):
    channels = images.shape[3]
    slab_count = N_LAYER
    kern = kernels.reshape(slab_count, SLAB, 9 * channels, channels)
    decays = damping.reshape(slab_count, SLAB, channels)
    flipped_all = jax.vmap(jax.vmap(flipped))(kern)
    matrices = jax.vmap(lambda kernel_set, decay_set: coarse(kernel_set[0], decay_set[0], SLAB))(kern, decays)

    ends = lax.map(lambda pair: sweep(images, pair[0], pair[1]), (kern, decays))
    start_states = jnp.concatenate([images[None], ends[:-1]], axis=0)

    def second(group):
        start, kernel_set, decay_set, matrix = group
        return sweep(start, kernel_set, decay_set) - transform(start, matrix)

    offsets = lax.map(second, (start_states, kern, decays, matrices))

    def chain_step(carried, group):
        matrix, offset = group
        following = transform(carried, matrix) + offset
        return following, (carried, following)

    _, (begins, coarse_out) = lax.scan(chain_step, images, (matrices, offsets))

    def third(group):
        begin, kernel_set, decay_set = group
        current = begin
        act_list = []
        input_list = []
        for layer_id in range(SLAB):
            input_list.append(current.astype(jnp.bfloat16))
            current, activation = advance(current, kernel_set[layer_id], decay_set[layer_id])
            act_list.append(activation)
        return current, jnp.stack(act_list), jnp.stack(input_list)

    finals, acts, inputs = lax.map(third, (begins, kern, decays))

    heads = lax.map(lambda group: sweep_back(cotangent, group[0], group[1], group[2]), (acts, flipped_all, decays))
    top_states = jnp.concatenate([heads[1:], cotangent[None]], axis=0)

    def adjoint_second(group):
        top, act_set, back_set, decay_set, matrix = group
        return sweep_back(top, act_set, back_set, decay_set) - transform(top, matrix.T)

    back_offsets = lax.map(adjoint_second, (top_states, acts, flipped_all, decays, matrices))

    def back_step(carried, group):
        matrix, offset = group
        following = transform(carried, matrix.T) + offset
        return following, (carried, following)

    _, (adjoint_tops, adjoint_out) = lax.scan(back_step, cotangent, (matrices, back_offsets), reverse=True)

    def third_back(group):
        top, act_set, input_set, back_set, decay_set = group
        adjoint = top
        grad_list = [None] * SLAB
        for layer_id in reversed(range(SLAB)):
            adjoint, scaled = retreat(adjoint, act_set[layer_id], back_set[layer_id], decay_set[layer_id])
            grad_list[layer_id] = lax.dot_general(patches(input_set[layer_id]), scaled.reshape(-1, channels), (((0,), (0,)), ((), ())), preferred_element_type=jnp.float32)
        return adjoint, jnp.stack(grad_list)

    starts_adjoint, grad_all = lax.map(third_back, (adjoint_tops, acts, inputs, flipped_all, decays))
    return finals, coarse_out, starts_adjoint, adjoint_out, grad_all.reshape(slab_count * SLAB, 9 * channels, channels)
```

```python
import functools

import jax
import jax.numpy as jnp
from jax import lax
from jax.experimental import pallas as pl
from jax.experimental.pallas import tpu as pltpu
from jax.sharding import PartitionSpec as P

STEP = 0.125
F32 = jnp.float32
BF16 = jnp.bfloat16
MESH = pl.DeviceIdType.MESH
VMEM_BYTES = 60 * 1024 * 1024
WIDE = 64
GROUP = 4


def coarse(kernel, decay, layers):
    channels = kernel.shape[1]
    tap_sum = jnp.sum(kernel.astype(F32).reshape(9, channels, channels), axis=0)
    return jnp.diag(1.0 - layers * STEP * decay) + layers * STEP * tap_sum


def split(value):
    high = value.astype(BF16)
    return high, (value - high.astype(F32)).astype(BF16)


def pack_matrix(matrix, transposed):
    high, low = split(matrix)
    if transposed:
        top = jnp.concatenate([high, high], axis=1)
        bottom = jnp.concatenate([low, jnp.zeros_like(low)], axis=1)
    else:
        top = jnp.concatenate([high, low], axis=1)
        bottom = jnp.concatenate([high, jnp.zeros_like(low)], axis=1)
    return jnp.concatenate([top, bottom], axis=0)


def times(rows, packed, transposed):
    channels = rows.shape[1]
    both = jnp.concatenate(split(rows), axis=1)
    dims = (((1,), (1 if transposed else 0,)), ((), ()))
    result = lax.dot_general(both, packed, dims, preferred_element_type=F32)
    return result[:, :channels] + result[:, channels:]


def clear_edges(packed):
    zeros = jnp.zeros(packed.shape[3:], packed.dtype)
    for col in range(3):
        packed[col, 0, 0] = zeros
        packed[col, 1, packed.shape[2] - 1] = zeros


def pack_rows(packed, first, even, odd):
    count, side, channels = even.shape
    fill = jnp.zeros((count, WIDE - side, channels), F32)
    for parity, value in ((1, even), (0, odd)):
        start = first if parity == 1 else first + 1
        wide = jnp.concatenate([value, fill], axis=1)
        for col, shift in ((1, 0), (0, 1), (2, WIDE - 1)):
            moved = wide if shift == 0 else pltpu.roll(wide, shift, 1)
            packed[col, parity, pl.ds(start, count)] = moved.astype(BF16)


def pieces(packed, first, count):
    channels = packed.shape[-1]
    rows = count * packed.shape[3]
    out = []
    for col in range(3):
        for parity, ahead in ((1, 0), (0, 1), (0, 0), (1, 1)):
            out.append(packed[col, parity, pl.ds(first + ahead, count)].reshape(rows, channels))
    return out


OFFSETS = (0, 1, -1, 2)


def fill_weights(weights, kernel, backward):
    channels = weights.shape[1] // 2 if not backward else weights.shape[0] // 2
    zero = jnp.zeros((channels, channels), BF16)
    for col in range(3):
        for place, offset in enumerate(OFFSETS):
            at = pl.ds((col * 4 + place) * channels, channels)
            for row in range(2):
                tap = offset - row + 1
                if 0 <= tap <= 2:
                    index = tap * 3 + col
                    block = kernel(8 - index if backward else index).astype(BF16)
                else:
                    block = zero
                out = pl.ds(row * channels, channels)
                if backward:
                    weights[out, at] = block
                else:
                    weights[at, out] = block


def convolve(packed, weights, first, count, side, backward):
    left = jnp.concatenate(pieces(packed, first, count), axis=1)
    dims = (((1,), (1 if backward else 0,)), ((), ()))
    result = lax.dot_general(left, weights[...], dims, preferred_element_type=F32)
    channels = result.shape[1] // 2
    result = result.reshape(count, WIDE, 2 * channels)[:, :side]
    return result[:, :, :channels], result[:, :, channels:]


def each_group(pairs, body):
    def step(index, carry):
        body(index * GROUP)
        return carry

    lax.fori_loop(0, pairs // GROUP, step, 0)


def pack_field(packed, field):
    def body(first):
        part = field[pl.ds(first, GROUP)]
        pack_rows(packed, first, part[:, 0], part[:, 1])

    each_group(field.shape[0], body)


def tap_of(ref, layer, channels):
    return lambda tap: ref[layer, pl.ds(tap * channels, channels), :]


def run_forward(source, target, packs, weights, kernels, damping, gates=None, kept=None):
    layers = kernels.shape[0]
    pairs, _, side, channels = source.shape
    for layer in range(layers):
        now, later = packs[layer % 2], packs[(layer + 1) % 2]
        fill_weights(weights, tap_of(kernels, layer, channels), False)
        decay = damping[layer, :].reshape(1, 1, channels)
        state = source if layer == 0 else target

        def body(first):
            outs = convolve(now, weights, first, GROUP, side, False)
            nexts = []
            for row in range(2):
                act = jnp.tanh(outs[row])
                if gates is not None:
                    gates[layer, pl.ds(first, GROUP), row] = STEP * (1.0 - act * act)
                current = state[pl.ds(first, GROUP), row]
                moved = current + STEP * (act - decay * current)
                target[pl.ds(first, GROUP), row] = moved
                nexts.append(moved)
            if kept is not None:
                kept[layer, 0, pl.ds(first, GROUP)] = now[1, 1, pl.ds(first, GROUP)]
                kept[layer, 1, pl.ds(first, GROUP)] = now[1, 0, pl.ds(first + 1, GROUP)]
            if layer + 1 < layers:
                pack_rows(later, first, nexts[0], nexts[1])

        each_group(pairs, body)


def pack_scaled(packed, gates, layer, adjoint):
    def body(first):
        at = pl.ds(first, GROUP)
        pack_rows(packed, first, gates[layer, at, 0] * adjoint[at, 0], gates[layer, at, 1] * adjoint[at, 1])

    each_group(adjoint.shape[0], body)


def run_backward(source, target, packs, weights, kernels, damping, gates, grads=None, kept=None):
    layers = kernels.shape[0]
    pairs, _, side, channels = source.shape
    pack_scaled(packs[0], gates, layers - 1, source)
    for turn, layer in enumerate(reversed(range(layers))):
        now, later = packs[turn % 2], packs[(turn + 1) % 2]
        fill_weights(weights, tap_of(kernels, layer, channels), True)
        decay = damping[layer, :].reshape(1, 1, channels)
        state = source if turn == 0 else target

        def body(first):
            at = pl.ds(first, GROUP)
            outs = convolve(now, weights, first, GROUP, side, True)
            nexts = []
            for row in range(2):
                current = state[at, row]
                moved = current - STEP * decay * current + outs[row]
                target[at, row] = moved
                if layer > 0:
                    nexts.append(gates[layer - 1, at, row] * moved)
            if layer > 0:
                pack_rows(later, first, nexts[0], nexts[1])

        each_group(pairs, body)
        if grads is not None:
            gradient(now, kept, layer, grads)


def gradient(packed, kept, layer, grads):
    channels = packed.shape[-1]
    pairs = packed.shape[2] - 1
    left = jnp.concatenate([kept[layer, row].reshape(pairs * WIDE, channels) for row in range(2)], axis=1)
    for col in range(3):
        parts = []
        for parity, ahead in ((1, 0), (0, 1), (0, 0), (1, 1)):
            parts.append(packed[col, parity, pl.ds(ahead, pairs)].reshape(pairs * WIDE, channels))
        out = lax.dot_general(
            left, jnp.concatenate(parts, axis=1), (((0,), (0,)), ((), ())), preferred_element_type=F32
        )

        def block(row, offset):
            place = OFFSETS.index(offset)
            return out[row * channels : (row + 1) * channels, place * channels : (place + 1) * channels]

        for tap in range(3):
            total = block(0, 1 - tap) + block(1, 2 - tap)
            index = tap * 3 + (2 - col)
            grads[layer, pl.ds(index * channels, channels), :] = total


def rows_times(source, packed_matrix, transposed, put):
    pairs, _, side, channels = source.shape

    def body(first):
        at = pl.ds(first, GROUP)
        for row in range(2):
            rows = source[at, row].reshape(GROUP * side, channels)
            put(at, row, times(rows, packed_matrix, transposed).reshape(GROUP, side, channels))

    each_group(pairs, body)


def offsets_kernel(first_ref, images, before, kernels, damp_before, damping, matrix, out, start, pack_a, pack_b, weights):
    packs = (pack_a, pack_b)
    for packed in packs:
        clear_edges(packed)
    pack_field(pack_a, images)
    run_forward(images, start, packs, weights, before, damp_before)
    is_first = first_ref[0] == 1

    def choose(first):
        at = pl.ds(first, GROUP)
        start[at] = jnp.where(is_first, images[at], start[at])

    each_group(images.shape[0], choose)
    pack_field(pack_a, start)
    run_forward(start, out, packs, weights, kernels, damping)
    packed_matrix = pack_matrix(matrix[...], False)

    def put(at, row, value):
        out[at, row] = out[at, row] - value

    rows_times(start, packed_matrix, False, put)


def middle_kernel(
    last_ref, begins, offsets, cotangent, kernels, after, damping, damp_after, matrix,
    slab_end, coarse_end, back_offset, gates, kept,
    gates_after, state, pack_a, pack_b, weights, weights_back,
):
    packs = (pack_a, pack_b)
    for packed in packs:
        clear_edges(packed)
    packed_matrix = pack_matrix(matrix[...], False)
    packed_transposed = pack_matrix(matrix[...], True)

    def put(at, row, value):
        coarse_end[at, row] = value + offsets[at, row]

    rows_times(begins, packed_matrix, False, put)
    pack_field(pack_a, begins)
    run_forward(begins, slab_end, packs, weights, kernels, damping, gates, kept)
    pack_field(pack_a, coarse_end)
    run_forward(coarse_end, state, packs, weights, after, damp_after, gates_after)
    run_backward(cotangent, state, packs, weights_back, after, damp_after, gates_after)
    is_last = last_ref[0] == 1

    def choose(first):
        at = pl.ds(first, GROUP)
        state[at] = jnp.where(is_last, cotangent[at], state[at])

    each_group(begins.shape[0], choose)
    run_backward(state, back_offset, packs, weights_back, kernels, damping, gates)

    def put_back(at, row, value):
        back_offset[at, row] = back_offset[at, row] - value

    rows_times(state, packed_transposed, True, put_back)


def final_kernel(
    tops, back_offset, kernels, damping, matrix, gates, kept,
    start, coarse_start, grads,
    pack_a, pack_b, weights,
):
    packs = (pack_a, pack_b)
    for packed in packs:
        clear_edges(packed)
    packed_transposed = pack_matrix(matrix[...], True)

    def put(at, row, value):
        coarse_start[at, row] = value + back_offset[at, row]

    run_backward(tops, start, packs, weights, kernels, damping, gates, grads, kept)
    rows_times(tops, packed_transposed, True, put)


def in_vmem(count, scalars=0):
    return [pl.BlockSpec(memory_space=pltpu.SMEM)] * scalars + [
        pl.BlockSpec(memory_space=pltpu.VMEM)
    ] * count


def local_call(kernel, outs, scratch, *args, scalars=0, name=None):
    return pl.pallas_call(
        kernel,
        out_shape=outs,
        in_specs=in_vmem(len(args) - scalars, scalars),
        out_specs=tuple(in_vmem(len(outs))),
        scratch_shapes=scratch,
        compiler_params=pltpu.CompilerParams(vmem_limit_bytes=VMEM_BYTES),
        name=name,
    )(*args)


def chain_kernel(
    chips, backward, window, seed, terms, matrices, out,
    partner_terms, composed, inbox, outbox, returned, partner_out, packs,
    pair_send, pair_recv, in_send, in_recv, back_send, back_recv, out_send, out_recv,
):
    me = lax.axis_index("layer")
    chip = me // 2
    core = me % 2
    partner = me + 1 - 2 * core
    half = seed.shape[0] // 2
    lead = 1 if backward else 0
    is_lead = core == lead
    tiles = half // 8

    def start_of(other):
        return pl.multiple_of((other * tiles) // chips * 8, 8)

    barrier = pltpu.get_barrier_semaphore()
    pl.semaphore_signal(barrier, inc=1, device_id={"layer": partner}, device_id_type=MESH)

    def greet(step, carry):
        other = lax.rem(chip + step, chips)
        pl.semaphore_signal(barrier, inc=1, device_id={"layer": other * 2 + core}, device_id_type=MESH)
        return carry

    lax.fori_loop(1, chips, greet, 0)
    pl.semaphore_wait(barrier, chips)

    own_rows = pl.ds(pl.multiple_of(core * half, 8), half)
    other_rows = pl.ds(pl.multiple_of((1 - core) * half, 8), half)
    exchange = pltpu.make_async_remote_copy(
        src_ref=terms.at[other_rows],
        dst_ref=partner_terms,
        send_sem=pair_send,
        recv_sem=pair_recv,
        device_id={"layer": partner},
        device_id_type=MESH,
    )
    exchange.start()

    def prepare(index, carry):
        packs[index] = pack_matrix(matrices[index], backward)
        return carry

    lax.fori_loop(0, 2 * chips, prepare, 0)
    lead_slab = 2 * chip + lead
    next_slab = 2 * chip + 1 - lead
    exchange.wait()

    block = half // 7
    base = pl.multiple_of(core * half, 8)

    def lead_terms(at, own_at):
        return jnp.where(is_lead, terms[own_at], partner_terms[at])

    def compose(index, carry):
        at = pl.ds(pl.multiple_of(index * block, 8), block)
        own_at = pl.ds(pl.multiple_of(base + index * block, 8), block)
        own, theirs = terms[own_at], partner_terms[at]
        led = jnp.where(is_lead, own, theirs)
        following = jnp.where(is_lead, theirs, own)
        composed[at] = times(led, packs[next_slab], backward) + following
        return carry

    lax.fori_loop(0, 7, compose, 0)

    def in_copy(other):
        return pltpu.make_async_remote_copy(
            src_ref=composed.at[pl.ds(start_of(other), window)],
            dst_ref=inbox.at[chip],
            send_sem=in_send.at[other],
            recv_sem=in_recv.at[chip],
            device_id={"layer": other * 2 + core},
            device_id_type=MESH,
        )

    def send_in(step, carry):
        in_copy(lax.rem(chip + step, chips)).start()
        return carry

    lax.fori_loop(1, chips, send_in, 0)
    inbox[chip] = composed[pl.ds(start_of(chip), window)]

    def in_arrival(other):
        return pltpu.make_async_remote_copy(
            src_ref=composed.at[pl.ds(start_of(other), window)],
            dst_ref=inbox.at[other],
            send_sem=in_send.at[other],
            recv_sem=in_recv.at[other],
            device_id={"layer": other * 2 + core},
            device_id_type=MESH,
        )

    def back_copy(other):
        return pltpu.make_async_remote_copy(
            src_ref=outbox.at[other],
            dst_ref=returned.at[chip],
            send_sem=back_send.at[other],
            recv_sem=back_recv.at[chip],
            device_id={"layer": other * 2 + core},
            device_id_type=MESH,
        )

    def back_arrival(other):
        return pltpu.make_async_remote_copy(
            src_ref=outbox.at[other],
            dst_ref=returned.at[other],
            send_sem=back_send.at[other],
            recv_sem=back_recv.at[other],
            device_id={"layer": other * 2 + core},
            device_id_type=MESH,
        )

    def scan(step, rows):
        at = chips - 1 - step if backward else step
        outbox[at] = rows

        @pl.when(at != chip)
        def _():
            back_copy(at).start()
            in_arrival(at).wait_recv()

        rows = times(rows, packs[2 * at + lead], backward)
        return times(rows, packs[2 * at + 1 - lead], backward) + inbox[at]

    seed_at = pl.multiple_of(base + start_of(chip), 8)
    lax.fori_loop(0, chips, scan, seed[pl.ds(seed_at, window)])

    def gather(step, carry):
        other = lax.rem(chip + step, chips)
        back_arrival(other).wait_recv()
        partner_terms_at = pl.ds(start_of(other), window)
        leads[partner_terms_at] = returned[other]
        return carry

    leads = composed

    def drain_in(step, carry):
        in_copy(lax.rem(chip + step, chips)).wait_send()
        return carry

    lax.fori_loop(1, chips, drain_in, 0)
    lax.fori_loop(1, chips, gather, 0)
    leads[pl.ds(start_of(chip), window)] = outbox[chip]

    def finish(index, carry):
        at = pl.ds(pl.multiple_of(index * block, 8), block)
        own_at = pl.ds(pl.multiple_of(base + index * block, 8), block)
        led = leads[at]
        following = times(led, packs[lead_slab], backward) + lead_terms(at, own_at)
        out[own_at] = jnp.where(is_lead, led, following)
        leads[at] = jnp.where(is_lead, following, led)
        return carry

    lax.fori_loop(0, 7, finish, 0)
    hand = pltpu.make_async_remote_copy(
        src_ref=leads,
        dst_ref=partner_out,
        send_sem=out_send,
        recv_sem=out_recv,
        device_id={"layer": partner},
        device_id_type=MESH,
    )
    hand.start()

    def drain_back(step, carry):
        back_copy(lax.rem(chip + step, chips)).wait_send()
        return carry

    lax.fori_loop(1, chips, drain_back, 0)
    hand.wait()
    out[other_rows] = partner_out[...]


def run_chain(seed, terms, matrices, backward):
    slabs = matrices.shape[0]
    chips = slabs // 2
    rows, channels = terms.shape
    half = rows // 2
    window = -(-(half // 8) // chips) * 8
    dma = pltpu.SemaphoreType.DMA
    return pl.pallas_call(
        functools.partial(chain_kernel, chips, backward, window),
        out_shape=jax.ShapeDtypeStruct((rows, channels), F32),
        in_specs=in_vmem(3),
        out_specs=in_vmem(1)[0],
        scratch_shapes=[
            pltpu.VMEM((half, channels), F32),
            pltpu.VMEM((half, channels), F32),
            pltpu.VMEM((chips, window, channels), F32),
            pltpu.VMEM((chips, window, channels), F32),
            pltpu.VMEM((chips, window, channels), F32),
            pltpu.VMEM((half, channels), F32),
            pltpu.VMEM((slabs, 2 * channels, 2 * channels), BF16),
            dma, dma, dma((chips,)), dma((chips,)), dma((chips,)), dma((chips,)), dma, dma,
        ],
        compiler_params=pltpu.CompilerParams(
            vmem_limit_bytes=VMEM_BYTES,
            collective_id=2 if backward else 1,
            has_side_effects=True,
        ),
        name="chain_back" if backward else "chain",
    )(seed, terms, matrices)


def per_device(images, kernels, damping, cotangent):
    slab, _, channels = kernels.shape
    side = images.shape[1]
    slabs = lax.axis_size("layer")
    position = lax.axis_index("layer")
    pairs = side // 2
    field = (pairs, 2, side, channels)
    rows = (side * side, channels)

    ahead = [(i, i + 1) for i in range(slabs - 1)]
    behind = [(i + 1, i) for i in range(slabs - 1)]
    kernels_f32 = kernels.astype(F32)
    before = lax.ppermute(kernels_f32, "layer", ahead)
    damp_before = lax.ppermute(damping, "layer", ahead)
    after = lax.ppermute(kernels_f32, "layer", behind)
    damp_after = lax.ppermute(damping, "layer", behind)
    matrix = coarse(kernels[0], damping[0], slab)
    matrices = lax.all_gather(matrix, "layer")

    is_first = (position == 0).astype(jnp.int32).reshape(1)
    is_last = (position == slabs - 1).astype(jnp.int32).reshape(1)
    packed = [pltpu.VMEM((3, 2, pairs + 1, WIDE, channels), BF16)] * 2
    weights = [pltpu.VMEM((12 * channels, 2 * channels), BF16)]
    weights_back = [pltpu.VMEM((2 * channels, 12 * channels), BF16)]
    state = jax.ShapeDtypeStruct(field, F32)
    image_pairs = images.reshape(field)
    cot_pairs = cotangent.reshape(field)

    (offsets,) = local_call(
        offsets_kernel, (state,), [pltpu.VMEM(field, F32)] + packed + weights,
        is_first, image_pairs, before, kernels, damp_before, damping, matrix,
        scalars=1, name="offsets",
    )
    begins = run_chain(images.reshape(rows), offsets.reshape(rows), matrices, False)
    gates_shape = (slab,) + field
    slab_end, coarse_end, back_offsets, gates, kept = local_call(
        middle_kernel,
        (
            state, state, state,
            jax.ShapeDtypeStruct(gates_shape, F32),
            jax.ShapeDtypeStruct((slab, 2, pairs, WIDE, channels), BF16),
        ),
        [pltpu.VMEM(gates_shape, F32), pltpu.VMEM(field, F32)] + packed + weights + weights_back,
        is_last, begins.reshape(field), offsets, cot_pairs, kernels, after, damping, damp_after, matrix,
        scalars=1, name="middle",
    )
    tops = run_chain(cotangent.reshape(rows), back_offsets.reshape(rows), matrices, True)
    adjoint_start, adjoint_coarse, grads = local_call(
        final_kernel,
        (state, state, jax.ShapeDtypeStruct(kernels.shape, F32)),
        packed + weights_back,
        tops.reshape(field), back_offsets, kernels, damping, matrix, gates, kept,
        name="final",
    )
    grads = lax.psum(grads, "dp")
    full = (1,) + images.shape
    return (
        slab_end.reshape(full),
        coarse_end.reshape(full),
        adjoint_start.reshape(full),
        adjoint_coarse.reshape(full),
        grads,
    )


def solution(mesh):
    in_specs = (
        P("dp", None, None, None),
        P("layer", None, None),
        P("layer", None),
        P("dp", None, None, None),
    )
    out_specs = (
        P("layer", "dp", None, None, None),
        P("layer", "dp", None, None, None),
        P("layer", "dp", None, None, None),
        P("layer", "dp", None, None, None),
        P("layer", None, None),
    )
    return jax.shard_map(
        per_device, mesh=mesh, in_specs=in_specs, out_specs=out_specs, check_vma=False
    )
```

```python
import functools

import jax
import jax.numpy as jnp
from jax import lax
from jax.experimental import pallas as pl
from jax.experimental.pallas import tpu as pltpu
from jax.sharding import PartitionSpec as P

STEP = 0.125
F32 = jnp.float32
BF16 = jnp.bfloat16
MESH = pl.DeviceIdType.MESH
VMEM_BYTES = 60 * 1024 * 1024
WIDE = 64
GROUP = 7


def split(value):
    high = value.astype(BF16)
    return high, (value - high.astype(F32)).astype(BF16)


def pack_matrix(matrix, transposed):
    high, low = split(matrix)
    if transposed:
        top = jnp.concatenate([high, high], axis=1)
        bottom = jnp.concatenate([low, jnp.zeros_like(low)], axis=1)
    else:
        top = jnp.concatenate([high, low], axis=1)
        bottom = jnp.concatenate([high, jnp.zeros_like(low)], axis=1)
    return jnp.concatenate([top, bottom], axis=0)


def times(rows, packed, transposed):
    channels = rows.shape[1]
    both = jnp.concatenate(split(rows), axis=1)
    dims = (((1,), (1 if transposed else 0,)), ((), ()))
    result = lax.dot_general(both, packed, dims, preferred_element_type=F32)
    return result[:, :channels] + result[:, channels:]


def clear_edges(packed):
    zeros = jnp.zeros(packed.shape[3:], packed.dtype)
    for col in range(3):
        packed[col, 0, 0] = zeros
        packed[col, 1, packed.shape[2] - 1] = zeros


def pack_rows(packed, first, even, odd):
    count, side, channels = even.shape
    fill = jnp.zeros((count, WIDE - side, channels), F32)
    for parity, value in ((1, even), (0, odd)):
        start = first if parity == 1 else first + 1
        wide = jnp.concatenate([value, fill], axis=1)
        for col, shift in ((1, 0), (0, 1), (2, WIDE - 1)):
            moved = wide if shift == 0 else pltpu.roll(wide, shift, 1)
            packed[col, parity, pl.ds(start, count)] = moved.astype(BF16)


def pieces(packed, first, count):
    channels = packed.shape[-1]
    rows = count * packed.shape[3]
    out = []
    for col in range(3):
        for parity, ahead in ((1, 0), (0, 1), (0, 0), (1, 1)):
            out.append(packed[col, parity, pl.ds(first + ahead, count)].reshape(rows, channels))
    return out


OFFSETS = (0, 1, -1, 2)


def fill_weights(weights, kernel, backward):
    channels = weights.shape[1] // 2 if not backward else weights.shape[0] // 2
    zero = jnp.zeros((channels, channels), BF16)
    for col in range(3):
        for place, offset in enumerate(OFFSETS):
            at = pl.ds((col * 4 + place) * channels, channels)
            for row in range(2):
                tap = offset - row + 1
                if 0 <= tap <= 2:
                    index = tap * 3 + col
                    block = kernel(8 - index if backward else index).astype(BF16)
                else:
                    block = zero
                out = pl.ds(row * channels, channels)
                if backward:
                    weights[out, at] = block
                else:
                    weights[at, out] = block


def convolve(packed, weights, first, count, side, backward):
    left = jnp.concatenate(pieces(packed, first, count), axis=1)
    dims = (((1,), (1 if backward else 0,)), ((), ()))
    result = lax.dot_general(left, weights[...], dims, preferred_element_type=F32)
    channels = result.shape[1] // 2
    result = result.reshape(count, WIDE, 2 * channels)[:, :side]
    return result[:, :, :channels], result[:, :, channels:]


def each_group(pairs, body):
    def step(index, carry):
        body(index * GROUP)
        return carry

    lax.fori_loop(0, pairs // GROUP, step, 0, unroll=True)


def pack_field(packed, field):
    def body(first):
        part = field[pl.ds(first, GROUP)]
        pack_rows(packed, first, part[:, 0], part[:, 1])

    each_group(field.shape[0], body)


def tap_of(ref, layer, channels):
    return lambda tap: ref[layer, pl.ds(tap * channels, channels), :]


def run_forward(source, target, packs, weights, kernels, damping, gates=None, kept=None):
    layers = kernels.shape[0]
    pairs, _, side, channels = source.shape
    for layer in range(layers):
        now, later = packs[layer % 2], packs[(layer + 1) % 2]
        fill_weights(weights, tap_of(kernels, layer, channels), False)
        decay = damping[layer, :].reshape(1, 1, channels)
        state = source if layer == 0 else target

        def body(first):
            outs = convolve(now, weights, first, GROUP, side, False)
            nexts = []
            for row in range(2):
                act = jnp.tanh(outs[row])
                if gates is not None:
                    gates[layer, pl.ds(first, GROUP), row] = STEP * (1.0 - act * act)
                current = state[pl.ds(first, GROUP), row]
                moved = current + STEP * (act - decay * current)
                target[pl.ds(first, GROUP), row] = moved
                nexts.append(moved)
            if kept is not None:
                kept[layer, 0, pl.ds(first, GROUP)] = now[1, 1, pl.ds(first, GROUP)]
                kept[layer, 1, pl.ds(first, GROUP)] = now[1, 0, pl.ds(first + 1, GROUP)]
            if layer + 1 < layers:
                pack_rows(later, first, nexts[0], nexts[1])

        each_group(pairs, body)


def pack_scaled(packed, gates, layer, adjoint):
    def body(first):
        at = pl.ds(first, GROUP)
        pack_rows(packed, first, gates[layer, at, 0] * adjoint[at, 0], gates[layer, at, 1] * adjoint[at, 1])

    each_group(adjoint.shape[0], body)


def retreat_layer(turn, layers, source, target, packs, weights, kernels, damping, gates):
    _, _, side, channels = source.shape
    layer = layers - 1 - turn
    now, later = packs[turn % 2], packs[(turn + 1) % 2]
    fill_weights(weights, tap_of(kernels, layer, channels), True)
    decay = damping[layer, :].reshape(1, 1, channels)
    state = source if turn == 0 else target

    def body(first):
        at = pl.ds(first, GROUP)
        outs = convolve(now, weights, first, GROUP, side, True)
        nexts = []
        for row in range(2):
            current = state[at, row]
            moved = current - STEP * decay * current + outs[row]
            target[at, row] = moved
            if layer > 0:
                nexts.append(gates[layer - 1, at, row] * moved)
        if layer > 0:
            pack_rows(later, first, nexts[0], nexts[1])

    each_group(source.shape[0], body)


def run_backward(source, target, packs, weights, kernels, damping, gates):
    layers = gates.shape[0]
    pack_scaled(packs[0], gates, layers - 1, source)
    for turn in range(layers):
        retreat_layer(turn, layers, source, target, packs, weights, kernels, damping, gates)


def gradient(packed, kept, layer, grads):
    channels = packed.shape[-1]
    pairs = packed.shape[2] - 1
    left = jnp.concatenate([kept[layer, row].reshape(pairs * WIDE, channels) for row in range(2)], axis=1)
    for col in range(3):
        parts = []
        for parity, ahead in ((1, 0), (0, 1), (0, 0), (1, 1)):
            parts.append(packed[col, parity, pl.ds(ahead, pairs)].reshape(pairs * WIDE, channels))
        out = lax.dot_general(
            left, jnp.concatenate(parts, axis=1), (((0,), (0,)), ((), ())), preferred_element_type=F32
        )

        def block(row, offset):
            place = OFFSETS.index(offset)
            return out[row * channels : (row + 1) * channels, place * channels : (place + 1) * channels]

        for tap in range(3):
            total = block(0, 1 - tap) + block(1, 2 - tap)
            index = tap * 3 + (2 - col)
            grads[layer, pl.ds(index * channels, channels), :] = total


def rows_times(source, packed_matrix, transposed, put):
    pairs, _, side, channels = source.shape

    def body(first):
        at = pl.ds(first, GROUP)
        for row in range(2):
            rows = source[at, row].reshape(GROUP * side, channels)
            put(at, row, times(rows, packed_matrix, transposed).reshape(GROUP, side, channels))

    each_group(pairs, body)


def offsets_kernel(first_ref, images, before, kernels, damp_before, damping, matrix, out, start, pack_a, pack_b, weights):
    packs = (pack_a, pack_b)
    for packed in packs:
        clear_edges(packed)
    pack_field(pack_a, images)
    run_forward(images, start, packs, weights, before, damp_before)
    is_first = first_ref[0] == 1

    def choose(first):
        at = pl.ds(first, GROUP)
        start[at] = jnp.where(is_first, images[at], start[at])

    each_group(images.shape[0], choose)
    pack_field(pack_a, start)
    run_forward(start, out, packs, weights, kernels, damping)
    packed_matrix = pack_matrix(matrix[...], False)

    def put(at, row, value):
        out[at, row] = out[at, row] - value

    rows_times(start, packed_matrix, False, put)


def middle_kernel(
    last_ref, begins, offsets, cotangent, kernels, after, damping, damp_after, matrix,
    slab_end, coarse_end, back_offset, gates, kept,
    gates_after, state, pack_a, pack_b, weights, weights_back,
):
    packs = (pack_a, pack_b)
    for packed in packs:
        clear_edges(packed)
    packed_matrix = pack_matrix(matrix[...], False)
    packed_transposed = pack_matrix(matrix[...], True)

    def put(at, row, value):
        coarse_end[at, row] = value + offsets[at, row]

    rows_times(begins, packed_matrix, False, put)
    pack_field(pack_a, begins)
    run_forward(begins, slab_end, packs, weights, kernels, damping, gates, kept)
    pack_field(pack_a, coarse_end)
    run_forward(coarse_end, state, packs, weights, after, damp_after, gates_after)
    run_backward(cotangent, state, packs, weights_back, after, damp_after, gates_after)
    is_last = last_ref[0] == 1

    def choose(first):
        at = pl.ds(first, GROUP)
        state[at] = jnp.where(is_last, cotangent[at], state[at])

    each_group(begins.shape[0], choose)
    run_backward(state, back_offset, packs, weights_back, kernels, damping, gates)

    def put_back(at, row, value):
        back_offset[at, row] = back_offset[at, row] - value

    rows_times(state, packed_transposed, True, put_back)


def final_kernel(
    ring, tops, back_offset, kernels, damping, matrix, gates, kept,
    start, coarse_start, grads,
    pack_a, pack_b, weights, local, total, landed,
    reduce_send, reduce_recv, gather_send, gather_recv,
):
    layers = kernels.shape[0]
    me = lax.axis_index("dp")
    neighbours = (lax.rem(me + 1, ring), lax.rem(me + ring - 1, ring))
    barrier = pltpu.get_barrier_semaphore()
    for neighbour in neighbours:
        pl.semaphore_signal(barrier, inc=1, device_id={"dp": neighbour}, device_id_type=MESH)

    size = kernels.shape[1] // (2 * ring)

    def rows_of(way, step):
        chunk = lax.rem(me + (2 * ring - step if way == 0 else step + ring), ring)
        return pl.ds(pl.multiple_of((way * ring + chunk) * size, 8), size)

    def reduce_copy(layer, way, step):
        slot = (layer * 2 + way) * (ring - 1) + step
        return pltpu.make_async_remote_copy(
            src_ref=local.at[layer, rows_of(way, step)],
            dst_ref=landed.at[slot],
            send_sem=reduce_send.at[slot],
            recv_sem=reduce_recv.at[slot],
            device_id={"dp": neighbours[way]},
            device_id_type=MESH,
        )

    def gather_copy(layer, way, step):
        slot = (layer * 2 + way) * (ring - 1) + step
        rows = rows_of(way, step - 1)
        return pltpu.make_async_remote_copy(
            src_ref=total.at[layer, rows],
            dst_ref=total.at[layer, rows],
            send_sem=gather_send.at[slot],
            recv_sem=gather_recv.at[slot],
            device_id={"dp": neighbours[way]},
            device_id_type=MESH,
        )

    def advance_ring(layer, stage):
        last = ring - 1
        for way in range(2):
            if 1 <= stage <= last:
                slot = (layer * 2 + way) * last + stage - 1
                reduce_copy(layer, way, stage - 1).wait_recv()
                rows = rows_of(way, stage)
                value = local[layer, rows] + landed[slot]
                if stage < last:
                    local[layer, rows] = value
                else:
                    total[layer, rows] = value
            elif stage > last:
                gather_copy(layer, way, stage - last - 1).wait_recv()
            if stage < last:
                reduce_copy(layer, way, stage).start()
            elif stage < 2 * last:
                gather_copy(layer, way, stage - last).start()

    packs = (pack_a, pack_b)
    for packed in packs:
        clear_edges(packed)
    packed_transposed = pack_matrix(matrix[...], True)

    def put(at, row, value):
        coarse_start[at, row] = value + back_offset[at, row]

    stages = 2 * (ring - 1) + 1
    reached = [0] * layers
    pack_scaled(pack_a, gates, layers - 1, tops)
    for turn in range(layers):
        layer = layers - 1 - turn
        gradient(packs[turn % 2], kept, layer, local)
        if turn == 0:
            pl.semaphore_wait(barrier, 2)
        for other in range(turn + 1):
            earlier = layers - 1 - other
            advance_ring(earlier, reached[earlier])
            reached[earlier] += 1
        retreat_layer(turn, layers, tops, start, packs, weights, kernels, damping, gates)
    rows_times(tops, packed_transposed, True, put)
    while min(reached) < stages:
        for layer in reversed(range(layers)):
            if reached[layer] < stages:
                advance_ring(layer, reached[layer])
                reached[layer] += 1
    for layer in range(layers):
        for way in range(2):
            for step in range(ring - 1):
                reduce_copy(layer, way, step).wait_send()
                gather_copy(layer, way, step).wait_send()
    grads[...] = total[...]


def in_vmem(count, scalars=0):
    return [pl.BlockSpec(memory_space=pltpu.SMEM)] * scalars + [
        pl.BlockSpec(memory_space=pltpu.VMEM)
    ] * count


def local_call(kernel, outs, scratch, *args, scalars=0, name=None, collective_id=None):
    return pl.pallas_call(
        kernel,
        out_shape=outs,
        in_specs=in_vmem(len(args) - scalars, scalars),
        out_specs=tuple(in_vmem(len(outs))),
        scratch_shapes=scratch,
        compiler_params=pltpu.CompilerParams(
            vmem_limit_bytes=VMEM_BYTES,
            collective_id=collective_id,
            has_side_effects=collective_id is not None,
        ),
        name=name,
    )(*args)


def chain_kernel(
    chips, ring, backward, window, *refs,
):
    relay = not backward
    if relay:
        seed, terms, matrices, quarter, out, after = refs[:6]
        refs = refs[6:]
        relay_send, relay_recv = refs[-2:]
        refs = refs[:-2]
    else:
        seed, terms, matrices, out = refs[:4]
        refs = refs[4:]
    (
        partner_terms, composed, inbox, outbox, returned, handed, partner_out, packs, own_seed,
        pair_send, pair_recv, in_send, in_recv, back_send, back_recv, out_send, out_recv, seed_sem,
    ) = refs
    me = lax.axis_index("layer")
    line = lax.axis_index("dp")
    chip = me // 2
    core = me % 2
    partner = me + 1 - 2 * core
    half = terms.shape[0] // 2
    lead = 1 if backward else 0
    is_lead = core == lead
    tiles = half // 8

    def start_of(other):
        return pl.multiple_of((other * tiles) // chips * 8, 8)

    def own_rows(other):
        return pl.ds(pl.multiple_of(core * half + start_of(other), 8), window)

    def other_rows(other):
        return pl.ds(pl.multiple_of((1 - core) * half + start_of(other), 8), window)

    def turned(step):
        return lax.rem(chip + step, chips)

    barrier = pltpu.get_barrier_semaphore()
    pl.semaphore_signal(barrier, inc=1, device_id={"layer": partner}, device_id_type=MESH)

    def greet(step, carry):
        pl.semaphore_signal(barrier, inc=1, device_id={"layer": turned(step) * 2 + core}, device_id_type=MESH)
        return carry

    lax.fori_loop(1, chips, greet, 0)
    if relay:
        for step in range(1, ring):
            pl.semaphore_signal(
                barrier, inc=1, device_id={"dp": lax.rem(line + step, ring)}, device_id_type=MESH
            )
    seed_copy = pltpu.make_async_copy(seed.at[own_rows(chip)], own_seed, seed_sem)
    seed_copy.start()
    pl.semaphore_wait(barrier, chips + (ring - 1 if relay else 0))

    def pair_copy(other):
        return pltpu.make_async_remote_copy(
            src_ref=terms.at[other_rows(other)],
            dst_ref=partner_terms.at[other],
            send_sem=pair_send.at[other],
            recv_sem=pair_recv.at[other],
            device_id={"layer": partner},
            device_id_type=MESH,
        )

    def send_pair(step, carry):
        pair_copy(turned(step)).start()
        return carry

    lax.fori_loop(1, chips + 1, send_pair, 0)

    if relay:
        share = quarter.shape[1]

        def relay_copy(step):
            rows = pl.ds(pl.multiple_of(line * share, 8), share)
            return pltpu.make_async_remote_copy(
                src_ref=quarter,
                dst_ref=after.at[:, rows],
                send_sem=relay_send.at[step - 1],
                recv_sem=relay_recv.at[step - 1],
                device_id={"dp": lax.rem(line + step, ring)},
                device_id_type=MESH,
            )

        def relay_arrival(step):
            rows = pl.ds(pl.multiple_of(lax.rem(line + ring - step, ring) * share, 8), share)
            return pltpu.make_async_remote_copy(
                src_ref=quarter,
                dst_ref=after.at[:, rows],
                send_sem=relay_send.at[step - 1],
                recv_sem=relay_recv.at[step - 1],
                device_id={"dp": lax.rem(line + step, ring)},
                device_id_type=MESH,
            )

        for step in range(1, ring):
            relay_copy(step).start()
        after[:, pl.ds(pl.multiple_of(line * share, 8), share)] = quarter[...]

    lead_slab = 2 * chip + lead
    next_slab = 2 * chip + 1 - lead
    packs[next_slab] = pack_matrix(matrices[next_slab], backward)

    def in_copy(other):
        return pltpu.make_async_remote_copy(
            src_ref=composed.at[other],
            dst_ref=inbox.at[chip],
            send_sem=in_send.at[other],
            recv_sem=in_recv.at[chip],
            device_id={"layer": other * 2 + core},
            device_id_type=MESH,
        )

    def in_arrival(other):
        return pltpu.make_async_remote_copy(
            src_ref=composed.at[other],
            dst_ref=inbox.at[other],
            send_sem=in_send.at[other],
            recv_sem=in_recv.at[other],
            device_id={"layer": other * 2 + core},
            device_id_type=MESH,
        )

    def compose(other):
        pair_copy(other).wait_recv()
        own, theirs = terms[own_rows(other)], partner_terms[other]
        led = jnp.where(is_lead, own, theirs)
        following = jnp.where(is_lead, theirs, own)
        return times(led, packs[next_slab], backward) + following

    def compose_send(step, carry):
        other = turned(step)
        composed[other] = compose(other)
        in_copy(other).start()
        return carry

    lax.fori_loop(1, chips, compose_send, 0)
    inbox[chip] = compose(chip)

    def prepare(index, carry):
        packs[index] = pack_matrix(matrices[index], backward)
        return carry

    lax.fori_loop(0, 2 * chips, prepare, 0, unroll=4)

    def back_copy(other):
        return pltpu.make_async_remote_copy(
            src_ref=outbox.at[other],
            dst_ref=returned.at[chip],
            send_sem=back_send.at[other],
            recv_sem=back_recv.at[chip],
            device_id={"layer": other * 2 + core},
            device_id_type=MESH,
        )

    def back_arrival(other):
        return pltpu.make_async_remote_copy(
            src_ref=outbox.at[other],
            dst_ref=returned.at[other],
            send_sem=back_send.at[other],
            recv_sem=back_recv.at[other],
            device_id={"layer": other * 2 + core},
            device_id_type=MESH,
        )

    def scan(step, rows):
        at = chips - 1 - step if backward else step
        outbox[at] = rows

        @pl.when(at != chip)
        def _():
            back_copy(at).start()
            in_arrival(at).wait_recv()

        rows = times(rows, packs[2 * at + lead], backward)
        return times(rows, packs[2 * at + 1 - lead], backward) + inbox[at]

    seed_copy.wait()
    lax.fori_loop(0, chips, scan, own_seed[...])

    def hand_copy(other):
        return pltpu.make_async_remote_copy(
            src_ref=handed.at[other],
            dst_ref=partner_out.at[other],
            send_sem=out_send.at[other],
            recv_sem=out_recv.at[other],
            device_id={"layer": partner},
            device_id_type=MESH,
        )

    def finish(other, led):
        lead_terms = jnp.where(is_lead, terms[own_rows(other)], partner_terms[other])
        following = times(led, packs[lead_slab], backward) + lead_terms
        out[own_rows(other)] = jnp.where(is_lead, led, following)
        handed[other] = jnp.where(is_lead, following, led)
        hand_copy(other).start()

    finish(chip, outbox[chip])

    def finish_next(step, carry):
        other = turned(step)
        back_arrival(other).wait_recv()
        finish(other, returned[other])
        return carry

    lax.fori_loop(1, chips, finish_next, 0)

    def drain(step, carry):
        in_copy(turned(step)).wait_send()
        back_copy(turned(step)).wait_send()
        return carry

    lax.fori_loop(1, chips, drain, 0)

    def collect(step, carry):
        other = turned(step)
        pair_copy(other).wait_send()
        hand_copy(other).wait()
        out[other_rows(other)] = partner_out[other]
        return carry

    lax.fori_loop(0, chips, collect, 0)
    if relay:
        for step in range(1, ring):
            relay_copy(step).wait_send()
            relay_arrival(step).wait_recv()


def run_chain(seed, terms, matrices, backward, ring=0, quarter=None):
    slabs = matrices.shape[0]
    chips = slabs // 2
    rows, channels = terms.shape
    window = -(-(rows // 16) // chips) * 8
    dma = pltpu.SemaphoreType.DMA
    blocks = pltpu.VMEM((chips, window, channels), F32)
    outs = (jax.ShapeDtypeStruct((rows, channels), F32),)
    args = (seed, terms, matrices)
    relay_sems = []
    if quarter is not None:
        layers, share, _ = quarter.shape
        outs += (jax.ShapeDtypeStruct((layers, share * ring, channels), F32),)
        args += (quarter,)
        relay_sems = [dma((ring - 1,)), dma((ring - 1,))]
    return pl.pallas_call(
        functools.partial(chain_kernel, chips, ring, backward, window),
        out_shape=outs,
        in_specs=[pl.BlockSpec(memory_space=pl.ANY)] + in_vmem(len(args) - 1),
        out_specs=tuple(in_vmem(len(outs))),
        scratch_shapes=[blocks] * 7
        + [
            pltpu.VMEM((slabs, 2 * channels, 2 * channels), BF16),
            pltpu.VMEM((window, channels), F32),
        ]
        + [dma((chips,))] * 8
        + [dma]
        + relay_sems,
        compiler_params=pltpu.CompilerParams(
            vmem_limit_bytes=VMEM_BYTES,
            collective_id=2 if backward else 1,
            has_side_effects=True,
        ),
        name="chain_back" if backward else "chain",
    )(*args)


def fetch_kernel(
    chips, ring, kernels, damping, before, damp_before, quarter, damp_after, matrices, own_matrix,
    wide, damp_wide,
    full_send, full_recv, part_send, part_recv, relay_send, relay_recv,
    next_send, next_recv, damp_send, damp_recv, far_send, far_recv, pair_send, pair_recv,
):
    layers, depth, channels = kernels.shape
    share = depth // ring
    slabs = 2 * chips
    me = lax.axis_index("layer")
    line = lax.axis_index("dp")
    chip = me // 2
    core = me % 2
    partner = me + 1 - 2 * core
    across = (core == 1) & (me < slabs - 1)
    from_across = (core == 0) & (me > 0)

    def turned(step):
        return lax.rem(chip + step, chips)

    barrier = pltpu.get_barrier_semaphore()
    pl.semaphore_signal(barrier, inc=1, device_id={"layer": partner}, device_id_type=MESH)

    def greet(step, carry):
        pl.semaphore_signal(barrier, inc=1, device_id={"layer": turned(step) * 2 + core}, device_id_type=MESH)
        return carry

    lax.fori_loop(1, chips, greet, 0)
    for step in range(1, ring):
        pl.semaphore_signal(barrier, inc=1, device_id={"dp": lax.rem(line + step, ring)}, device_id_type=MESH)

    @pl.when(across)
    def _():
        pl.semaphore_signal(barrier, inc=1, device_id={"layer": me + 1}, device_id_type=MESH)

    @pl.when(from_across)
    def _():
        pl.semaphore_signal(barrier, inc=1, device_id={"layer": me - 1}, device_id_type=MESH)

    wide[...] = kernels[...].astype(F32)
    damp_wide[...] = jnp.zeros_like(damp_wide)
    damp_wide[pl.ds(0, layers)] = damping[...]
    pl.semaphore_wait(barrier, chips + ring - 1 + across.astype(jnp.int32) + from_across.astype(jnp.int32))

    own_share = pl.ds(pl.multiple_of(line * share, 8), share)

    def to(source, target, send, recv, device):
        return pltpu.make_async_remote_copy(
            src_ref=source, dst_ref=target, send_sem=send, recv_sem=recv, device_id=device, device_id_type=MESH
        )

    after_slab = {"layer": lax.rem(me + 1, slabs)}
    before_slab = {"layer": lax.rem(me + slabs - 1, slabs)}

    def full_copy(layer):
        return to(wide.at[layer], before.at[layer], full_send.at[layer], full_recv.at[layer], after_slab)

    def part_copy(layer):
        return to(
            wide.at[layer, own_share], before.at[layer, own_share], part_send.at[layer], part_recv.at[layer], after_slab
        )

    def damp_copy(way, target, device):
        return to(damp_wide, target, damp_send.at[way], damp_recv.at[way], device)

    def next_copy():
        return to(wide.at[:, own_share], quarter, next_send, next_recv, before_slab)

    damp_up = damp_copy(0, damp_before, after_slab)
    damp_down = damp_copy(1, damp_after, before_slab)

    @pl.when(core == 0)
    def _():
        damp_up.start()
        for layer in range(layers):
            full_copy(layer).start()

    @pl.when(across)
    def _():
        damp_up.start()
        for layer in range(layers):
            part_copy(layer).start()

    taps = wide[0].reshape(depth // channels, channels, channels)
    tap_sum = taps[0]
    for tap in range(1, depth // channels):
        tap_sum = tap_sum + taps[tap]
    scale = layers * STEP
    line_at = lax.broadcasted_iota(jnp.int32, (channels, channels), 0)
    col_at = lax.broadcasted_iota(jnp.int32, (channels, channels), 1)
    decay = jnp.broadcast_to((1.0 - scale * damping[0, :]).reshape(1, channels), (channels, channels))
    matrix = jnp.where(line_at == col_at, decay, 0.0) + scale * tap_sum
    own_matrix[...] = matrix
    matrices[me] = matrix

    def far_copy(other):
        return to(
            own_matrix, matrices.at[me], far_send.at[other], far_recv.at[chip], {"layer": other * 2 + core}
        )

    def far_arrival(other):
        return to(
            own_matrix, matrices.at[other * 2 + core], far_send.at[other], far_recv.at[other],
            {"layer": other * 2 + core},
        )

    def pair_copy(other):
        slab = other * 2 + core
        return to(matrices.at[slab], matrices.at[slab], pair_send.at[other], pair_recv.at[other], {"layer": partner})

    def pair_arrival(other):
        slab = other * 2 + 1 - core
        return to(matrices.at[slab], matrices.at[slab], pair_send.at[other], pair_recv.at[other], {"layer": partner})

    def send_far(step, carry):
        far_copy(turned(step)).start()
        return carry

    lax.fori_loop(1, chips, send_far, 0)
    pair_copy(chip).start()

    @pl.when(me > 0)
    def _():
        damp_down.start()
        next_copy().start()

    def relay_copy(layer, step):
        return to(
            before.at[layer, own_share], before.at[layer, own_share],
            relay_send.at[layer * ring + step], relay_recv.at[layer * ring + step],
            {"dp": lax.rem(line + step, ring)},
        )

    def relay_arrival(layer, step):
        rows = pl.ds(pl.multiple_of(lax.rem(line + ring - step, ring) * share, 8), share)
        return to(
            before.at[layer, rows], before.at[layer, rows],
            relay_send.at[layer * ring + step], relay_recv.at[layer * ring + step],
            {"dp": lax.rem(line + step, ring)},
        )

    @pl.when(from_across)
    def _():
        for layer in range(layers):
            part_copy(layer).wait_recv()
            for step in range(1, ring):
                relay_copy(layer, step).start()

    def pass_on(step, carry):
        other = turned(step)
        far_arrival(other).wait_recv()
        pair_copy(other).start()
        return carry

    lax.fori_loop(1, chips, pass_on, 0)

    @pl.when(from_across)
    def _():
        for layer in range(layers):
            for step in range(1, ring):
                relay_arrival(layer, step).wait_recv()
                relay_copy(layer, step).wait_send()

    @pl.when(core == 1)
    def _():
        for layer in range(layers):
            full_copy(layer).wait_recv()

    @pl.when(me > 0)
    def _():
        damp_up.wait_recv()
        damp_down.wait_send()
        next_copy().wait_send()

    @pl.when(me == 0)
    def _():
        before[...] = jnp.zeros_like(before)
        damp_before[...] = jnp.zeros_like(damp_before)

    @pl.when(me < slabs - 1)
    def _():
        damp_up.wait_send()
        damp_down.wait_recv()
        next_copy().wait_recv()

    @pl.when(me == slabs - 1)
    def _():
        quarter[...] = jnp.zeros_like(quarter)
        damp_after[...] = jnp.zeros_like(damp_after)

    @pl.when(core == 0)
    def _():
        for layer in range(layers):
            full_copy(layer).wait_send()

    @pl.when(across)
    def _():
        for layer in range(layers):
            part_copy(layer).wait_send()

    def settle(step, carry):
        other = turned(step)
        far_copy(other).wait_send()
        return carry

    lax.fori_loop(1, chips, settle, 0)

    def settle_pair(step, carry):
        other = turned(step)
        pair_copy(other).wait_send()
        pair_arrival(other).wait_recv()
        return carry

    lax.fori_loop(0, chips, settle_pair, 0)


def run_fetch(kernels, damping, slabs, ring):
    chips = slabs // 2
    layers, depth, channels = kernels.shape
    dma = pltpu.SemaphoreType.DMA
    outs = (
        jax.ShapeDtypeStruct(kernels.shape, F32),
        jax.ShapeDtypeStruct((8, channels), F32),
        jax.ShapeDtypeStruct((layers, depth // ring, channels), F32),
        jax.ShapeDtypeStruct((8, channels), F32),
        jax.ShapeDtypeStruct((slabs, channels, channels), F32),
        jax.ShapeDtypeStruct((channels, channels), F32),
    )
    return pl.pallas_call(
        functools.partial(fetch_kernel, chips, ring),
        out_shape=outs,
        in_specs=in_vmem(2),
        out_specs=tuple(in_vmem(len(outs))),
        scratch_shapes=[pltpu.VMEM(kernels.shape, F32), pltpu.VMEM((8, channels), F32)]
        + [dma((layers,))] * 4
        + [dma((layers * ring,))] * 2
        + [dma, dma, dma((2,)), dma((2,))]
        + [dma((chips,))] * 4,
        compiler_params=pltpu.CompilerParams(
            vmem_limit_bytes=VMEM_BYTES, collective_id=3, has_side_effects=True
        ),
        name="fetch",
    )(kernels, damping)


def per_device(images, kernels, damping, cotangent):
    slab, _, channels = kernels.shape
    side = images.shape[1]
    slabs = lax.axis_size("layer")
    position = lax.axis_index("layer")
    pairs = side // 2
    field = (pairs, 2, side, channels)
    rows = (side * side, channels)

    ring = lax.axis_size("dp")
    before, damp_before, quarter, damp_after, matrices, matrix = run_fetch(kernels, damping, slabs, ring)

    is_first = (position == 0).astype(jnp.int32).reshape(1)
    is_last = (position == slabs - 1).astype(jnp.int32).reshape(1)
    packed = [pltpu.VMEM((3, 2, pairs + 1, WIDE, channels), BF16)] * 2
    weights = [pltpu.VMEM((12 * channels, 2 * channels), BF16)]
    weights_back = [pltpu.VMEM((2 * channels, 12 * channels), BF16)]
    state = jax.ShapeDtypeStruct(field, F32)
    image_pairs = images.reshape(field)
    cot_pairs = cotangent.reshape(field)

    (offsets,) = local_call(
        offsets_kernel, (state,), [pltpu.VMEM(field, F32)] + packed + weights,
        is_first, image_pairs, before, kernels, damp_before, damping, matrix,
        scalars=1, name="offsets",
    )
    begins, after = run_chain(images.reshape(rows), offsets.reshape(rows), matrices, False, ring, quarter)
    gates_shape = (slab,) + field
    slab_end, coarse_end, back_offsets, gates, kept = local_call(
        middle_kernel,
        (
            state, state, state,
            jax.ShapeDtypeStruct(gates_shape, F32),
            jax.ShapeDtypeStruct((slab, 2, pairs, WIDE, channels), BF16),
        ),
        [pltpu.VMEM(gates_shape, F32), pltpu.VMEM(field, F32)] + packed + weights + weights_back,
        is_last, begins.reshape(field), offsets, cot_pairs, kernels, after, damping, damp_after, matrix,
        scalars=1, name="middle",
    )
    (tops,) = run_chain(cotangent.reshape(rows), back_offsets.reshape(rows), matrices, True)
    moves = slab * 2 * (ring - 1)
    adjoint_start, adjoint_coarse, grads = local_call(
        functools.partial(final_kernel, ring),
        (state, state, jax.ShapeDtypeStruct(kernels.shape, F32)),
        packed
        + weights_back
        + [
            pltpu.VMEM(kernels.shape, F32),
            pltpu.VMEM(kernels.shape, F32),
            pltpu.VMEM((moves, kernels.shape[1] // (2 * ring), channels), F32),
        ]
        + [pltpu.SemaphoreType.DMA((moves,))] * 4,
        tops.reshape(field), back_offsets, kernels, damping, matrix, gates, kept,
        name="final", collective_id=4,
    )
    full = (1,) + images.shape
    return (
        slab_end.reshape(full),
        coarse_end.reshape(full),
        adjoint_start.reshape(full),
        adjoint_coarse.reshape(full),
        grads,
    )


def solution(mesh):
    in_specs = (
        P("dp", None, None, None),
        P("layer", None, None),
        P("layer", None),
        P("dp", None, None, None),
    )
    out_specs = (
        P("layer", "dp", None, None, None),
        P("layer", "dp", None, None, None),
        P("layer", "dp", None, None, None),
        P("layer", "dp", None, None, None),
        P("layer", None, None),
    )
    return jax.shard_map(
        per_device, mesh=mesh, in_specs=in_specs, out_specs=out_specs, check_vma=False
    )
```

```python
import functools

import jax
import jax.numpy as jnp
from jax import lax
from jax.experimental import pallas as pl
from jax.experimental.pallas import tpu as pltpu
from jax.sharding import PartitionSpec as P

STEP = 0.125
F32 = jnp.float32
BF16 = jnp.bfloat16
MESH = pl.DeviceIdType.MESH
VMEM_BYTES = 60 * 1024 * 1024
WIDE = 64
GROUP = 7


def split(value):
    high = value.astype(BF16)
    return high, (value - high.astype(F32)).astype(BF16)


def pack_matrix(matrix, transposed):
    high, low = split(matrix)
    if transposed:
        top = jnp.concatenate([high, high], axis=1)
        bottom = jnp.concatenate([low, jnp.zeros_like(low)], axis=1)
    else:
        top = jnp.concatenate([high, low], axis=1)
        bottom = jnp.concatenate([high, jnp.zeros_like(low)], axis=1)
    return jnp.concatenate([top, bottom], axis=0)


def times(rows, packed, transposed):
    channels = rows.shape[1]
    both = jnp.concatenate(split(rows), axis=1)
    dims = (((1,), (1 if transposed else 0,)), ((), ()))
    result = lax.dot_general(both, packed, dims, preferred_element_type=F32)
    return result[:, :channels] + result[:, channels:]


def clear_edges(packed):
    zeros = jnp.zeros(packed.shape[3:], packed.dtype)
    for col in range(3):
        packed[col, 0, 0] = zeros
        packed[col, 1, packed.shape[2] - 1] = zeros


def pack_rows(packed, first, even, odd):
    count, side, channels = even.shape
    fill = jnp.zeros((count, WIDE - side, channels), F32)
    for parity, value in ((1, even), (0, odd)):
        start = first if parity == 1 else first + 1
        wide = jnp.concatenate([value, fill], axis=1)
        for col, shift in ((1, 0), (0, 1), (2, WIDE - 1)):
            moved = wide if shift == 0 else pltpu.roll(wide, shift, 1)
            packed[col, parity, pl.ds(start, count)] = moved.astype(BF16)


def pieces(packed, first, count):
    channels = packed.shape[-1]
    rows = count * packed.shape[3]
    out = []
    for col in range(3):
        for parity, ahead in ((1, 0), (0, 1), (0, 0), (1, 1)):
            out.append(packed[col, parity, pl.ds(first + ahead, count)].reshape(rows, channels))
    return out


OFFSETS = (0, 1, -1, 2)


def fill_weights(weights, kernel, backward):
    channels = weights.shape[1] // 2 if not backward else weights.shape[0] // 2
    zero = jnp.zeros((channels, channels), BF16)
    for col in range(3):
        for place, offset in enumerate(OFFSETS):
            at = pl.ds((col * 4 + place) * channels, channels)
            for row in range(2):
                tap = offset - row + 1
                if 0 <= tap <= 2:
                    index = tap * 3 + col
                    block = kernel(8 - index if backward else index).astype(BF16)
                else:
                    block = zero
                out = pl.ds(row * channels, channels)
                if backward:
                    weights[out, at] = block
                else:
                    weights[at, out] = block


def convolve(packed, weights, first, count, side, backward):
    left = jnp.concatenate(pieces(packed, first, count), axis=1)
    dims = (((1,), (1 if backward else 0,)), ((), ()))
    result = lax.dot_general(left, weights[...], dims, preferred_element_type=F32)
    channels = result.shape[1] // 2
    result = result.reshape(count, WIDE, 2 * channels)[:, :side]
    return result[:, :, :channels], result[:, :, channels:]


def each_group(pairs, body):
    def step(index, carry):
        body(index * GROUP)
        return carry

    lax.fori_loop(0, pairs // GROUP, step, 0, unroll=True)


def rows_at(first, side):
    return pl.ds(pl.multiple_of(first * 2 * side, 8), GROUP * 2 * side)


def pair_rows(value, side):
    value = value.reshape(GROUP, 2, side, value.shape[-1])
    return value[:, 0], value[:, 1]


def flat_rows(even, odd):
    return jnp.stack([even, odd], axis=1).reshape(-1, even.shape[-1])


def pack_field(packed, field):
    pairs = packed.shape[2] - 1

    def body(first):
        even, odd = pair_rows(field[rows_at(first, 2 * pairs)], 2 * pairs)
        pack_rows(packed, first, even, odd)

    each_group(pairs, body)


def tap_of(ref, layer, channels):
    return lambda tap: ref[layer, pl.ds(tap * channels, channels), :]


def advance_layer(layer, layers, source, target, packs, weights, kernels, damping, gates=None, kept=None):
    channels = source.shape[-1]
    pairs = packs[0].shape[2] - 1
    side = 2 * pairs
    now, later = packs[layer % 2], packs[(layer + 1) % 2]
    fill_weights(weights, tap_of(kernels, layer, channels), False)
    decay = damping[layer, :].reshape(1, 1, channels)
    state = source if layer == 0 else target

    def body(first):
        at = rows_at(first, side)
        outs = convolve(now, weights, first, GROUP, side, False)
        nexts, slopes = [], []
        for out, current in zip(outs, pair_rows(state[at], side)):
            act = jnp.tanh(out)
            slopes.append(STEP * (1.0 - act * act))
            nexts.append(current + STEP * (act - decay * current))
        target[at] = flat_rows(*nexts)
        if gates is not None:
            gates[layer, at] = flat_rows(*slopes)
        if kept is not None:
            kept[layer, 0, pl.ds(first, GROUP)] = now[1, 1, pl.ds(first, GROUP)]
            kept[layer, 1, pl.ds(first, GROUP)] = now[1, 0, pl.ds(first + 1, GROUP)]
        if layer + 1 < layers:
            pack_rows(later, first, *nexts)

    each_group(pairs, body)


def run_forward(source, target, packs, weights, kernels, damping, gates=None, kept=None):
    layers = kernels.shape[0]
    for layer in range(layers):
        advance_layer(layer, layers, source, target, packs, weights, kernels, damping, gates, kept)


def pack_scaled(packed, gates, layer, adjoint):
    pairs = packed.shape[2] - 1

    def body(first):
        at = rows_at(first, 2 * pairs)
        pack_rows(packed, first, *pair_rows(gates[layer, at] * adjoint[at], 2 * pairs))

    each_group(pairs, body)


def retreat_layer(turn, layers, source, target, packs, weights, kernels, damping, gates):
    channels = source.shape[-1]
    pairs = packs[0].shape[2] - 1
    side = 2 * pairs
    layer = layers - 1 - turn
    now, later = packs[turn % 2], packs[(turn + 1) % 2]
    fill_weights(weights, tap_of(kernels, layer, channels), True)
    decay = damping[layer, :].reshape(1, 1, channels)
    state = source if turn == 0 else target

    def body(first):
        at = rows_at(first, side)
        outs = convolve(now, weights, first, GROUP, side, True)
        nexts = []
        for out, current in zip(outs, pair_rows(state[at], side)):
            nexts.append(current - STEP * decay * current + out)
        target[at] = flat_rows(*nexts)
        if layer > 0:
            scaled = [gate * moved for gate, moved in zip(pair_rows(gates[layer - 1, at], side), nexts)]
            pack_rows(later, first, *scaled)

    each_group(pairs, body)


def run_backward(source, target, packs, weights, kernels, damping, gates):
    layers = gates.shape[0]
    pack_scaled(packs[0], gates, layers - 1, source)
    for turn in range(layers):
        retreat_layer(turn, layers, source, target, packs, weights, kernels, damping, gates)


def gradient(packed, kept, layer, grads):
    channels = packed.shape[-1]
    pairs = packed.shape[2] - 1
    left = jnp.concatenate([kept[layer, row].reshape(pairs * WIDE, channels) for row in range(2)], axis=1)
    for col in range(3):
        parts = []
        for parity, ahead in ((1, 0), (0, 1), (0, 0), (1, 1)):
            parts.append(packed[col, parity, pl.ds(ahead, pairs)].reshape(pairs * WIDE, channels))
        out = lax.dot_general(
            left, jnp.concatenate(parts, axis=1), (((0,), (0,)), ((), ())), preferred_element_type=F32
        )

        def block(row, offset):
            place = OFFSETS.index(offset)
            return out[row * channels : (row + 1) * channels, place * channels : (place + 1) * channels]

        for tap in range(3):
            total = block(0, 1 - tap) + block(1, 2 - tap)
            index = tap * 3 + (2 - col)
            grads[layer, pl.ds(index * channels, channels), :] = total


def rows_times(source, packed_matrix, transposed, put):
    parts = 7
    size = source.shape[0] // parts

    def body(index, carry):
        at = pl.ds(pl.multiple_of(index * size, 8), size)
        put(at, times(source[at], packed_matrix, transposed))
        return carry

    lax.fori_loop(0, parts, body, 0, unroll=True)


def choose_rows(flag, chosen, target):
    @pl.when(flag)
    def _():
        target[...] = chosen[...]


def middle_kernel(
    last_ref, begins, offsets, cotangent, kernels, after, damping, damp_after, matrix,
    slab_end, coarse_end, back_offset, gates, kept,
    gates_after, state, pack_a, pack_b, weights, weights_back,
):
    packs = (pack_a, pack_b)
    for packed in packs:
        clear_edges(packed)
    packed_matrix = pack_matrix(matrix[...], False)
    packed_transposed = pack_matrix(matrix[...], True)

    def put(at, value):
        coarse_end[at] = value + offsets[at]

    rows_times(begins, packed_matrix, False, put)
    pack_field(pack_a, begins)
    run_forward(begins, slab_end, packs, weights, kernels, damping, gates, kept)
    pack_field(pack_a, coarse_end)
    run_forward(coarse_end, state, packs, weights, after, damp_after, gates_after)
    run_backward(cotangent, state, packs, weights_back, after, damp_after, gates_after)
    is_last = last_ref[0] == 1
    choose_rows(is_last, cotangent, state)
    run_backward(state, back_offset, packs, weights_back, kernels, damping, gates)

    def put_back(at, value):
        back_offset[at] = back_offset[at] - value

    rows_times(state, packed_transposed, True, put_back)


def final_kernel(
    ring, tops, kernels, damping, matrix, back_hbm, gates_hbm, kept_hbm,
    start_hbm, coarse_hbm, grads_hbm,
    pack_a, pack_b, weights, back_offset, gates, kept, start, coarse_start, local, total, landed,
    reduce_send, reduce_recv, gather_send, gather_recv, load_sems, store_sems,
):
    layers = kernels.shape[0]
    me = lax.axis_index("dp")
    neighbours = (lax.rem(me + 1, ring), lax.rem(me + ring - 1, ring))
    barrier = pltpu.get_barrier_semaphore()
    for neighbour in neighbours:
        pl.semaphore_signal(barrier, inc=1, device_id={"dp": neighbour}, device_id_type=MESH)

    loads = []
    for layer in reversed(range(layers)):
        loads.append(pltpu.make_async_copy(gates_hbm.at[layer], gates.at[layer], load_sems.at[2 * layer]))
        loads.append(pltpu.make_async_copy(kept_hbm.at[layer], kept.at[layer], load_sems.at[2 * layer + 1]))
    loads.append(pltpu.make_async_copy(back_hbm, back_offset, load_sems.at[2 * layers]))
    for load in loads:
        load.start()
    size = kernels.shape[1] // (2 * ring)

    def rows_of(way, step):
        chunk = lax.rem(me + (2 * ring - step if way == 0 else step + ring), ring)
        return pl.ds(pl.multiple_of((way * ring + chunk) * size, 8), size)

    def reduce_copy(layer, way, step):
        slot = (layer * 2 + way) * (ring - 1) + step
        return pltpu.make_async_remote_copy(
            src_ref=local.at[layer, rows_of(way, step)],
            dst_ref=landed.at[slot],
            send_sem=reduce_send.at[slot],
            recv_sem=reduce_recv.at[slot],
            device_id={"dp": neighbours[way]},
            device_id_type=MESH,
        )

    def gather_copy(layer, way, step):
        slot = (layer * 2 + way) * (ring - 1) + step
        rows = rows_of(way, step - 1)
        return pltpu.make_async_remote_copy(
            src_ref=total.at[layer, rows],
            dst_ref=total.at[layer, rows],
            send_sem=gather_send.at[slot],
            recv_sem=gather_recv.at[slot],
            device_id={"dp": neighbours[way]},
            device_id_type=MESH,
        )

    def advance_ring(layer, stage):
        last = ring - 1
        for way in range(2):
            if 1 <= stage <= last:
                slot = (layer * 2 + way) * last + stage - 1
                reduce_copy(layer, way, stage - 1).wait_recv()
                rows = rows_of(way, stage)
                value = local[layer, rows] + landed[slot]
                if stage < last:
                    local[layer, rows] = value
                else:
                    total[layer, rows] = value
            elif stage > last:
                gather_copy(layer, way, stage - last - 1).wait_recv()
            if stage < last:
                reduce_copy(layer, way, stage).start()
            elif stage < 2 * last:
                gather_copy(layer, way, stage - last).start()

    packs = (pack_a, pack_b)
    for packed in packs:
        clear_edges(packed)
    packed_transposed = pack_matrix(matrix[...], True)

    def put(at, value):
        coarse_start[at] = value + back_offset[at]

    stages = 2 * (ring - 1) + 1
    reached = [0] * layers
    loads[0].wait()
    pack_scaled(pack_a, gates, layers - 1, tops)
    for turn in range(layers):
        layer = layers - 1 - turn
        loads[2 * turn + 1].wait()
        gradient(packs[turn % 2], kept, layer, local)
        if turn == 0:
            pl.semaphore_wait(barrier, 2)
        for other in range(turn + 1):
            earlier = layers - 1 - other
            advance_ring(earlier, reached[earlier])
            reached[earlier] += 1
        if layer > 0:
            loads[2 * turn + 2].wait()
        retreat_layer(turn, layers, tops, start, packs, weights, kernels, damping, gates)
    stores = [pltpu.make_async_copy(start, start_hbm, store_sems.at[layers])]
    stores[0].start()
    for layer in range(layers):
        advance_ring(layer, reached[layer])
        reached[layer] += 1
    loads[2 * layers].wait()
    rows_times(tops, packed_transposed, True, put)
    stores.append(pltpu.make_async_copy(coarse_start, coarse_hbm, store_sems.at[layers + 1]))
    stores[1].start()
    while min(reached) < stages:
        for layer in range(layers):
            if reached[layer] < stages:
                advance_ring(layer, reached[layer])
                reached[layer] += 1
                if reached[layer] == stages:
                    store = pltpu.make_async_copy(total.at[layer], grads_hbm.at[layer], store_sems.at[layer])
                    store.start()
                    stores.append(store)
    for layer in range(layers):
        for way in range(2):
            for step in range(ring - 1):
                reduce_copy(layer, way, step).wait_send()
                gather_copy(layer, way, step).wait_send()
    for store in stores:
        store.wait()


def in_vmem(count, scalars=0):
    return [pl.BlockSpec(memory_space=pltpu.SMEM)] * scalars + [
        pl.BlockSpec(memory_space=pltpu.VMEM)
    ] * count


def local_call(kernel, outs, scratch, *args, scalars=0, name=None):
    return pl.pallas_call(
        kernel,
        out_shape=outs,
        in_specs=in_vmem(len(args) - scalars, scalars),
        out_specs=tuple(in_vmem(len(outs))),
        scratch_shapes=scratch,
        compiler_params=pltpu.CompilerParams(vmem_limit_bytes=VMEM_BYTES),
        name=name,
    )(*args)


def nothing():
    pass


def chain_steps(
    chips, backward, window, seed, terms, matrices, out, scratch, pair_ready=nothing, all_ready=nothing
):
    (
        partner_terms, composed, inbox, outbox, returned, handed, partner_out, packs,
        pair_send, pair_recv, in_send, in_recv, back_send, back_recv, out_send, out_recv,
    ) = scratch
    me = lax.axis_index("layer")
    chip = me // 2
    core = me % 2
    partner = me + 1 - 2 * core
    half = terms.shape[0] // 2
    lead = 1 if backward else 0
    is_lead = core == lead
    tiles = half // 8

    def start_of(other):
        return pl.multiple_of((other * tiles) // chips * 8, 8)

    def own_rows(other):
        return pl.ds(pl.multiple_of(core * half + start_of(other), 8), window)

    def other_rows(other):
        return pl.ds(pl.multiple_of((1 - core) * half + start_of(other), 8), window)

    def turned(step):
        return lax.rem(chip + step, chips)

    def pair_copy(other):
        return pltpu.make_async_remote_copy(
            src_ref=terms.at[other_rows(other)],
            dst_ref=partner_terms.at[other],
            send_sem=pair_send.at[other],
            recv_sem=pair_recv.at[other],
            device_id={"layer": partner},
            device_id_type=MESH,
        )

    def send_pair(step, carry):
        pair_copy(turned(step)).start()
        return carry

    lax.fori_loop(1, chips + 1, send_pair, 0)

    lead_slab = 2 * chip + lead
    next_slab = 2 * chip + 1 - lead
    pair_ready()
    packs[next_slab] = pack_matrix(matrices[next_slab], backward)

    def in_copy(other):
        return pltpu.make_async_remote_copy(
            src_ref=composed.at[other],
            dst_ref=inbox.at[chip],
            send_sem=in_send.at[other],
            recv_sem=in_recv.at[chip],
            device_id={"layer": other * 2 + core},
            device_id_type=MESH,
        )

    def in_arrival(other):
        return pltpu.make_async_remote_copy(
            src_ref=composed.at[other],
            dst_ref=inbox.at[other],
            send_sem=in_send.at[other],
            recv_sem=in_recv.at[other],
            device_id={"layer": other * 2 + core},
            device_id_type=MESH,
        )

    def compose(other):
        pair_copy(other).wait_recv()
        own, theirs = terms[own_rows(other)], partner_terms[other]
        led = jnp.where(is_lead, own, theirs)
        following = jnp.where(is_lead, theirs, own)
        return times(led, packs[next_slab], backward) + following

    def compose_send(step, carry):
        other = turned(step)
        composed[other] = compose(other)
        in_copy(other).start()
        return carry

    lax.fori_loop(1, chips, compose_send, 0)
    inbox[chip] = compose(chip)

    all_ready()

    def prepare(index, carry):
        packs[index] = pack_matrix(matrices[index], backward)
        return carry

    lax.fori_loop(0, 2 * chips, prepare, 0, unroll=4)

    def back_copy(other):
        return pltpu.make_async_remote_copy(
            src_ref=outbox.at[other],
            dst_ref=returned.at[chip],
            send_sem=back_send.at[other],
            recv_sem=back_recv.at[chip],
            device_id={"layer": other * 2 + core},
            device_id_type=MESH,
        )

    def back_arrival(other):
        return pltpu.make_async_remote_copy(
            src_ref=outbox.at[other],
            dst_ref=returned.at[other],
            send_sem=back_send.at[other],
            recv_sem=back_recv.at[other],
            device_id={"layer": other * 2 + core},
            device_id_type=MESH,
        )

    def scan(step, rows):
        at = chips - 1 - step if backward else step
        outbox[at] = rows

        @pl.when(at != chip)
        def _():
            back_copy(at).start()
            in_arrival(at).wait_recv()

        rows = times(rows, packs[2 * at + lead], backward)
        return times(rows, packs[2 * at + 1 - lead], backward) + inbox[at]

    lax.fori_loop(0, chips, scan, seed[own_rows(chip)])

    def hand_copy(other):
        return pltpu.make_async_remote_copy(
            src_ref=handed.at[other],
            dst_ref=partner_out.at[other],
            send_sem=out_send.at[other],
            recv_sem=out_recv.at[other],
            device_id={"layer": partner},
            device_id_type=MESH,
        )

    def finish(other, led):
        lead_terms = jnp.where(is_lead, terms[own_rows(other)], partner_terms[other])
        following = times(led, packs[lead_slab], backward) + lead_terms
        out[own_rows(other)] = jnp.where(is_lead, led, following)
        handed[other] = jnp.where(is_lead, following, led)
        hand_copy(other).start()

    finish(chip, outbox[chip])

    def finish_next(step, carry):
        other = turned(step)
        back_arrival(other).wait_recv()
        finish(other, returned[other])
        return carry

    lax.fori_loop(1, chips, finish_next, 0)

    def drain(step, carry):
        in_copy(turned(step)).wait_send()
        back_copy(turned(step)).wait_send()
        return carry

    lax.fori_loop(1, chips, drain, 0)

    def collect(step, carry):
        other = turned(step)
        pair_copy(other).wait_send()
        hand_copy(other).wait()
        out[other_rows(other)] = partner_out[other]
        return carry

    lax.fori_loop(0, chips, collect, 0)

def chain_scratch(rows, slabs, channels):
    chips = slabs // 2
    window = -(-(rows // 16) // chips) * 8
    blocks = pltpu.VMEM((chips, window, channels), F32)
    packs = pltpu.VMEM((slabs, 2 * channels, 2 * channels), BF16)
    return window, [blocks] * 7 + [packs] + [pltpu.SemaphoreType.DMA((chips,))] * 8


def greet_chain(chips):
    me = lax.axis_index("layer")
    barrier = pltpu.get_barrier_semaphore()
    pl.semaphore_signal(barrier, inc=1, device_id={"layer": me + 1 - 2 * (me % 2)}, device_id_type=MESH)

    def greet(step, carry):
        other = lax.rem(me // 2 + step, chips) * 2 + me % 2
        pl.semaphore_signal(barrier, inc=1, device_id={"layer": other}, device_id_type=MESH)
        return carry

    lax.fori_loop(1, chips, greet, 0)


def chain_back_kernel(chips, window, seed, terms, matrices, out, *scratch):
    greet_chain(chips)
    pl.semaphore_wait(pltpu.get_barrier_semaphore(), chips)
    chain_steps(chips, True, window, seed, terms, matrices, out, scratch)


def run_chain_back(seed, terms, matrices):
    slabs, channels, _ = matrices.shape
    window, scratch = chain_scratch(terms.shape[0], slabs, channels)
    return pl.pallas_call(
        functools.partial(chain_back_kernel, slabs // 2, window),
        out_shape=jax.ShapeDtypeStruct(terms.shape, F32),
        in_specs=in_vmem(3),
        out_specs=in_vmem(1)[0],
        scratch_shapes=scratch,
        compiler_params=pltpu.CompilerParams(
            vmem_limit_bytes=VMEM_BYTES, collective_id=2, has_side_effects=True
        ),
        name="chain_back",
    )(seed, terms, matrices)


def forward_kernel(
    chips, ring, window, images, kernels, damping,
    begins, offsets, after, damp_after, matrices, own_matrix,
    wide, damp_wide, before, damp_before, quarter, start, pack_a, pack_b, weights,
    full_send, full_recv, part_send, part_recv, relay_send, relay_recv,
    next_send, next_recv, damp_send, damp_recv, far_send, far_recv, pair_send, pair_recv,
    after_send, after_recv, *chain,
):
    layers, depth, channels = kernels.shape
    share = depth // ring
    slabs = 2 * chips
    me = lax.axis_index("layer")
    line = lax.axis_index("dp")
    chip = me // 2
    core = me % 2
    partner = me + 1 - 2 * core
    across = (core == 1) & (me < slabs - 1)
    from_across = (core == 0) & (me > 0)

    def turned(step):
        return lax.rem(chip + step, chips)

    barrier = pltpu.get_barrier_semaphore()
    greet_chain(chips)
    for step in range(1, ring):
        pl.semaphore_signal(barrier, inc=1, device_id={"dp": lax.rem(line + step, ring)}, device_id_type=MESH)

    @pl.when(across)
    def _():
        pl.semaphore_signal(barrier, inc=1, device_id={"layer": me + 1}, device_id_type=MESH)

    @pl.when(from_across)
    def _():
        pl.semaphore_signal(barrier, inc=1, device_id={"layer": me - 1}, device_id_type=MESH)

    wide[...] = kernels[...].astype(F32)
    damp_wide[...] = jnp.zeros_like(damp_wide)
    damp_wide[pl.ds(0, layers)] = damping[...]
    packs = (pack_a, pack_b)
    for packed in packs:
        clear_edges(packed)
    pl.semaphore_wait(barrier, chips + ring - 1 + across.astype(jnp.int32) + from_across.astype(jnp.int32))

    own_share = pl.ds(pl.multiple_of(line * share, 8), share)

    def to(source, target, send, recv, device):
        return pltpu.make_async_remote_copy(
            src_ref=source, dst_ref=target, send_sem=send, recv_sem=recv, device_id=device, device_id_type=MESH
        )

    after_slab = {"layer": lax.rem(me + 1, slabs)}
    before_slab = {"layer": lax.rem(me + slabs - 1, slabs)}

    def full_copy(layer):
        return to(wide.at[layer], before.at[layer], full_send.at[layer], full_recv.at[layer], after_slab)

    def part_copy(layer):
        return to(
            wide.at[layer, own_share], before.at[layer, own_share], part_send.at[layer], part_recv.at[layer], after_slab
        )

    def damp_copy(way, target, device):
        return to(damp_wide, target, damp_send.at[way], damp_recv.at[way], device)

    def next_copy():
        return to(wide.at[:, own_share], quarter, next_send, next_recv, before_slab)

    damp_up = damp_copy(0, damp_before, after_slab)
    damp_down = damp_copy(1, damp_after, before_slab)

    @pl.when(core == 0)
    def _():
        damp_up.start()
        for layer in range(layers):
            full_copy(layer).start()

    @pl.when(across)
    def _():
        damp_up.start()
        for layer in range(layers):
            part_copy(layer).start()

    pack_field(pack_a, images)

    taps = wide[0].reshape(depth // channels, channels, channels)
    tap_sum = taps[0]
    for tap in range(1, depth // channels):
        tap_sum = tap_sum + taps[tap]
    scale = layers * STEP
    line_at = lax.broadcasted_iota(jnp.int32, (channels, channels), 0)
    col_at = lax.broadcasted_iota(jnp.int32, (channels, channels), 1)
    decay = jnp.broadcast_to((1.0 - scale * damping[0, :]).reshape(1, channels), (channels, channels))
    matrix = jnp.where(line_at == col_at, decay, 0.0) + scale * tap_sum
    own_matrix[...] = matrix
    matrices[me] = matrix

    def far_copy(other):
        return to(
            own_matrix, matrices.at[me], far_send.at[other], far_recv.at[chip], {"layer": other * 2 + core}
        )

    def far_arrival(other):
        return to(
            own_matrix, matrices.at[other * 2 + core], far_send.at[other], far_recv.at[other],
            {"layer": other * 2 + core},
        )

    def pair_copy(other):
        slab = other * 2 + core
        return to(matrices.at[slab], matrices.at[slab], pair_send.at[other], pair_recv.at[other], {"layer": partner})

    def pair_arrival(other):
        slab = other * 2 + 1 - core
        return to(matrices.at[slab], matrices.at[slab], pair_send.at[other], pair_recv.at[other], {"layer": partner})

    def send_far(step, carry):
        far_copy(turned(step)).start()
        return carry

    def relay_copy(layer, step):
        return to(
            before.at[layer, own_share], before.at[layer, own_share],
            relay_send.at[layer * ring + step], relay_recv.at[layer * ring + step],
            {"dp": lax.rem(line + step, ring)},
        )

    def relay_arrival(layer, step):
        rows = pl.ds(pl.multiple_of(lax.rem(line + ring - step, ring) * share, 8), share)
        return to(
            before.at[layer, rows], before.at[layer, rows],
            relay_send.at[layer * ring + step], relay_recv.at[layer * ring + step],
            {"dp": lax.rem(line + step, ring)},
        )

    @pl.when(from_across)
    def _():
        for layer in range(layers):
            part_copy(layer).wait_recv()
            for step in range(1, ring):
                relay_copy(layer, step).start()

    lax.fori_loop(1, chips, send_far, 0)
    pair_copy(chip).start()

    @pl.when(me > 0)
    def _():
        damp_down.start()
        next_copy().start()

    @pl.when(me == 0)
    def _():
        before[...] = jnp.zeros_like(before)
        damp_before[...] = jnp.zeros_like(damp_before)

    @pl.when(me > 0)
    def _():
        damp_up.wait_recv()

    for layer in range(layers):

        @pl.when(from_across)
        def _():
            for step in range(1, ring):
                relay_arrival(layer, step).wait_recv()

        @pl.when(core == 1)
        def _():
            full_copy(layer).wait_recv()

        advance_layer(layer, layers, images, start, packs, weights, before, damp_before)

    choose_rows(me == 0, images, start)

    @pl.when(me < slabs - 1)
    def _():
        next_copy().wait_recv()

    @pl.when(me == slabs - 1)
    def _():
        quarter[...] = jnp.zeros_like(quarter)

    def after_rows(step):
        return pl.ds(pl.multiple_of(lax.rem(line + ring - step, ring) * share, 8), share)

    def after_copy(step):
        return to(
            quarter, after.at[:, own_share], after_send.at[step - 1], after_recv.at[step - 1],
            {"dp": lax.rem(line + step, ring)},
        )

    def after_arrival(step):
        return to(
            quarter, after.at[:, after_rows(step)], after_send.at[step - 1], after_recv.at[step - 1],
            {"dp": lax.rem(line + step, ring)},
        )

    for step in range(1, ring):
        after_copy(step).start()
    after[:, own_share] = quarter[...]

    pack_field(pack_a, start)
    run_forward(start, offsets, packs, weights, kernels, damping)
    packed_matrix = pack_matrix(matrix, False)

    def put(at, value):
        offsets[at] = offsets[at] - value

    rows_times(start, packed_matrix, False, put)

    def pass_on(step, carry):
        other = turned(step)
        far_arrival(other).wait_recv()
        pair_copy(other).start()
        return carry

    def pair_ready():
        pair_arrival(chip).wait_recv()

    def all_ready():
        lax.fori_loop(1, chips, pass_on, 0)

        def arrived(step, carry):
            pair_arrival(turned(step)).wait_recv()
            return carry

        lax.fori_loop(1, chips, arrived, 0)

    chain_steps(chips, False, window, images, offsets, matrices, begins, chain, pair_ready, all_ready)

    @pl.when(from_across)
    def _():
        for layer in range(layers):
            for step in range(1, ring):
                relay_copy(layer, step).wait_send()

    @pl.when(me > 0)
    def _():
        damp_down.wait_send()
        next_copy().wait_send()

    @pl.when(me < slabs - 1)
    def _():
        damp_up.wait_send()
        damp_down.wait_recv()

    @pl.when(me == slabs - 1)
    def _():
        damp_after[...] = jnp.zeros_like(damp_after)

    @pl.when(core == 0)
    def _():
        for layer in range(layers):
            full_copy(layer).wait_send()

    @pl.when(across)
    def _():
        for layer in range(layers):
            part_copy(layer).wait_send()

    def settle(step, carry):
        far_copy(turned(step)).wait_send()
        return carry

    lax.fori_loop(1, chips, settle, 0)

    def settle_pair(step, carry):
        pair_copy(turned(step)).wait_send()
        return carry

    lax.fori_loop(0, chips, settle_pair, 0)
    for step in range(1, ring):
        after_copy(step).wait_send()
        after_arrival(step).wait_recv()


def run_forward_kernel(images, kernels, damping, slabs, ring, packed, weights):
    chips = slabs // 2
    layers, depth, channels = kernels.shape
    dma = pltpu.SemaphoreType.DMA
    window, chain = chain_scratch(images.shape[0], slabs, channels)
    field = jax.ShapeDtypeStruct(images.shape, F32)
    outs = (
        field,
        field,
        jax.ShapeDtypeStruct(kernels.shape, F32),
        jax.ShapeDtypeStruct((8, channels), F32),
        jax.ShapeDtypeStruct((slabs, channels, channels), F32),
        jax.ShapeDtypeStruct((channels, channels), F32),
    )
    return pl.pallas_call(
        functools.partial(forward_kernel, chips, ring, window),
        out_shape=outs,
        in_specs=in_vmem(3),
        out_specs=tuple(in_vmem(len(outs))),
        scratch_shapes=[
            pltpu.VMEM(kernels.shape, F32),
            pltpu.VMEM((8, channels), F32),
            pltpu.VMEM(kernels.shape, F32),
            pltpu.VMEM((8, channels), F32),
            pltpu.VMEM((layers, depth // ring, channels), F32),
            pltpu.VMEM(images.shape, F32),
        ]
        + packed
        + weights
        + [dma((layers,))] * 4
        + [dma((layers * ring,))] * 2
        + [dma, dma, dma((2,)), dma((2,))]
        + [dma((chips,))] * 4
        + [dma((ring - 1,))] * 2
        + chain,
        compiler_params=pltpu.CompilerParams(
            vmem_limit_bytes=VMEM_BYTES, collective_id=1, has_side_effects=True
        ),
        name="forward",
    )(images, kernels, damping)


def place_kernel(*refs):
    half = len(refs) // 2
    for source, target in zip(refs[:half], refs[half:]):
        target[...] = source[...]


def place(*arrays):
    parts = 4

    def specs():
        return [pl.BlockSpec((a.shape[0] // parts, a.shape[1]), lambda i: (i, 0)) for a in arrays]

    return pl.pallas_call(
        place_kernel,
        grid=(parts,),
        out_shape=[jax.ShapeDtypeStruct(a.shape, a.dtype) for a in arrays],
        in_specs=specs(),
        out_specs=specs(),
        compiler_params=pltpu.CompilerParams(vmem_limit_bytes=VMEM_BYTES),
        name="place",
    )(*arrays)


def run_final(tops, kernels, damping, matrix, back_offsets, gates, kept, ring, packed, weights):
    layers, depth, channels = kernels.shape
    moves = layers * 2 * (ring - 1)
    dma = pltpu.SemaphoreType.DMA
    state = jax.ShapeDtypeStruct(tops.shape, F32)
    anywhere = pl.BlockSpec(memory_space=pl.ANY)
    return pl.pallas_call(
        functools.partial(final_kernel, ring),
        out_shape=(state, state, jax.ShapeDtypeStruct(kernels.shape, F32)),
        in_specs=in_vmem(4) + [anywhere] * 3,
        out_specs=(anywhere,) * 3,
        scratch_shapes=packed
        + weights
        + [
            pltpu.VMEM(tops.shape, F32),
            pltpu.VMEM(gates.shape, F32),
            pltpu.VMEM(kept.shape, BF16),
            pltpu.VMEM(tops.shape, F32),
            pltpu.VMEM(tops.shape, F32),
            pltpu.VMEM(kernels.shape, F32),
            pltpu.VMEM(kernels.shape, F32),
            pltpu.VMEM((moves, depth // (2 * ring), channels), F32),
        ]
        + [dma((moves,))] * 4
        + [dma((2 * layers + 1,)), dma((layers + 2,))],
        compiler_params=pltpu.CompilerParams(
            vmem_limit_bytes=VMEM_BYTES, collective_id=4, has_side_effects=True
        ),
        name="final",
    )(tops, kernels, damping, matrix, back_offsets, gates, kept)


def per_device(images, kernels, damping, cotangent):
    slab, depth, channels = kernels.shape
    side = images.shape[1]
    slabs = lax.axis_size("layer")
    ring = lax.axis_size("dp")
    position = lax.axis_index("layer")
    pairs = side // 2
    flat = (side * side, channels)
    images_flat, cot_flat = images.reshape(flat), cotangent.reshape(flat)
    is_last = (position == slabs - 1).astype(jnp.int32).reshape(1)
    packed = [pltpu.VMEM((3, 2, pairs + 1, WIDE, channels), BF16)] * 2
    weights = [pltpu.VMEM((12 * channels, 2 * channels), BF16)]
    weights_back = [pltpu.VMEM((2 * channels, 12 * channels), BF16)]
    state = jax.ShapeDtypeStruct(flat, F32)

    begins, offsets, after, damp_after, matrices, matrix = run_forward_kernel(
        images_flat, kernels, damping, slabs, ring, packed, weights
    )
    gates_shape = (slab,) + flat
    slab_end, coarse_end, back_offsets, gates, kept = local_call(
        middle_kernel,
        (
            state, state, state,
            jax.ShapeDtypeStruct(gates_shape, F32),
            jax.ShapeDtypeStruct((slab, 2, pairs, WIDE, channels), BF16),
        ),
        [pltpu.VMEM(gates_shape, F32), pltpu.VMEM(flat, F32)] + packed + weights + weights_back,
        is_last, begins, offsets, cot_flat, kernels, after, damping, damp_after, matrix,
        scalars=1, name="middle",
    )
    tops = run_chain_back(cot_flat, back_offsets, matrices)
    adjoint_start, adjoint_coarse, grads = run_final(
        tops, kernels, damping, matrix, back_offsets, gates, kept, ring, packed, weights_back
    )
    adjoint_start, adjoint_coarse, grads = place(
        adjoint_start, adjoint_coarse, grads.reshape(slab * depth, channels)
    )
    full = (1,) + images.shape
    return (
        slab_end.reshape(full),
        coarse_end.reshape(full),
        adjoint_start.reshape(full),
        adjoint_coarse.reshape(full),
        grads.reshape(kernels.shape),
    )


def solution(mesh):
    in_specs = (
        P("dp", None, None, None),
        P("layer", None, None),
        P("layer", None),
        P("dp", None, None, None),
    )
    out_specs = (
        P("layer", "dp", None, None, None),
        P("layer", "dp", None, None, None),
        P("layer", "dp", None, None, None),
        P("layer", "dp", None, None, None),
        P("layer", None, None),
    )
    return jax.shard_map(
        per_device, mesh=mesh, in_specs=in_specs, out_specs=out_specs, check_vma=False
    )
```

```python
import functools

import jax
import jax.numpy as jnp
from jax import lax
from jax.experimental import pallas as pl
from jax.experimental.pallas import tpu as pltpu
from jax.sharding import PartitionSpec as P

STEP = 0.125
F32 = jnp.float32
BF16 = jnp.bfloat16
MESH = pl.DeviceIdType.MESH
VMEM_BYTES = 60 * 1024 * 1024
WIDE = 64
GROUP = 7


def split(value):
    high = value.astype(BF16)
    return high, (value - high.astype(F32)).astype(BF16)


def pack_matrix(matrix, transposed):
    high, low = split(matrix)
    if transposed:
        top = jnp.concatenate([high, high], axis=1)
        bottom = jnp.concatenate([low, jnp.zeros_like(low)], axis=1)
    else:
        top = jnp.concatenate([high, low], axis=1)
        bottom = jnp.concatenate([high, jnp.zeros_like(low)], axis=1)
    return jnp.concatenate([top, bottom], axis=0)


def times(rows, packed, transposed):
    channels = rows.shape[1]
    both = jnp.concatenate(split(rows), axis=1)
    dims = (((1,), (1 if transposed else 0,)), ((), ()))
    result = lax.dot_general(both, packed, dims, preferred_element_type=F32)
    return result[:, :channels] + result[:, channels:]


def clear_edges(packed):
    zeros = jnp.zeros(packed.shape[3:], packed.dtype)
    for col in range(3):
        packed[col, 0, 0] = zeros
        packed[col, 1, packed.shape[2] - 1] = zeros


def pack_rows(packed, first, even, odd):
    count, side, channels = even.shape
    fill = jnp.zeros((count, WIDE - side, channels), F32)
    for parity, value in ((1, even), (0, odd)):
        start = first if parity == 1 else first + 1
        wide = jnp.concatenate([value, fill], axis=1)
        for col, shift in ((1, 0), (0, 1), (2, WIDE - 1)):
            moved = wide if shift == 0 else pltpu.roll(wide, shift, 1)
            packed[col, parity, pl.ds(start, count)] = moved.astype(BF16)


def pieces(packed, first, count):
    channels = packed.shape[-1]
    rows = count * packed.shape[3]
    out = []
    for col in range(3):
        for parity, ahead in ((1, 0), (0, 1), (0, 0), (1, 1)):
            out.append(packed[col, parity, pl.ds(first + ahead, count)].reshape(rows, channels))
    return out


OFFSETS = (0, 1, -1, 2)


def fill_weights(weights, kernel, backward):
    channels = weights.shape[1] // 2 if not backward else weights.shape[0] // 2
    zero = jnp.zeros((channels, channels), BF16)
    for col in range(3):
        for place, offset in enumerate(OFFSETS):
            at = pl.ds((col * 4 + place) * channels, channels)
            for row in range(2):
                tap = offset - row + 1
                if 0 <= tap <= 2:
                    index = tap * 3 + col
                    block = kernel(8 - index if backward else index).astype(BF16)
                else:
                    block = zero
                out = pl.ds(row * channels, channels)
                if backward:
                    weights[out, at] = block
                else:
                    weights[at, out] = block


def convolve(packed, weights, first, count, side, backward):
    left = jnp.concatenate(pieces(packed, first, count), axis=1)
    dims = (((1,), (1 if backward else 0,)), ((), ()))
    result = lax.dot_general(left, weights[...], dims, preferred_element_type=F32)
    channels = result.shape[1] // 2
    result = result.reshape(count, WIDE, 2 * channels)[:, :side]
    return result[:, :, :channels], result[:, :, channels:]


def each_group(pairs, body):
    def step(index, carry):
        body(index * GROUP)
        return carry

    lax.fori_loop(0, pairs // GROUP, step, 0, unroll=True)


def rows_at(first, side):
    return pl.ds(pl.multiple_of(first * 2 * side, 8), GROUP * 2 * side)


def pair_rows(value, side):
    value = value.reshape(GROUP, 2, side, value.shape[-1])
    return value[:, 0], value[:, 1]


def flat_rows(even, odd):
    return jnp.stack([even, odd], axis=1).reshape(-1, even.shape[-1])


def pack_field(packed, field):
    pairs = packed.shape[2] - 1

    def body(first):
        even, odd = pair_rows(field[rows_at(first, 2 * pairs)], 2 * pairs)
        pack_rows(packed, first, even, odd)

    each_group(pairs, body)


def tap_of(ref, layer, channels):
    return lambda tap: ref[layer, pl.ds(tap * channels, channels), :]


def advance_layer(layer, layers, source, target, packs, weights, kernels, damping, gates=None, kept=None):
    channels = source.shape[-1]
    pairs = packs[0].shape[2] - 1
    side = 2 * pairs
    now, later = packs[layer % 2], packs[(layer + 1) % 2]
    fill_weights(weights, tap_of(kernels, layer, channels), False)
    decay = damping[layer, :].reshape(1, 1, channels)
    state = source if layer == 0 else target

    def body(first):
        at = rows_at(first, side)
        outs = convolve(now, weights, first, GROUP, side, False)
        nexts, slopes = [], []
        for out, current in zip(outs, pair_rows(state[at], side)):
            act = jnp.tanh(out)
            slopes.append(STEP * (1.0 - act * act))
            nexts.append(current + STEP * (act - decay * current))
        target[at] = flat_rows(*nexts)
        if gates is not None:
            gates[layer, at] = flat_rows(*slopes)
        if kept is not None:
            kept[layer, 0, pl.ds(first, GROUP)] = now[1, 1, pl.ds(first, GROUP)]
            kept[layer, 1, pl.ds(first, GROUP)] = now[1, 0, pl.ds(first + 1, GROUP)]
        if layer + 1 < layers:
            pack_rows(later, first, *nexts)

    each_group(pairs, body)


def run_forward(source, target, packs, weights, kernels, damping, gates=None, kept=None):
    layers = kernels.shape[0]
    for layer in range(layers):
        advance_layer(layer, layers, source, target, packs, weights, kernels, damping, gates, kept)


def pack_scaled(packed, gates, layer, adjoint):
    pairs = packed.shape[2] - 1

    def body(first):
        at = rows_at(first, 2 * pairs)
        pack_rows(packed, first, *pair_rows(gates[layer, at] * adjoint[at], 2 * pairs))

    each_group(pairs, body)


def retreat_layer(turn, layers, source, target, packs, weights, kernels, damping, gates):
    channels = source.shape[-1]
    pairs = packs[0].shape[2] - 1
    side = 2 * pairs
    layer = layers - 1 - turn
    now, later = packs[turn % 2], packs[(turn + 1) % 2]
    fill_weights(weights, tap_of(kernels, layer, channels), True)
    decay = damping[layer, :].reshape(1, 1, channels)
    state = source if turn == 0 else target

    def body(first):
        at = rows_at(first, side)
        outs = convolve(now, weights, first, GROUP, side, True)
        nexts = []
        for out, current in zip(outs, pair_rows(state[at], side)):
            nexts.append(current - STEP * decay * current + out)
        target[at] = flat_rows(*nexts)
        if layer > 0:
            scaled = [gate * moved for gate, moved in zip(pair_rows(gates[layer - 1, at], side), nexts)]
            pack_rows(later, first, *scaled)

    each_group(pairs, body)


def run_backward(source, target, packs, weights, kernels, damping, gates):
    layers = gates.shape[0]
    pack_scaled(packs[0], gates, layers - 1, source)
    for turn in range(layers):
        retreat_layer(turn, layers, source, target, packs, weights, kernels, damping, gates)


def gradient(packed, kept, layer, grads):
    channels = packed.shape[-1]
    pairs = packed.shape[2] - 1
    left = jnp.concatenate([kept[layer, row].reshape(pairs * WIDE, channels) for row in range(2)], axis=1)
    for col in range(3):
        parts = []
        for parity, ahead in ((1, 0), (0, 1), (0, 0), (1, 1)):
            parts.append(packed[col, parity, pl.ds(ahead, pairs)].reshape(pairs * WIDE, channels))
        out = lax.dot_general(
            left, jnp.concatenate(parts, axis=1), (((0,), (0,)), ((), ())), preferred_element_type=F32
        )

        def block(row, offset):
            place = OFFSETS.index(offset)
            return out[row * channels : (row + 1) * channels, place * channels : (place + 1) * channels]

        for tap in range(3):
            total = block(0, 1 - tap) + block(1, 2 - tap)
            index = tap * 3 + (2 - col)
            grads[layer, pl.ds(index * channels, channels), :] = total


def rows_times(source, packed_matrix, transposed, put):
    parts = 7
    size = source.shape[0] // parts

    def body(index, carry):
        at = pl.ds(pl.multiple_of(index * size, 8), size)
        put(at, times(source[at], packed_matrix, transposed))
        return carry

    lax.fori_loop(0, parts, body, 0, unroll=True)


def choose_rows(flag, chosen, target):
    @pl.when(flag)
    def _():
        target[...] = chosen[...]


def final_kernel(
    ring, tops, kernels, damping, matrix, back_hbm, gates_hbm, kept_hbm,
    start_hbm, coarse_hbm, grads_hbm,
    pack_a, pack_b, weights, back_offset, gates, kept, start, coarse_start, local, total, landed,
    reduce_send, reduce_recv, gather_send, gather_recv, load_sems, store_sems,
):
    layers = kernels.shape[0]
    me = lax.axis_index("dp")
    neighbours = (lax.rem(me + 1, ring), lax.rem(me + ring - 1, ring))
    barrier = pltpu.get_barrier_semaphore()
    for neighbour in neighbours:
        pl.semaphore_signal(barrier, inc=1, device_id={"dp": neighbour}, device_id_type=MESH)

    loads = []
    for layer in reversed(range(layers)):
        loads.append(pltpu.make_async_copy(gates_hbm.at[layer], gates.at[layer], load_sems.at[2 * layer]))
        loads.append(pltpu.make_async_copy(kept_hbm.at[layer], kept.at[layer], load_sems.at[2 * layer + 1]))
    loads.append(pltpu.make_async_copy(back_hbm, back_offset, load_sems.at[2 * layers]))
    for load in loads:
        load.start()
    size = kernels.shape[1] // (2 * ring)

    def rows_of(way, step):
        chunk = lax.rem(me + (2 * ring - step if way == 0 else step + ring), ring)
        return pl.ds(pl.multiple_of((way * ring + chunk) * size, 8), size)

    def reduce_copy(layer, way, step):
        slot = (layer * 2 + way) * (ring - 1) + step
        return pltpu.make_async_remote_copy(
            src_ref=local.at[layer, rows_of(way, step)],
            dst_ref=landed.at[slot],
            send_sem=reduce_send.at[slot],
            recv_sem=reduce_recv.at[slot],
            device_id={"dp": neighbours[way]},
            device_id_type=MESH,
        )

    def gather_copy(layer, way, step):
        slot = (layer * 2 + way) * (ring - 1) + step
        rows = rows_of(way, step - 1)
        return pltpu.make_async_remote_copy(
            src_ref=total.at[layer, rows],
            dst_ref=total.at[layer, rows],
            send_sem=gather_send.at[slot],
            recv_sem=gather_recv.at[slot],
            device_id={"dp": neighbours[way]},
            device_id_type=MESH,
        )

    def advance_ring(layer, stage):
        last = ring - 1
        for way in range(2):
            if 1 <= stage <= last:
                slot = (layer * 2 + way) * last + stage - 1
                reduce_copy(layer, way, stage - 1).wait_recv()
                rows = rows_of(way, stage)
                value = local[layer, rows] + landed[slot]
                if stage < last:
                    local[layer, rows] = value
                else:
                    total[layer, rows] = value
            elif stage > last:
                gather_copy(layer, way, stage - last - 1).wait_recv()
            if stage < last:
                reduce_copy(layer, way, stage).start()
            elif stage < 2 * last:
                gather_copy(layer, way, stage - last).start()

    packs = (pack_a, pack_b)
    for packed in packs:
        clear_edges(packed)
    packed_transposed = pack_matrix(matrix[...], True)

    def put(at, value):
        coarse_start[at] = value + back_offset[at]

    stages = 2 * (ring - 1) + 1
    reached = [0] * layers
    loads[0].wait()
    pack_scaled(pack_a, gates, layers - 1, tops)
    for turn in range(layers):
        layer = layers - 1 - turn
        loads[2 * turn + 1].wait()
        gradient(packs[turn % 2], kept, layer, local)
        if turn == 0:
            pl.semaphore_wait(barrier, 2)
        for other in range(turn + 1):
            earlier = layers - 1 - other
            advance_ring(earlier, reached[earlier])
            reached[earlier] += 1
        if layer > 0:
            loads[2 * turn + 2].wait()
        retreat_layer(turn, layers, tops, start, packs, weights, kernels, damping, gates)
    stores = [pltpu.make_async_copy(start, start_hbm, store_sems.at[layers])]
    stores[0].start()
    for layer in range(layers):
        advance_ring(layer, reached[layer])
        reached[layer] += 1
    loads[2 * layers].wait()
    rows_times(tops, packed_transposed, True, put)
    stores.append(pltpu.make_async_copy(coarse_start, coarse_hbm, store_sems.at[layers + 1]))
    stores[1].start()
    while min(reached) < stages:
        for layer in range(layers):
            if reached[layer] < stages:
                advance_ring(layer, reached[layer])
                reached[layer] += 1
                if reached[layer] == stages:
                    store = pltpu.make_async_copy(total.at[layer], grads_hbm.at[layer], store_sems.at[layer])
                    store.start()
                    stores.append(store)
    for layer in range(layers):
        for way in range(2):
            for step in range(ring - 1):
                reduce_copy(layer, way, step).wait_send()
                gather_copy(layer, way, step).wait_send()
    for store in stores:
        store.wait()


def in_vmem(count, scalars=0):
    return [pl.BlockSpec(memory_space=pltpu.SMEM)] * scalars + [
        pl.BlockSpec(memory_space=pltpu.VMEM)
    ] * count


def nothing():
    pass


def chain_steps(
    chips, backward, window, seed, terms, matrices, out, scratch, pair_ready=nothing, all_ready=nothing
):
    (
        partner_terms, composed, inbox, outbox, returned, handed, partner_out, packs,
        pair_send, pair_recv, in_send, in_recv, back_send, back_recv, out_send, out_recv,
    ) = scratch
    me = lax.axis_index("layer")
    chip = me // 2
    core = me % 2
    partner = me + 1 - 2 * core
    half = terms.shape[0] // 2
    lead = 1 if backward else 0
    is_lead = core == lead
    tiles = half // 8

    def start_of(other):
        return pl.multiple_of((other * tiles) // chips * 8, 8)

    def own_rows(other):
        return pl.ds(pl.multiple_of(core * half + start_of(other), 8), window)

    def other_rows(other):
        return pl.ds(pl.multiple_of((1 - core) * half + start_of(other), 8), window)

    def turned(step):
        return lax.rem(chip + step, chips)

    def pair_copy(other):
        return pltpu.make_async_remote_copy(
            src_ref=terms.at[other_rows(other)],
            dst_ref=partner_terms.at[other],
            send_sem=pair_send.at[other],
            recv_sem=pair_recv.at[other],
            device_id={"layer": partner},
            device_id_type=MESH,
        )

    def send_pair(step, carry):
        pair_copy(turned(step)).start()
        return carry

    lax.fori_loop(1, chips + 1, send_pair, 0)

    lead_slab = 2 * chip + lead
    next_slab = 2 * chip + 1 - lead
    pair_ready()
    packs[next_slab] = pack_matrix(matrices[next_slab], backward)

    def in_copy(other):
        return pltpu.make_async_remote_copy(
            src_ref=composed.at[other],
            dst_ref=inbox.at[chip],
            send_sem=in_send.at[other],
            recv_sem=in_recv.at[chip],
            device_id={"layer": other * 2 + core},
            device_id_type=MESH,
        )

    def in_arrival(other):
        return pltpu.make_async_remote_copy(
            src_ref=composed.at[other],
            dst_ref=inbox.at[other],
            send_sem=in_send.at[other],
            recv_sem=in_recv.at[other],
            device_id={"layer": other * 2 + core},
            device_id_type=MESH,
        )

    def compose(other):
        pair_copy(other).wait_recv()
        own, theirs = terms[own_rows(other)], partner_terms[other]
        led = jnp.where(is_lead, own, theirs)
        following = jnp.where(is_lead, theirs, own)
        return times(led, packs[next_slab], backward) + following

    def compose_send(step, carry):
        other = turned(step)
        composed[other] = compose(other)
        in_copy(other).start()
        return carry

    lax.fori_loop(1, chips, compose_send, 0)
    inbox[chip] = compose(chip)

    all_ready()

    def prepare(index, carry):
        packs[index] = pack_matrix(matrices[index], backward)
        return carry

    lax.fori_loop(0, 2 * chips, prepare, 0, unroll=4)

    def back_copy(other):
        return pltpu.make_async_remote_copy(
            src_ref=outbox.at[other],
            dst_ref=returned.at[chip],
            send_sem=back_send.at[other],
            recv_sem=back_recv.at[chip],
            device_id={"layer": other * 2 + core},
            device_id_type=MESH,
        )

    def back_arrival(other):
        return pltpu.make_async_remote_copy(
            src_ref=outbox.at[other],
            dst_ref=returned.at[other],
            send_sem=back_send.at[other],
            recv_sem=back_recv.at[other],
            device_id={"layer": other * 2 + core},
            device_id_type=MESH,
        )

    def scan(step, rows):
        at = chips - 1 - step if backward else step
        outbox[at] = rows

        @pl.when(at != chip)
        def _():
            back_copy(at).start()
            in_arrival(at).wait_recv()

        rows = times(rows, packs[2 * at + lead], backward)
        return times(rows, packs[2 * at + 1 - lead], backward) + inbox[at]

    lax.fori_loop(0, chips, scan, seed[own_rows(chip)])

    def hand_copy(other):
        return pltpu.make_async_remote_copy(
            src_ref=handed.at[other],
            dst_ref=partner_out.at[other],
            send_sem=out_send.at[other],
            recv_sem=out_recv.at[other],
            device_id={"layer": partner},
            device_id_type=MESH,
        )

    def finish(other, led):
        lead_terms = jnp.where(is_lead, terms[own_rows(other)], partner_terms[other])
        following = times(led, packs[lead_slab], backward) + lead_terms
        out[own_rows(other)] = jnp.where(is_lead, led, following)
        handed[other] = jnp.where(is_lead, following, led)
        hand_copy(other).start()

    finish(chip, outbox[chip])

    def finish_next(step, carry):
        other = turned(step)
        back_arrival(other).wait_recv()
        finish(other, returned[other])
        return carry

    lax.fori_loop(1, chips, finish_next, 0)

    def drain(step, carry):
        in_copy(turned(step)).wait_send()
        back_copy(turned(step)).wait_send()
        return carry

    lax.fori_loop(1, chips, drain, 0)

    def collect(step, carry):
        other = turned(step)
        pair_copy(other).wait_send()
        hand_copy(other).wait()
        out[other_rows(other)] = partner_out[other]
        return carry

    lax.fori_loop(0, chips, collect, 0)

def chain_scratch(rows, slabs, channels):
    chips = slabs // 2
    window = -(-(rows // 16) // chips) * 8
    blocks = pltpu.VMEM((chips, window, channels), F32)
    packs = pltpu.VMEM((slabs, 2 * channels, 2 * channels), BF16)
    return window, [blocks] * 7 + [packs] + [pltpu.SemaphoreType.DMA((chips,))] * 8


def greet_chain(chips):
    me = lax.axis_index("layer")
    barrier = pltpu.get_barrier_semaphore()
    pl.semaphore_signal(barrier, inc=1, device_id={"layer": me + 1 - 2 * (me % 2)}, device_id_type=MESH)

    def greet(step, carry):
        other = lax.rem(me // 2 + step, chips) * 2 + me % 2
        pl.semaphore_signal(barrier, inc=1, device_id={"layer": other}, device_id_type=MESH)
        return carry

    lax.fori_loop(1, chips, greet, 0)


def middle_kernel(
    chips, window, begins, kernels, damping, damp_after, matrix,
    offsets_hbm, after_hbm, cot_hbm, matrices_hbm,
    slab_hbm, coarse_hbm, back_hbm, gates_hbm, kept_hbm, tops,
    offsets, after, cotangent, matrices, slab_end, coarse_end, back_offset, gates, kept,
    gates_after, state, pack_a, pack_b, weights, weights_back, load_sems, store_sems, *chain,
):
    slabs = 2 * chips
    layers = kernels.shape[0]
    greet_chain(chips)
    sources = (offsets_hbm, after_hbm, cot_hbm, matrices_hbm)
    loads = [
        pltpu.make_async_copy(source, target, load_sems.at[place])
        for place, (source, target) in enumerate(zip(sources, (offsets, after, cotangent, matrices)))
    ]
    for load in loads:
        load.start()
    stores = []

    def keep(source, target):
        stores.append(pltpu.make_async_copy(source, target, store_sems.at[len(stores)]))
        stores[-1].start()

    packs = (pack_a, pack_b)
    for packed in packs:
        clear_edges(packed)
    packed_matrix = pack_matrix(matrix[...], False)
    packed_transposed = pack_matrix(matrix[...], True)
    pack_field(pack_a, begins)
    for layer in range(layers):
        advance_layer(layer, layers, begins, slab_end, packs, weights, kernels, damping, gates, kept)
        keep(gates.at[layer], gates_hbm.at[layer])
        keep(kept.at[layer], kept_hbm.at[layer])
    keep(slab_end, slab_hbm)
    loads[0].wait()

    def put(at, value):
        coarse_end[at] = value + offsets[at]

    rows_times(begins, packed_matrix, False, put)
    keep(coarse_end, coarse_hbm)
    loads[1].wait()
    pack_field(pack_a, coarse_end)
    run_forward(coarse_end, state, packs, weights, after, damp_after, gates_after)
    loads[2].wait()
    run_backward(cotangent, state, packs, weights_back, after, damp_after, gates_after)
    choose_rows(lax.axis_index("layer") == slabs - 1, cotangent, state)
    run_backward(state, back_offset, packs, weights_back, kernels, damping, gates)

    def put_back(at, value):
        back_offset[at] = back_offset[at] - value

    rows_times(state, packed_transposed, True, put_back)
    keep(back_offset, back_hbm)
    loads[3].wait()
    pl.semaphore_wait(pltpu.get_barrier_semaphore(), chips)
    chain_steps(chips, True, window, cotangent, back_offset, matrices, tops, chain)
    for store in stores:
        store.wait()


def run_middle(begins, kernels, damping, damp_after, matrix, offsets, after, cotangent, matrices, packed, weights):
    layers, depth, channels = kernels.shape
    slabs = matrices.shape[0]
    pairs = packed[0].shape[2] - 1
    window, chain = chain_scratch(begins.shape[0], slabs, channels)
    field = jax.ShapeDtypeStruct(begins.shape, F32)
    gates = jax.ShapeDtypeStruct((layers,) + begins.shape, F32)
    kept = jax.ShapeDtypeStruct((layers, 2, pairs, WIDE, channels), BF16)
    anywhere = pl.BlockSpec(memory_space=pl.ANY)
    dma = pltpu.SemaphoreType.DMA
    flat = pltpu.VMEM(begins.shape, F32)
    return pl.pallas_call(
        functools.partial(middle_kernel, slabs // 2, window),
        out_shape=(field, field, field, gates, kept, field),
        in_specs=in_vmem(5) + [anywhere] * 4,
        out_specs=(anywhere,) * 5 + tuple(in_vmem(1)),
        scratch_shapes=[
            flat,
            pltpu.VMEM(kernels.shape, F32),
            flat,
            pltpu.VMEM(matrices.shape, F32),
            flat,
            flat,
            flat,
            pltpu.VMEM(gates.shape, F32),
            pltpu.VMEM(kept.shape, BF16),
            pltpu.VMEM(gates.shape, F32),
            flat,
        ]
        + packed
        + weights
        + [dma((4,)), dma((2 * layers + 3,))]
        + chain,
        compiler_params=pltpu.CompilerParams(
            vmem_limit_bytes=VMEM_BYTES, collective_id=2, has_side_effects=True
        ),
        name="middle",
    )(begins, kernels, damping, damp_after, matrix, offsets, after, cotangent, matrices)


def forward_kernel(
    chips, ring, window, images, kernels, damping,
    begins, offsets, after, damp_after, matrices, own_matrix,
    wide, damp_wide, before, damp_before, quarter, start, pack_a, pack_b, weights,
    full_send, full_recv, part_send, part_recv, relay_send, relay_recv,
    next_send, next_recv, damp_send, damp_recv, far_send, far_recv, pair_send, pair_recv,
    after_send, after_recv, back_send, back_recv, *chain,
):
    layers, depth, channels = kernels.shape
    share = depth // ring
    slabs = 2 * chips
    me = lax.axis_index("layer")
    line = lax.axis_index("dp")
    chip = me // 2
    core = me % 2
    partner = me + 1 - 2 * core
    across = (core == 1) & (me < slabs - 1)
    from_across = (core == 0) & (me > 0)

    def turned(step):
        return lax.rem(chip + step, chips)

    barrier = pltpu.get_barrier_semaphore()
    greet_chain(chips)
    for step in range(1, ring):
        pl.semaphore_signal(barrier, inc=1, device_id={"dp": lax.rem(line + step, ring)}, device_id_type=MESH)

    @pl.when(across)
    def _():
        pl.semaphore_signal(barrier, inc=1, device_id={"layer": me + 1}, device_id_type=MESH)

    @pl.when(from_across)
    def _():
        pl.semaphore_signal(barrier, inc=1, device_id={"layer": me - 1}, device_id_type=MESH)

    wide[...] = kernels[...].astype(F32)
    damp_wide[...] = jnp.zeros_like(damp_wide)
    damp_wide[pl.ds(0, layers)] = damping[...]
    packs = (pack_a, pack_b)
    for packed in packs:
        clear_edges(packed)
    pl.semaphore_wait(barrier, chips + ring - 1 + across.astype(jnp.int32) + from_across.astype(jnp.int32))

    own_share = pl.ds(pl.multiple_of(line * share, 8), share)

    def to(source, target, send, recv, device):
        return pltpu.make_async_remote_copy(
            src_ref=source, dst_ref=target, send_sem=send, recv_sem=recv, device_id=device, device_id_type=MESH
        )

    after_slab = {"layer": lax.rem(me + 1, slabs)}
    before_slab = {"layer": lax.rem(me + slabs - 1, slabs)}

    def full_copy(layer):
        return to(wide.at[layer], before.at[layer], full_send.at[layer], full_recv.at[layer], after_slab)

    def part_copy(layer):
        return to(
            wide.at[layer, own_share], before.at[layer, own_share], part_send.at[layer], part_recv.at[layer], after_slab
        )

    def damp_copy(way, target, device):
        return to(damp_wide, target, damp_send.at[way], damp_recv.at[way], device)

    def next_copy():
        return to(wide.at[:, own_share], quarter, next_send, next_recv, before_slab)

    def back_copy():
        return to(wide, after, back_send, back_recv, before_slab)

    damp_up = damp_copy(0, damp_before, after_slab)
    damp_down = damp_copy(1, damp_after, before_slab)

    @pl.when(core == 0)
    def _():
        damp_up.start()
        for layer in range(layers):
            full_copy(layer).start()

    @pl.when(across)
    def _():
        damp_up.start()
        for layer in range(layers):
            part_copy(layer).start()

    @pl.when(me > 0)
    def _():
        damp_down.start()

    @pl.when(from_across)
    def _():
        next_copy().start()

    @pl.when(core == 1)
    def _():
        back_copy().start()

    pack_field(pack_a, images)

    taps = wide[0].reshape(depth // channels, channels, channels)
    tap_sum = taps[0]
    for tap in range(1, depth // channels):
        tap_sum = tap_sum + taps[tap]
    scale = layers * STEP
    line_at = lax.broadcasted_iota(jnp.int32, (channels, channels), 0)
    col_at = lax.broadcasted_iota(jnp.int32, (channels, channels), 1)
    decay = jnp.broadcast_to((1.0 - scale * damping[0, :]).reshape(1, channels), (channels, channels))
    matrix = jnp.where(line_at == col_at, decay, 0.0) + scale * tap_sum
    own_matrix[...] = matrix
    matrices[me] = matrix

    def far_copy(other):
        return to(
            own_matrix, matrices.at[me], far_send.at[other], far_recv.at[chip], {"layer": other * 2 + core}
        )

    def far_arrival(other):
        return to(
            own_matrix, matrices.at[other * 2 + core], far_send.at[other], far_recv.at[other],
            {"layer": other * 2 + core},
        )

    def pair_copy(other):
        slab = other * 2 + core
        return to(matrices.at[slab], matrices.at[slab], pair_send.at[other], pair_recv.at[other], {"layer": partner})

    def pair_arrival(other):
        slab = other * 2 + 1 - core
        return to(matrices.at[slab], matrices.at[slab], pair_send.at[other], pair_recv.at[other], {"layer": partner})

    def send_far(step, carry):
        far_copy(turned(step)).start()
        return carry

    def relay_copy(layer, step):
        return to(
            before.at[layer, own_share], before.at[layer, own_share],
            relay_send.at[layer * ring + step], relay_recv.at[layer * ring + step],
            {"dp": lax.rem(line + step, ring)},
        )

    def relay_arrival(layer, step):
        rows = pl.ds(pl.multiple_of(lax.rem(line + ring - step, ring) * share, 8), share)
        return to(
            before.at[layer, rows], before.at[layer, rows],
            relay_send.at[layer * ring + step], relay_recv.at[layer * ring + step],
            {"dp": lax.rem(line + step, ring)},
        )

    @pl.when(from_across)
    def _():
        for layer in range(layers):
            part_copy(layer).wait_recv()
            for step in range(1, ring):
                relay_copy(layer, step).start()

    lax.fori_loop(1, chips, send_far, 0)
    pair_copy(chip).start()

    @pl.when(me == 0)
    def _():
        before[...] = jnp.zeros_like(before)
        damp_before[...] = jnp.zeros_like(damp_before)

    @pl.when(me > 0)
    def _():
        damp_up.wait_recv()

    for layer in range(layers):

        @pl.when(from_across)
        def _():
            for step in range(1, ring):
                relay_arrival(layer, step).wait_recv()

        @pl.when(core == 1)
        def _():
            full_copy(layer).wait_recv()

        advance_layer(layer, layers, images, start, packs, weights, before, damp_before)

    choose_rows(me == 0, images, start)

    def after_rows(step):
        return pl.ds(pl.multiple_of(lax.rem(line + ring - step, ring) * share, 8), share)

    def after_copy(step):
        return to(
            quarter, after.at[:, own_share], after_send.at[step - 1], after_recv.at[step - 1],
            {"dp": lax.rem(line + step, ring)},
        )

    def after_arrival(step):
        return to(
            quarter, after.at[:, after_rows(step)], after_send.at[step - 1], after_recv.at[step - 1],
            {"dp": lax.rem(line + step, ring)},
        )

    @pl.when(across)
    def _():
        next_copy().wait_recv()
        for step in range(1, ring):
            after_copy(step).start()
        after[:, own_share] = quarter[...]

    pack_field(pack_a, start)
    run_forward(start, offsets, packs, weights, kernels, damping)
    packed_matrix = pack_matrix(matrix, False)

    def put(at, value):
        offsets[at] = offsets[at] - value

    rows_times(start, packed_matrix, False, put)

    def pass_on(step, carry):
        other = turned(step)
        far_arrival(other).wait_recv()
        pair_copy(other).start()
        return carry

    def pair_ready():
        pair_arrival(chip).wait_recv()

    def all_ready():
        lax.fori_loop(1, chips, pass_on, 0)

        def arrived(step, carry):
            pair_arrival(turned(step)).wait_recv()
            return carry

        lax.fori_loop(1, chips, arrived, 0)

    chain_steps(chips, False, window, images, offsets, matrices, begins, chain, pair_ready, all_ready)

    @pl.when(from_across)
    def _():
        for layer in range(layers):
            for step in range(1, ring):
                relay_copy(layer, step).wait_send()

    @pl.when(me > 0)
    def _():
        damp_down.wait_send()

    @pl.when(from_across)
    def _():
        next_copy().wait_send()

    @pl.when(core == 1)
    def _():
        back_copy().wait_send()

    @pl.when(me < slabs - 1)
    def _():
        damp_up.wait_send()
        damp_down.wait_recv()

    @pl.when(me == slabs - 1)
    def _():
        damp_after[...] = jnp.zeros_like(damp_after)
        after[...] = jnp.zeros_like(after)

    @pl.when(core == 0)
    def _():
        back_copy().wait_recv()
        for layer in range(layers):
            full_copy(layer).wait_send()

    @pl.when(across)
    def _():
        for layer in range(layers):
            part_copy(layer).wait_send()

    def settle(step, carry):
        far_copy(turned(step)).wait_send()
        return carry

    lax.fori_loop(1, chips, settle, 0)

    def settle_pair(step, carry):
        pair_copy(turned(step)).wait_send()
        return carry

    lax.fori_loop(0, chips, settle_pair, 0)

    @pl.when(across)
    def _():
        for step in range(1, ring):
            after_copy(step).wait_send()
            after_arrival(step).wait_recv()


def run_forward_kernel(images, kernels, damping, slabs, ring, packed, weights):
    chips = slabs // 2
    layers, depth, channels = kernels.shape
    dma = pltpu.SemaphoreType.DMA
    window, chain = chain_scratch(images.shape[0], slabs, channels)
    field = jax.ShapeDtypeStruct(images.shape, F32)
    outs = (
        field,
        field,
        jax.ShapeDtypeStruct(kernels.shape, F32),
        jax.ShapeDtypeStruct((8, channels), F32),
        jax.ShapeDtypeStruct((slabs, channels, channels), F32),
        jax.ShapeDtypeStruct((channels, channels), F32),
    )
    return pl.pallas_call(
        functools.partial(forward_kernel, chips, ring, window),
        out_shape=outs,
        in_specs=in_vmem(3),
        out_specs=tuple(in_vmem(len(outs))),
        scratch_shapes=[
            pltpu.VMEM(kernels.shape, F32),
            pltpu.VMEM((8, channels), F32),
            pltpu.VMEM(kernels.shape, F32),
            pltpu.VMEM((8, channels), F32),
            pltpu.VMEM((layers, depth // ring, channels), F32),
            pltpu.VMEM(images.shape, F32),
        ]
        + packed
        + weights
        + [dma((layers,))] * 4
        + [dma((layers * ring,))] * 2
        + [dma, dma, dma((2,)), dma((2,))]
        + [dma((chips,))] * 4
        + [dma((ring - 1,))] * 2
        + [dma] * 2
        + chain,
        compiler_params=pltpu.CompilerParams(
            vmem_limit_bytes=VMEM_BYTES, collective_id=1, has_side_effects=True
        ),
        name="forward",
    )(images, kernels, damping)


def place_kernel(*refs):
    half = len(refs) // 2
    for source, target in zip(refs[:half], refs[half:]):
        target[...] = source[...]


def place(*arrays):
    parts = 2

    def specs():
        return [pl.BlockSpec((a.shape[0] // parts, a.shape[1]), lambda i: (i, 0)) for a in arrays]

    return pl.pallas_call(
        place_kernel,
        grid=(parts,),
        out_shape=[jax.ShapeDtypeStruct(a.shape, a.dtype) for a in arrays],
        in_specs=specs(),
        out_specs=specs(),
        compiler_params=pltpu.CompilerParams(vmem_limit_bytes=VMEM_BYTES),
        name="place",
    )(*arrays)


def run_final(tops, kernels, damping, matrix, back_offsets, gates, kept, ring, packed, weights):
    layers, depth, channels = kernels.shape
    moves = layers * 2 * (ring - 1)
    dma = pltpu.SemaphoreType.DMA
    state = jax.ShapeDtypeStruct(tops.shape, F32)
    anywhere = pl.BlockSpec(memory_space=pl.ANY)
    return pl.pallas_call(
        functools.partial(final_kernel, ring),
        out_shape=(state, state, jax.ShapeDtypeStruct(kernels.shape, F32)),
        in_specs=in_vmem(4) + [anywhere] * 3,
        out_specs=(anywhere,) * 3,
        scratch_shapes=packed
        + weights
        + [
            pltpu.VMEM(tops.shape, F32),
            pltpu.VMEM(gates.shape, F32),
            pltpu.VMEM(kept.shape, BF16),
            pltpu.VMEM(tops.shape, F32),
            pltpu.VMEM(tops.shape, F32),
            pltpu.VMEM(kernels.shape, F32),
            pltpu.VMEM(kernels.shape, F32),
            pltpu.VMEM((moves, depth // (2 * ring), channels), F32),
        ]
        + [dma((moves,))] * 4
        + [dma((2 * layers + 1,)), dma((layers + 2,))],
        compiler_params=pltpu.CompilerParams(
            vmem_limit_bytes=VMEM_BYTES, collective_id=4, has_side_effects=True
        ),
        name="final",
    )(tops, kernels, damping, matrix, back_offsets, gates, kept)


def per_device(images, kernels, damping, cotangent):
    slab, depth, channels = kernels.shape
    side = images.shape[1]
    slabs = lax.axis_size("layer")
    ring = lax.axis_size("dp")
    pairs = side // 2
    flat = (side * side, channels)
    images_flat, cot_flat = images.reshape(flat), cotangent.reshape(flat)
    packed = [pltpu.VMEM((3, 2, pairs + 1, WIDE, channels), BF16)] * 2
    weights = [pltpu.VMEM((12 * channels, 2 * channels), BF16)]
    weights_back = [pltpu.VMEM((2 * channels, 12 * channels), BF16)]

    begins, offsets, after, damp_after, matrices, matrix = run_forward_kernel(
        images_flat, kernels, damping, slabs, ring, packed, weights
    )
    slab_end, coarse_end, back_offsets, gates, kept, tops = run_middle(
        begins, kernels, damping, damp_after, matrix, offsets, after, cot_flat, matrices, packed, weights + weights_back
    )
    adjoint_start, adjoint_coarse, grads = run_final(
        tops, kernels, damping, matrix, back_offsets, gates, kept, ring, packed, weights_back
    )
    slab_end, coarse_end, adjoint_start, adjoint_coarse, grads = place(
        slab_end, coarse_end, adjoint_start, adjoint_coarse, grads.reshape(slab * depth, channels)
    )
    full = (1,) + images.shape
    return (
        slab_end.reshape(full),
        coarse_end.reshape(full),
        adjoint_start.reshape(full),
        adjoint_coarse.reshape(full),
        grads.reshape(kernels.shape),
    )


def solution(mesh):
    in_specs = (
        P("dp", None, None, None),
        P("layer", None, None),
        P("layer", None),
        P("dp", None, None, None),
    )
    out_specs = (
        P("layer", "dp", None, None, None),
        P("layer", "dp", None, None, None),
        P("layer", "dp", None, None, None),
        P("layer", "dp", None, None, None),
        P("layer", None, None),
    )
    return jax.shard_map(
        per_device, mesh=mesh, in_specs=in_specs, out_specs=out_specs, check_vma=False
    )
```

```python
import functools

import jax
import jax.numpy as jnp
from jax import lax
from jax.experimental import pallas as pl
from jax.experimental.pallas import tpu as pltpu
from jax.sharding import PartitionSpec as P

STEP = 0.125
F32 = jnp.float32
BF16 = jnp.bfloat16
MESH = pl.DeviceIdType.MESH
VMEM_BYTES = 60 * 1024 * 1024
WIDE = 64
GROUP = 7


def split(value):
    high = value.astype(BF16)
    return high, (value - high.astype(F32)).astype(BF16)


def pack_matrix(matrix, transposed):
    high, low = split(matrix)
    if transposed:
        top = jnp.concatenate([high, high], axis=1)
        bottom = jnp.concatenate([low, jnp.zeros_like(low)], axis=1)
    else:
        top = jnp.concatenate([high, low], axis=1)
        bottom = jnp.concatenate([high, jnp.zeros_like(low)], axis=1)
    return jnp.concatenate([top, bottom], axis=0)


def times(rows, packed, transposed):
    channels = rows.shape[1]
    both = jnp.concatenate(split(rows), axis=1)
    dims = (((1,), (1 if transposed else 0,)), ((), ()))
    result = lax.dot_general(both, packed, dims, preferred_element_type=F32)
    return result[:, :channels] + result[:, channels:]


def clear_edges(packed):
    zeros = jnp.zeros(packed.shape[3:], packed.dtype)
    for col in range(3):
        packed[col, 0, 0] = zeros
        packed[col, 1, packed.shape[2] - 1] = zeros


def pack_rows(packed, first, even, odd):
    count, side, channels = even.shape
    fill = jnp.zeros((count, WIDE - side, channels), F32)
    for parity, value in ((1, even), (0, odd)):
        start = first if parity == 1 else first + 1
        wide = jnp.concatenate([value, fill], axis=1)
        for col, shift in ((1, 0), (0, 1), (2, WIDE - 1)):
            moved = wide if shift == 0 else pltpu.roll(wide, shift, 1)
            packed[col, parity, pl.ds(start, count)] = moved.astype(BF16)


def pieces(packed, first, count):
    channels = packed.shape[-1]
    rows = count * packed.shape[3]
    out = []
    for col in range(3):
        for parity, ahead in ((1, 0), (0, 1), (0, 0), (1, 1)):
            out.append(packed[col, parity, pl.ds(first + ahead, count)].reshape(rows, channels))
    return out


OFFSETS = (0, 1, -1, 2)


def fill_weights(weights, kernel, backward):
    channels = weights.shape[1] // 2 if not backward else weights.shape[0] // 2
    zero = jnp.zeros((channels, channels), BF16)
    for col in range(3):
        for place, offset in enumerate(OFFSETS):
            at = pl.ds((col * 4 + place) * channels, channels)
            for row in range(2):
                tap = offset - row + 1
                if 0 <= tap <= 2:
                    index = tap * 3 + col
                    block = kernel(8 - index if backward else index).astype(BF16)
                else:
                    block = zero
                out = pl.ds(row * channels, channels)
                if backward:
                    weights[out, at] = block
                else:
                    weights[at, out] = block


def convolve(packed, weights, first, count, side, backward):
    left = jnp.concatenate(pieces(packed, first, count), axis=1)
    dims = (((1,), (1 if backward else 0,)), ((), ()))
    result = lax.dot_general(left, weights[...], dims, preferred_element_type=F32)
    channels = result.shape[1] // 2
    result = result.reshape(count, WIDE, 2 * channels)[:, :side]
    return result[:, :, :channels], result[:, :, channels:]


def each_group(pairs, body):
    def step(index, carry):
        body(index * GROUP)
        return carry

    lax.fori_loop(0, pairs // GROUP, step, 0, unroll=True)


def rows_at(first, side):
    return pl.ds(pl.multiple_of(first * 2 * side, 8), GROUP * 2 * side)


def pair_rows(value, side):
    value = value.reshape(GROUP, 2, side, value.shape[-1])
    return value[:, 0], value[:, 1]


def flat_rows(even, odd):
    return jnp.stack([even, odd], axis=1).reshape(-1, even.shape[-1])


def pack_field(packed, field):
    pairs = packed.shape[2] - 1

    def body(first):
        even, odd = pair_rows(field[rows_at(first, 2 * pairs)], 2 * pairs)
        pack_rows(packed, first, even, odd)

    each_group(pairs, body)


def tap_of(ref, layer, channels):
    return lambda tap: ref[layer, pl.ds(tap * channels, channels), :]


def advance_layer(layer, layers, source, target, packs, weights, kernels, damping, gates=None, kept=None):
    channels = source.shape[-1]
    pairs = packs[0].shape[2] - 1
    side = 2 * pairs
    now, later = packs[layer % 2], packs[(layer + 1) % 2]
    fill_weights(weights, tap_of(kernels, layer, channels), False)
    decay = damping[layer, :].reshape(1, 1, channels)
    state = source if layer == 0 else target

    def body(first):
        at = rows_at(first, side)
        outs = convolve(now, weights, first, GROUP, side, False)
        nexts, slopes = [], []
        for out, current in zip(outs, pair_rows(state[at], side)):
            act = jnp.tanh(out)
            slopes.append(STEP * (1.0 - act * act))
            nexts.append(current + STEP * (act - decay * current))
        target[at] = flat_rows(*nexts)
        if gates is not None:
            gates[layer, at] = flat_rows(*slopes)
        if kept is not None:
            kept[layer, 0, pl.ds(first, GROUP)] = now[1, 1, pl.ds(first, GROUP)]
            kept[layer, 1, pl.ds(first, GROUP)] = now[1, 0, pl.ds(first + 1, GROUP)]
        if layer + 1 < layers:
            pack_rows(later, first, *nexts)

    each_group(pairs, body)


def run_forward(source, target, packs, weights, kernels, damping, gates=None, kept=None):
    layers = kernels.shape[0]
    for layer in range(layers):
        advance_layer(layer, layers, source, target, packs, weights, kernels, damping, gates, kept)


def pack_scaled(packed, gates, layer, adjoint):
    pairs = packed.shape[2] - 1

    def body(first):
        at = rows_at(first, 2 * pairs)
        pack_rows(packed, first, *pair_rows(gates[layer, at] * adjoint[at], 2 * pairs))

    each_group(pairs, body)


def retreat_layer(turn, layers, source, target, packs, weights, kernels, damping, gates):
    channels = source.shape[-1]
    pairs = packs[0].shape[2] - 1
    side = 2 * pairs
    layer = layers - 1 - turn
    now, later = packs[turn % 2], packs[(turn + 1) % 2]
    fill_weights(weights, tap_of(kernels, layer, channels), True)
    decay = damping[layer, :].reshape(1, 1, channels)
    state = source if turn == 0 else target

    def body(first):
        at = rows_at(first, side)
        outs = convolve(now, weights, first, GROUP, side, True)
        nexts = []
        for out, current in zip(outs, pair_rows(state[at], side)):
            nexts.append(current - STEP * decay * current + out)
        target[at] = flat_rows(*nexts)
        if layer > 0:
            scaled = [gate * moved for gate, moved in zip(pair_rows(gates[layer - 1, at], side), nexts)]
            pack_rows(later, first, *scaled)

    each_group(pairs, body)


def run_backward(source, target, packs, weights, kernels, damping, gates):
    layers = gates.shape[0]
    pack_scaled(packs[0], gates, layers - 1, source)
    for turn in range(layers):
        retreat_layer(turn, layers, source, target, packs, weights, kernels, damping, gates)


def gradient(packed, kept, layer, grads):
    channels = packed.shape[-1]
    pairs = packed.shape[2] - 1
    left = jnp.concatenate([kept[layer, row].reshape(pairs * WIDE, channels) for row in range(2)], axis=1)
    for col in range(3):
        parts = []
        for parity, ahead in ((1, 0), (0, 1), (0, 0), (1, 1)):
            parts.append(packed[col, parity, pl.ds(ahead, pairs)].reshape(pairs * WIDE, channels))
        out = lax.dot_general(
            left, jnp.concatenate(parts, axis=1), (((0,), (0,)), ((), ())), preferred_element_type=F32
        )

        def block(row, offset):
            place = OFFSETS.index(offset)
            return out[row * channels : (row + 1) * channels, place * channels : (place + 1) * channels]

        for tap in range(3):
            total = block(0, 1 - tap) + block(1, 2 - tap)
            index = tap * 3 + (2 - col)
            grads[layer, pl.ds(index * channels, channels), :] = total


def rows_times(source, packed_matrix, transposed, put):
    parts = 7
    size = source.shape[0] // parts

    def body(index, carry):
        at = pl.ds(pl.multiple_of(index * size, 8), size)
        put(at, times(source[at], packed_matrix, transposed))
        return carry

    lax.fori_loop(0, parts, body, 0, unroll=True)


def choose_rows(flag, chosen, target):
    @pl.when(flag)
    def _():
        target[...] = chosen[...]


def final_kernel(
    ring, tops, kernels, damping, matrix, back_hbm, gates_hbm, kept_hbm,
    start_hbm, coarse_hbm, grads_hbm,
    pack_a, pack_b, weights, back_offset, gates, kept, start, coarse_start, local, total, landed,
    reduce_send, reduce_recv, gather_send, gather_recv, load_sems, store_sems,
):
    layers = kernels.shape[0]
    me = lax.axis_index("dp")
    neighbours = (lax.rem(me + 1, ring), lax.rem(me + ring - 1, ring))
    barrier = pltpu.get_barrier_semaphore()
    for neighbour in neighbours:
        pl.semaphore_signal(barrier, inc=1, device_id={"dp": neighbour}, device_id_type=MESH)

    loads = []
    for layer in reversed(range(layers)):
        loads.append(pltpu.make_async_copy(gates_hbm.at[layer], gates.at[layer], load_sems.at[2 * layer]))
        loads.append(pltpu.make_async_copy(kept_hbm.at[layer], kept.at[layer], load_sems.at[2 * layer + 1]))
    loads.append(pltpu.make_async_copy(back_hbm, back_offset, load_sems.at[2 * layers]))
    for load in loads:
        load.start()
    size = kernels.shape[1] // (2 * ring)

    def rows_of(way, step):
        chunk = lax.rem(me + (2 * ring - step if way == 0 else step + ring), ring)
        return pl.ds(pl.multiple_of((way * ring + chunk) * size, 8), size)

    def reduce_copy(layer, way, step):
        slot = (layer * 2 + way) * (ring - 1) + step
        return pltpu.make_async_remote_copy(
            src_ref=local.at[layer, rows_of(way, step)],
            dst_ref=landed.at[slot],
            send_sem=reduce_send.at[slot],
            recv_sem=reduce_recv.at[slot],
            device_id={"dp": neighbours[way]},
            device_id_type=MESH,
        )

    def gather_copy(layer, way, step):
        slot = (layer * 2 + way) * (ring - 1) + step
        rows = rows_of(way, step - 1)
        return pltpu.make_async_remote_copy(
            src_ref=total.at[layer, rows],
            dst_ref=total.at[layer, rows],
            send_sem=gather_send.at[slot],
            recv_sem=gather_recv.at[slot],
            device_id={"dp": neighbours[way]},
            device_id_type=MESH,
        )

    def advance_ring(layer, stage):
        last = ring - 1
        for way in range(2):
            if 1 <= stage <= last:
                slot = (layer * 2 + way) * last + stage - 1
                reduce_copy(layer, way, stage - 1).wait_recv()
                rows = rows_of(way, stage)
                value = local[layer, rows] + landed[slot]
                if stage < last:
                    local[layer, rows] = value
                else:
                    total[layer, rows] = value
            elif stage > last:
                gather_copy(layer, way, stage - last - 1).wait_recv()
            if stage < last:
                reduce_copy(layer, way, stage).start()
            elif stage < 2 * last:
                gather_copy(layer, way, stage - last).start()

    packs = (pack_a, pack_b)
    for packed in packs:
        clear_edges(packed)
    packed_transposed = pack_matrix(matrix[...], True)

    def put(at, value):
        coarse_start[at] = value + back_offset[at]

    stages = 2 * (ring - 1) + 1
    reached = [0] * layers
    loads[0].wait()
    pack_scaled(pack_a, gates, layers - 1, tops)
    for turn in range(layers):
        layer = layers - 1 - turn
        loads[2 * turn + 1].wait()
        gradient(packs[turn % 2], kept, layer, local)
        if turn == 0:
            pl.semaphore_wait(barrier, 2)
        for other in range(turn + 1):
            earlier = layers - 1 - other
            advance_ring(earlier, reached[earlier])
            reached[earlier] += 1
        if layer > 0:
            loads[2 * turn + 2].wait()
        retreat_layer(turn, layers, tops, start, packs, weights, kernels, damping, gates)
    stores = [pltpu.make_async_copy(start, start_hbm, store_sems.at[layers])]
    stores[0].start()
    for layer in range(layers):
        advance_ring(layer, reached[layer])
        reached[layer] += 1
    loads[2 * layers].wait()
    rows_times(tops, packed_transposed, True, put)
    stores.append(pltpu.make_async_copy(coarse_start, coarse_hbm, store_sems.at[layers + 1]))
    stores[1].start()
    while min(reached) < stages:
        for layer in range(layers):
            if reached[layer] < stages:
                advance_ring(layer, reached[layer])
                reached[layer] += 1
                if reached[layer] == stages:
                    store = pltpu.make_async_copy(total.at[layer], grads_hbm.at[layer], store_sems.at[layer])
                    store.start()
                    stores.append(store)
    for layer in range(layers):
        for way in range(2):
            for step in range(ring - 1):
                reduce_copy(layer, way, step).wait_send()
                gather_copy(layer, way, step).wait_send()
    for store in stores:
        store.wait()


def in_vmem(count, scalars=0):
    return [pl.BlockSpec(memory_space=pltpu.SMEM)] * scalars + [
        pl.BlockSpec(memory_space=pltpu.VMEM)
    ] * count


def nothing():
    pass


def chain_steps(
    chips, backward, window, seed, terms, matrices, out, scratch, pair_ready=nothing, all_ready=nothing
):
    (
        partner_terms, composed, inbox, outbox, returned, handed, partner_out, packs,
        pair_send, pair_recv, in_send, in_recv, back_send, back_recv, out_send, out_recv,
    ) = scratch
    me = lax.axis_index("layer")
    chip = me // 2
    core = me % 2
    partner = me + 1 - 2 * core
    half = terms.shape[0] // 2
    lead = 1 if backward else 0
    is_lead = core == lead
    tiles = half // 8

    def start_of(other):
        return pl.multiple_of((other * tiles) // chips * 8, 8)

    def own_rows(other):
        return pl.ds(pl.multiple_of(core * half + start_of(other), 8), window)

    def other_rows(other):
        return pl.ds(pl.multiple_of((1 - core) * half + start_of(other), 8), window)

    def turned(step):
        return lax.rem(chip + step, chips)

    def pair_copy(other):
        return pltpu.make_async_remote_copy(
            src_ref=terms.at[other_rows(other)],
            dst_ref=partner_terms.at[other],
            send_sem=pair_send.at[other],
            recv_sem=pair_recv.at[other],
            device_id={"layer": partner},
            device_id_type=MESH,
        )

    def send_pair(step, carry):
        pair_copy(turned(step)).start()
        return carry

    lax.fori_loop(1, chips + 1, send_pair, 0)

    lead_slab = 2 * chip + lead
    next_slab = 2 * chip + 1 - lead
    pair_ready()
    packs[next_slab] = pack_matrix(matrices[next_slab], backward)

    def in_copy(other):
        return pltpu.make_async_remote_copy(
            src_ref=composed.at[other],
            dst_ref=inbox.at[chip],
            send_sem=in_send.at[other],
            recv_sem=in_recv.at[chip],
            device_id={"layer": other * 2 + core},
            device_id_type=MESH,
        )

    def in_arrival(other):
        return pltpu.make_async_remote_copy(
            src_ref=composed.at[other],
            dst_ref=inbox.at[other],
            send_sem=in_send.at[other],
            recv_sem=in_recv.at[other],
            device_id={"layer": other * 2 + core},
            device_id_type=MESH,
        )

    def compose(other):
        pair_copy(other).wait_recv()
        own, theirs = terms[own_rows(other)], partner_terms[other]
        led = jnp.where(is_lead, own, theirs)
        following = jnp.where(is_lead, theirs, own)
        return times(led, packs[next_slab], backward) + following

    def compose_send(step, carry):
        other = turned(step)
        composed[other] = compose(other)
        in_copy(other).start()
        return carry

    lax.fori_loop(1, chips, compose_send, 0)
    inbox[chip] = compose(chip)

    all_ready()

    def prepare(index, carry):
        packs[index] = pack_matrix(matrices[index], backward)
        return carry

    lax.fori_loop(0, 2 * chips, prepare, 0, unroll=4)

    def back_copy(other):
        return pltpu.make_async_remote_copy(
            src_ref=outbox.at[other],
            dst_ref=returned.at[chip],
            send_sem=back_send.at[other],
            recv_sem=back_recv.at[chip],
            device_id={"layer": other * 2 + core},
            device_id_type=MESH,
        )

    def back_arrival(other):
        return pltpu.make_async_remote_copy(
            src_ref=outbox.at[other],
            dst_ref=returned.at[other],
            send_sem=back_send.at[other],
            recv_sem=back_recv.at[other],
            device_id={"layer": other * 2 + core},
            device_id_type=MESH,
        )

    rows = seed[own_rows(chip)]
    group = 4
    for first in range(0, chips, group):
        steps = range(first, min(first + group, chips))
        order = [chips - 1 - step if backward else step for step in steps]
        for at in order:

            @pl.when(chip != at)
            def _():
                in_arrival(at).wait_recv()

        for step, at in zip(steps, order):
            outbox[at] = rows
            if step < chips - 1:
                rows = times(rows, packs[2 * at + lead], backward)
                rows = times(rows, packs[2 * at + 1 - lead], backward) + inbox[at]
        for at in order:

            @pl.when(chip != at)
            def _():
                back_copy(at).start()

    def hand_copy(other):
        return pltpu.make_async_remote_copy(
            src_ref=handed.at[other],
            dst_ref=partner_out.at[other],
            send_sem=out_send.at[other],
            recv_sem=out_recv.at[other],
            device_id={"layer": partner},
            device_id_type=MESH,
        )

    def finish(other, led):
        lead_terms = jnp.where(is_lead, terms[own_rows(other)], partner_terms[other])
        following = times(led, packs[lead_slab], backward) + lead_terms
        out[own_rows(other)] = jnp.where(is_lead, led, following)
        handed[other] = jnp.where(is_lead, following, led)
        hand_copy(other).start()

    finish(chip, outbox[chip])

    def finish_next(step, carry):
        other = turned(step)
        back_arrival(other).wait_recv()
        finish(other, returned[other])
        return carry

    lax.fori_loop(1, chips, finish_next, 0)

    def drain(step, carry):
        in_copy(turned(step)).wait_send()
        back_copy(turned(step)).wait_send()
        return carry

    lax.fori_loop(1, chips, drain, 0)

    def collect(step, carry):
        other = turned(step)
        pair_copy(other).wait_send()
        hand_copy(other).wait()
        out[other_rows(other)] = partner_out[other]
        return carry

    lax.fori_loop(0, chips, collect, 0)

def chain_scratch(rows, slabs, channels):
    chips = slabs // 2
    window = -(-(rows // 16) // chips) * 8
    blocks = pltpu.VMEM((chips, window, channels), F32)
    packs = pltpu.VMEM((slabs, 2 * channels, 2 * channels), BF16)
    return window, [blocks] * 7 + [packs] + [pltpu.SemaphoreType.DMA((chips,))] * 8


def greet_chain(chips):
    me = lax.axis_index("layer")
    barrier = pltpu.get_barrier_semaphore()
    pl.semaphore_signal(barrier, inc=1, device_id={"layer": me + 1 - 2 * (me % 2)}, device_id_type=MESH)

    def greet(step, carry):
        other = lax.rem(me // 2 + step, chips) * 2 + me % 2
        pl.semaphore_signal(barrier, inc=1, device_id={"layer": other}, device_id_type=MESH)
        return carry

    lax.fori_loop(1, chips, greet, 0)


def middle_kernel(
    chips, window, begins, kernels, damping, damp_after, matrix,
    offsets_hbm, after_hbm, cot_hbm, matrices_hbm,
    slab_hbm, coarse_hbm, back_hbm, gates_hbm, kept_hbm, tops,
    offsets, after, cotangent, matrices, slab_end, coarse_end, back_offset, gates, kept,
    gates_after, state, pack_a, pack_b, weights, weights_back, load_sems, store_sems, *chain,
):
    slabs = 2 * chips
    layers = kernels.shape[0]
    greet_chain(chips)
    sources = (offsets_hbm, after_hbm, cot_hbm, matrices_hbm)
    loads = [
        pltpu.make_async_copy(source, target, load_sems.at[place])
        for place, (source, target) in enumerate(zip(sources, (offsets, after, cotangent, matrices)))
    ]
    for load in loads:
        load.start()
    stores = []

    def keep(source, target):
        stores.append(pltpu.make_async_copy(source, target, store_sems.at[len(stores)]))
        stores[-1].start()

    packs = (pack_a, pack_b)
    for packed in packs:
        clear_edges(packed)
    packed_matrix = pack_matrix(matrix[...], False)
    packed_transposed = pack_matrix(matrix[...], True)
    pack_field(pack_a, begins)
    for layer in range(layers):
        advance_layer(layer, layers, begins, slab_end, packs, weights, kernels, damping, gates, kept)
        keep(gates.at[layer], gates_hbm.at[layer])
        keep(kept.at[layer], kept_hbm.at[layer])
    keep(slab_end, slab_hbm)
    loads[0].wait()

    def put(at, value):
        coarse_end[at] = value + offsets[at]

    rows_times(begins, packed_matrix, False, put)
    keep(coarse_end, coarse_hbm)
    loads[1].wait()
    pack_field(pack_a, coarse_end)
    run_forward(coarse_end, state, packs, weights, after, damp_after, gates_after)
    loads[2].wait()
    run_backward(cotangent, state, packs, weights_back, after, damp_after, gates_after)
    choose_rows(lax.axis_index("layer") == slabs - 1, cotangent, state)
    run_backward(state, back_offset, packs, weights_back, kernels, damping, gates)

    def put_back(at, value):
        back_offset[at] = back_offset[at] - value

    rows_times(state, packed_transposed, True, put_back)
    keep(back_offset, back_hbm)
    loads[3].wait()
    pl.semaphore_wait(pltpu.get_barrier_semaphore(), chips)
    chain_steps(chips, True, window, cotangent, back_offset, matrices, tops, chain)
    for store in stores:
        store.wait()


def run_middle(begins, kernels, damping, damp_after, matrix, offsets, after, cotangent, matrices, packed, weights):
    layers, depth, channels = kernels.shape
    slabs = matrices.shape[0]
    pairs = packed[0].shape[2] - 1
    window, chain = chain_scratch(begins.shape[0], slabs, channels)
    field = jax.ShapeDtypeStruct(begins.shape, F32)
    gates = jax.ShapeDtypeStruct((layers,) + begins.shape, F32)
    kept = jax.ShapeDtypeStruct((layers, 2, pairs, WIDE, channels), BF16)
    anywhere = pl.BlockSpec(memory_space=pl.ANY)
    dma = pltpu.SemaphoreType.DMA
    flat = pltpu.VMEM(begins.shape, F32)
    return pl.pallas_call(
        functools.partial(middle_kernel, slabs // 2, window),
        out_shape=(field, field, field, gates, kept, field),
        in_specs=in_vmem(5) + [anywhere] * 4,
        out_specs=(anywhere,) * 5 + tuple(in_vmem(1)),
        scratch_shapes=[
            flat,
            pltpu.VMEM(kernels.shape, F32),
            flat,
            pltpu.VMEM(matrices.shape, F32),
            flat,
            flat,
            flat,
            pltpu.VMEM(gates.shape, F32),
            pltpu.VMEM(kept.shape, BF16),
            pltpu.VMEM(gates.shape, F32),
            flat,
        ]
        + packed
        + weights
        + [dma((4,)), dma((2 * layers + 3,))]
        + chain,
        compiler_params=pltpu.CompilerParams(
            vmem_limit_bytes=VMEM_BYTES, collective_id=2, has_side_effects=True
        ),
        name="middle",
    )(begins, kernels, damping, damp_after, matrix, offsets, after, cotangent, matrices)


def forward_kernel(
    chips, ring, window, images, kernels, damping,
    begins, offsets_hbm, after_hbm, damp_after, matrices_hbm, own_matrix,
    offsets, after, matrices,
    wide, damp_wide, before, damp_before, quarter, start, pack_a, pack_b, weights, store_sems,
    full_send, full_recv, part_send, part_recv, direct_send, direct_recv, relay_send, relay_recv,
    next_send, next_recv, damp_send, damp_recv, far_send, far_recv, pair_send, pair_recv,
    after_send, after_recv, back_send, back_recv, *chain,
):
    layers, depth, channels = kernels.shape
    share = depth // ring
    slabs = 2 * chips
    me = lax.axis_index("layer")
    line = lax.axis_index("dp")
    chip = me // 2
    core = me % 2
    partner = me + 1 - 2 * core
    across = (core == 1) & (me < slabs - 1)
    from_across = (core == 0) & (me > 0)

    def turned(step):
        return lax.rem(chip + step, chips)

    barrier = pltpu.get_barrier_semaphore()
    greet_chain(chips)
    for step in range(1, ring):
        pl.semaphore_signal(barrier, inc=1, device_id={"dp": lax.rem(line + step, ring)}, device_id_type=MESH)

    @pl.when(across)
    def _():
        pl.semaphore_signal(barrier, inc=1, device_id={"layer": me + 1}, device_id_type=MESH)

    @pl.when(from_across)
    def _():
        pl.semaphore_signal(barrier, inc=1, device_id={"layer": me - 1}, device_id_type=MESH)

    wide[...] = kernels[...].astype(F32)
    damp_wide[...] = jnp.zeros_like(damp_wide)
    damp_wide[pl.ds(0, layers)] = damping[...]
    packs = (pack_a, pack_b)
    for packed in packs:
        clear_edges(packed)
    pl.semaphore_wait(barrier, chips + ring - 1 + across.astype(jnp.int32) + from_across.astype(jnp.int32))

    own_share = pl.ds(pl.multiple_of(line * share, 8), share)

    def to(source, target, send, recv, device):
        return pltpu.make_async_remote_copy(
            src_ref=source, dst_ref=target, send_sem=send, recv_sem=recv, device_id=device, device_id_type=MESH
        )

    after_slab = {"layer": lax.rem(me + 1, slabs)}
    before_slab = {"layer": lax.rem(me + slabs - 1, slabs)}

    def full_copy(layer):
        return to(wide.at[layer], before.at[layer], full_send.at[layer], full_recv.at[layer], after_slab)

    def part_copy(layer):
        return to(
            wide.at[layer, own_share], before.at[layer, own_share], part_send.at[layer], part_recv.at[layer], after_slab
        )

    far_line = lax.rem(line + 2, ring)

    def direct_copy(layer):
        rows = pl.ds(pl.multiple_of(far_line * share + share // 2, 8), share // 2)
        return to(
            wide.at[layer, rows], before.at[layer, rows],
            direct_send.at[layer], direct_recv.at[layer], after_slab,
        )

    def damp_copy(way, target, device):
        return to(damp_wide, target, damp_send.at[way], damp_recv.at[way], device)

    def next_copy():
        return to(wide.at[:, own_share], quarter, next_send, next_recv, before_slab)

    def back_copy():
        return to(wide, after, back_send, back_recv, before_slab)

    damp_up = damp_copy(0, damp_before, after_slab)
    damp_down = damp_copy(1, damp_after, before_slab)

    @pl.when(core == 0)
    def _():
        damp_up.start()
        for layer in range(layers):
            full_copy(layer).start()

    @pl.when(across)
    def _():
        damp_up.start()
        for layer in range(layers):
            part_copy(layer).start()
            direct_copy(layer).start()

    @pl.when(me > 0)
    def _():
        damp_down.start()

    @pl.when(from_across)
    def _():
        next_copy().start()

    @pl.when(core == 1)
    def _():
        back_copy().start()

    pack_field(pack_a, images)

    taps = wide[0].reshape(depth // channels, channels, channels)
    tap_sum = taps[0]
    for tap in range(1, depth // channels):
        tap_sum = tap_sum + taps[tap]
    scale = layers * STEP
    line_at = lax.broadcasted_iota(jnp.int32, (channels, channels), 0)
    col_at = lax.broadcasted_iota(jnp.int32, (channels, channels), 1)
    decay = jnp.broadcast_to((1.0 - scale * damping[0, :]).reshape(1, channels), (channels, channels))
    matrix = jnp.where(line_at == col_at, decay, 0.0) + scale * tap_sum
    own_matrix[...] = matrix
    matrices[me] = matrix

    def far_copy(other):
        return to(
            own_matrix, matrices.at[me], far_send.at[other], far_recv.at[chip], {"layer": other * 2 + core}
        )

    def far_arrival(other):
        return to(
            own_matrix, matrices.at[other * 2 + core], far_send.at[other], far_recv.at[other],
            {"layer": other * 2 + core},
        )

    def pair_copy(other):
        slab = other * 2 + core
        return to(matrices.at[slab], matrices.at[slab], pair_send.at[other], pair_recv.at[other], {"layer": partner})

    def pair_arrival(other):
        slab = other * 2 + 1 - core
        return to(matrices.at[slab], matrices.at[slab], pair_send.at[other], pair_recv.at[other], {"layer": partner})

    def send_far(step, carry):
        far_copy(turned(step)).start()
        return carry

    def relay_copy(layer, step):
        rows = pl.ds(pl.multiple_of(line * share, 8), share // 2 if step == 2 else share)
        return to(
            before.at[layer, rows], before.at[layer, rows],
            relay_send.at[layer * ring + step], relay_recv.at[layer * ring + step],
            {"dp": lax.rem(line + step, ring)},
        )

    def relay_arrival(layer, step):
        size = share // 2 if step == 2 else share
        rows = pl.ds(pl.multiple_of(lax.rem(line + ring - step, ring) * share, 8), size)
        return to(
            before.at[layer, rows], before.at[layer, rows],
            relay_send.at[layer * ring + step], relay_recv.at[layer * ring + step],
            {"dp": lax.rem(line + step, ring)},
        )

    @pl.when(from_across)
    def _():
        for layer in range(layers):
            part_copy(layer).wait_recv()
            for step in range(1, ring):
                relay_copy(layer, step).start()

    pair_copy(chip).start()

    @pl.when(me == 0)
    def _():
        before[...] = jnp.zeros_like(before)
        damp_before[...] = jnp.zeros_like(damp_before)

    @pl.when(me > 0)
    def _():
        damp_up.wait_recv()

    for layer in range(layers):

        @pl.when(from_across)
        def _():
            direct_copy(layer).wait_recv()
            for step in range(1, ring):
                relay_arrival(layer, step).wait_recv()

        @pl.when(core == 1)
        def _():
            full_copy(layer).wait_recv()

        if layer == 1:
            lax.fori_loop(1, chips, send_far, 0)
        advance_layer(layer, layers, images, start, packs, weights, before, damp_before)

    choose_rows(me == 0, images, start)

    def after_rows(step):
        return pl.ds(pl.multiple_of(lax.rem(line + ring - step, ring) * share, 8), share)

    def after_copy(step):
        return to(
            quarter, after.at[:, own_share], after_send.at[step - 1], after_recv.at[step - 1],
            {"dp": lax.rem(line + step, ring)},
        )

    def after_arrival(step):
        return to(
            quarter, after.at[:, after_rows(step)], after_send.at[step - 1], after_recv.at[step - 1],
            {"dp": lax.rem(line + step, ring)},
        )

    @pl.when(across)
    def _():
        next_copy().wait_recv()
        for step in range(1, ring):
            after_copy(step).start()
        after[:, own_share] = quarter[...]

    pack_field(pack_a, start)
    run_forward(start, offsets, packs, weights, kernels, damping)
    packed_matrix = pack_matrix(matrix, False)

    def put(at, value):
        offsets[at] = offsets[at] - value

    rows_times(start, packed_matrix, False, put)
    stores = [pltpu.make_async_copy(offsets, offsets_hbm, store_sems.at[0])]
    stores[0].start()

    def pass_on(step, carry):
        other = turned(step)
        far_arrival(other).wait_recv()
        pair_copy(other).start()
        return carry

    def pair_ready():
        pair_arrival(chip).wait_recv()

    def all_ready():
        lax.fori_loop(1, chips, pass_on, 0)

        def arrived(step, carry):
            pair_arrival(turned(step)).wait_recv()
            return carry

        lax.fori_loop(1, chips, arrived, 0)
        stores.append(pltpu.make_async_copy(matrices, matrices_hbm, store_sems.at[1]))
        stores[1].start()

        @pl.when(me == slabs - 1)
        def _():
            after[...] = jnp.zeros_like(after)

        @pl.when(core == 0)
        def _():
            back_copy().wait_recv()

        @pl.when(across)
        def _():
            for step in range(1, ring):
                after_arrival(step).wait_recv()

        stores.append(pltpu.make_async_copy(after, after_hbm, store_sems.at[2]))
        stores[2].start()

    chain_steps(chips, False, window, images, offsets, matrices, begins, chain, pair_ready, all_ready)

    @pl.when(from_across)
    def _():
        for layer in range(layers):
            for step in range(1, ring):
                relay_copy(layer, step).wait_send()

    @pl.when(me > 0)
    def _():
        damp_down.wait_send()

    @pl.when(from_across)
    def _():
        next_copy().wait_send()

    @pl.when(core == 1)
    def _():
        back_copy().wait_send()

    @pl.when(me < slabs - 1)
    def _():
        damp_up.wait_send()
        damp_down.wait_recv()

    @pl.when(me == slabs - 1)
    def _():
        damp_after[...] = jnp.zeros_like(damp_after)

    @pl.when(core == 0)
    def _():
        for layer in range(layers):
            full_copy(layer).wait_send()

    @pl.when(across)
    def _():
        for layer in range(layers):
            part_copy(layer).wait_send()
            direct_copy(layer).wait_send()

    def settle(step, carry):
        far_copy(turned(step)).wait_send()
        return carry

    lax.fori_loop(1, chips, settle, 0)

    def settle_pair(step, carry):
        pair_copy(turned(step)).wait_send()
        return carry

    lax.fori_loop(0, chips, settle_pair, 0)

    @pl.when(across)
    def _():
        for step in range(1, ring):
            after_copy(step).wait_send()

    for store in stores:
        store.wait()


def run_forward_kernel(images, kernels, damping, slabs, ring, packed, weights):
    chips = slabs // 2
    layers, depth, channels = kernels.shape
    dma = pltpu.SemaphoreType.DMA
    window, chain = chain_scratch(images.shape[0], slabs, channels)
    field = jax.ShapeDtypeStruct(images.shape, F32)
    outs = (
        field,
        field,
        jax.ShapeDtypeStruct(kernels.shape, F32),
        jax.ShapeDtypeStruct((8, channels), F32),
        jax.ShapeDtypeStruct((slabs, channels, channels), F32),
        jax.ShapeDtypeStruct((channels, channels), F32),
    )
    anywhere = pl.BlockSpec(memory_space=pl.ANY)
    (vmem,) = in_vmem(1)
    return pl.pallas_call(
        functools.partial(forward_kernel, chips, ring, window),
        out_shape=outs,
        in_specs=in_vmem(3),
        out_specs=(vmem, anywhere, anywhere, vmem, anywhere, vmem),
        scratch_shapes=[
            pltpu.VMEM(images.shape, F32),
            pltpu.VMEM(kernels.shape, F32),
            pltpu.VMEM((slabs, channels, channels), F32),
            pltpu.VMEM(kernels.shape, F32),
            pltpu.VMEM((8, channels), F32),
            pltpu.VMEM(kernels.shape, F32),
            pltpu.VMEM((8, channels), F32),
            pltpu.VMEM((layers, depth // ring, channels), F32),
            pltpu.VMEM(images.shape, F32),
        ]
        + packed
        + weights
        + [dma((3,))]
        + [dma((layers,))] * 6
        + [dma((layers * ring,))] * 2
        + [dma, dma, dma((2,)), dma((2,))]
        + [dma((chips,))] * 4
        + [dma((ring - 1,))] * 2
        + [dma] * 2
        + chain,
        compiler_params=pltpu.CompilerParams(
            vmem_limit_bytes=VMEM_BYTES, collective_id=1, has_side_effects=True
        ),
        name="forward",
    )(images, kernels, damping)


def place_kernel(*refs):
    half = len(refs) // 2
    for source, target in zip(refs[:half], refs[half:]):
        target[...] = source[...]


def place(*arrays):
    parts = 2

    def specs():
        return [pl.BlockSpec((a.shape[0] // parts, a.shape[1]), lambda i: (i, 0)) for a in arrays]

    return pl.pallas_call(
        place_kernel,
        grid=(parts,),
        out_shape=[jax.ShapeDtypeStruct(a.shape, a.dtype) for a in arrays],
        in_specs=specs(),
        out_specs=specs(),
        compiler_params=pltpu.CompilerParams(vmem_limit_bytes=VMEM_BYTES),
        name="place",
    )(*arrays)


def run_final(tops, kernels, damping, matrix, back_offsets, gates, kept, ring, packed, weights):
    layers, depth, channels = kernels.shape
    moves = layers * 2 * (ring - 1)
    dma = pltpu.SemaphoreType.DMA
    state = jax.ShapeDtypeStruct(tops.shape, F32)
    anywhere = pl.BlockSpec(memory_space=pl.ANY)
    return pl.pallas_call(
        functools.partial(final_kernel, ring),
        out_shape=(state, state, jax.ShapeDtypeStruct(kernels.shape, F32)),
        in_specs=in_vmem(4) + [anywhere] * 3,
        out_specs=(anywhere,) * 3,
        scratch_shapes=packed
        + weights
        + [
            pltpu.VMEM(tops.shape, F32),
            pltpu.VMEM(gates.shape, F32),
            pltpu.VMEM(kept.shape, BF16),
            pltpu.VMEM(tops.shape, F32),
            pltpu.VMEM(tops.shape, F32),
            pltpu.VMEM(kernels.shape, F32),
            pltpu.VMEM(kernels.shape, F32),
            pltpu.VMEM((moves, depth // (2 * ring), channels), F32),
        ]
        + [dma((moves,))] * 4
        + [dma((2 * layers + 1,)), dma((layers + 2,))],
        compiler_params=pltpu.CompilerParams(
            vmem_limit_bytes=VMEM_BYTES, collective_id=4, has_side_effects=True
        ),
        name="final",
    )(tops, kernels, damping, matrix, back_offsets, gates, kept)


def per_device(images, kernels, damping, cotangent):
    slab, depth, channels = kernels.shape
    side = images.shape[1]
    slabs = lax.axis_size("layer")
    ring = lax.axis_size("dp")
    pairs = side // 2
    flat = (side * side, channels)
    images_flat, cot_flat = images.reshape(flat), cotangent.reshape(flat)
    packed = [pltpu.VMEM((3, 2, pairs + 1, WIDE, channels), BF16)] * 2
    weights = [pltpu.VMEM((12 * channels, 2 * channels), BF16)]
    weights_back = [pltpu.VMEM((2 * channels, 12 * channels), BF16)]

    begins, offsets, after, damp_after, matrices, matrix = run_forward_kernel(
        images_flat, kernels, damping, slabs, ring, packed, weights
    )
    slab_end, coarse_end, back_offsets, gates, kept, tops = run_middle(
        begins, kernels, damping, damp_after, matrix, offsets, after, cot_flat, matrices, packed, weights + weights_back
    )
    adjoint_start, adjoint_coarse, grads = run_final(
        tops, kernels, damping, matrix, back_offsets, gates, kept, ring, packed, weights_back
    )
    slab_end, coarse_end, adjoint_start, adjoint_coarse, grads = place(
        slab_end, coarse_end, adjoint_start, adjoint_coarse, grads.reshape(slab * depth, channels)
    )
    full = (1,) + images.shape
    return (
        slab_end.reshape(full),
        coarse_end.reshape(full),
        adjoint_start.reshape(full),
        adjoint_coarse.reshape(full),
        grads.reshape(kernels.shape),
    )


def solution(mesh):
    in_specs = (
        P("dp", None, None, None),
        P("layer", None, None),
        P("layer", None),
        P("dp", None, None, None),
    )
    out_specs = (
        P("layer", "dp", None, None, None),
        P("layer", "dp", None, None, None),
        P("layer", "dp", None, None, None),
        P("layer", "dp", None, None, None),
        P("layer", None, None),
    )
    return jax.shard_map(
        per_device, mesh=mesh, in_specs=in_specs, out_specs=out_specs, check_vma=False
    )
```

```python
import functools

import jax
import jax.numpy as jnp
from jax import lax
from jax.experimental import pallas as pl
from jax.experimental.pallas import tpu as pltpu
from jax.sharding import PartitionSpec as P

STEP = 0.125
F32 = jnp.float32
BF16 = jnp.bfloat16
MESH = pl.DeviceIdType.MESH
VMEM_BYTES = 60 * 1024 * 1024
GROUP = 7


def split(value):
    high = value.astype(BF16)
    return high, (value - high.astype(F32)).astype(BF16)


def pack_matrix(matrix, transposed):
    high, low = split(matrix)
    if transposed:
        top = jnp.concatenate([high, high], axis=1)
        bottom = jnp.concatenate([low, jnp.zeros_like(low)], axis=1)
    else:
        top = jnp.concatenate([high, low], axis=1)
        bottom = jnp.concatenate([high, jnp.zeros_like(low)], axis=1)
    return jnp.concatenate([top, bottom], axis=0)


def times(rows, packed, transposed):
    channels = rows.shape[1]
    both = jnp.concatenate(split(rows), axis=1)
    dims = (((1,), (1 if transposed else 0,)), ((), ()))
    result = lax.dot_general(both, packed, dims, preferred_element_type=F32)
    return result[:, :channels] + result[:, channels:]


def clear_edges(packed):
    zeros = jnp.zeros(packed.shape[3:], packed.dtype)
    for col in range(3):
        packed[col, 0, 0] = zeros
        packed[col, 1, packed.shape[2] - 1] = zeros


def pack_rows(packed, first, even, odd):
    count, side, channels = even.shape
    column = lax.broadcasted_iota(jnp.int32, even.shape, 1)
    for parity, value in ((1, even), (0, odd)):
        start = first if parity == 1 else first + 1
        left = jnp.where(column == 0, 0.0, pltpu.roll(value, 1, 1))
        right = jnp.where(column == side - 1, 0.0, pltpu.roll(value, side - 1, 1))
        for col, moved in enumerate((left, value, right)):
            packed[col, parity, pl.ds(start, count)] = moved.astype(BF16)


def pieces(packed, first, count):
    channels = packed.shape[-1]
    rows = count * packed.shape[3]
    out = []
    for col in range(3):
        for parity, ahead in ((1, 0), (0, 1), (0, 0), (1, 1)):
            out.append(packed[col, parity, pl.ds(first + ahead, count)].reshape(rows, channels))
    return out


OFFSETS = (0, 1, -1, 2)


def fill_weights(weights, kernel, backward):
    channels = weights.shape[1] // 2 if not backward else weights.shape[0] // 2
    zero = jnp.zeros((channels, channels), BF16)
    for col in range(3):
        for place, offset in enumerate(OFFSETS):
            at = pl.ds((col * 4 + place) * channels, channels)
            for row in range(2):
                tap = offset - row + 1
                if 0 <= tap <= 2:
                    index = tap * 3 + col
                    block = kernel(8 - index if backward else index).astype(BF16)
                else:
                    block = zero
                out = pl.ds(row * channels, channels)
                if backward:
                    weights[out, at] = block
                else:
                    weights[at, out] = block


def convolve(packed, weights, first, count, side, backward):
    left = jnp.concatenate(pieces(packed, first, count), axis=1)
    dims = (((1,), (1 if backward else 0,)), ((), ()))
    result = lax.dot_general(left, weights[...], dims, preferred_element_type=F32)
    channels = result.shape[1] // 2
    result = result.reshape(count, side, 2 * channels)
    return result[:, :, :channels], result[:, :, channels:]


def each_group(pairs, body):
    def step(index, carry):
        body(index * GROUP)
        return carry

    lax.fori_loop(0, pairs // GROUP, step, 0, unroll=True)


def rows_at(first, side):
    return pl.ds(pl.multiple_of(first * 2 * side, 8), GROUP * 2 * side)


def pair_rows(value, side):
    value = value.reshape(GROUP, 2, side, value.shape[-1])
    return value[:, 0], value[:, 1]


def flat_rows(even, odd):
    return jnp.stack([even, odd], axis=1).reshape(-1, even.shape[-1])


def pack_field(packed, field):
    pairs = packed.shape[2] - 1

    def body(first):
        even, odd = pair_rows(field[rows_at(first, 2 * pairs)], 2 * pairs)
        pack_rows(packed, first, even, odd)

    each_group(pairs, body)


def tap_of(ref, layer, channels):
    return lambda tap: ref[layer, pl.ds(tap * channels, channels), :]


def advance_layer(layer, layers, source, target, packs, weights, kernels, damping, gates=None, kept=None):
    channels = source.shape[-1]
    pairs = packs[0].shape[2] - 1
    side = 2 * pairs
    now, later = packs[layer % 2], packs[(layer + 1) % 2]
    fill_weights(weights, tap_of(kernels, layer, channels), False)
    decay = damping[layer, :].reshape(1, 1, channels)
    state = source if layer == 0 else target

    def body(first):
        at = rows_at(first, side)
        outs = convolve(now, weights, first, GROUP, side, False)
        nexts, slopes = [], []
        for out, current in zip(outs, pair_rows(state[at], side)):
            act = jnp.tanh(out)
            slopes.append(STEP * (1.0 - act * act))
            nexts.append(current + STEP * (act - decay * current))
        target[at] = flat_rows(*nexts)
        if gates is not None:
            gates[layer, at] = flat_rows(*slopes)
        if kept is not None:
            kept[layer, 0, pl.ds(first, GROUP)] = now[1, 1, pl.ds(first, GROUP)]
            kept[layer, 1, pl.ds(first, GROUP)] = now[1, 0, pl.ds(first + 1, GROUP)]
        if layer + 1 < layers:
            pack_rows(later, first, *nexts)

    each_group(pairs, body)


def run_forward(source, target, packs, weights, kernels, damping, gates=None, kept=None):
    layers = kernels.shape[0]
    for layer in range(layers):
        advance_layer(layer, layers, source, target, packs, weights, kernels, damping, gates, kept)


def pack_scaled(packed, gates, layer, adjoint):
    pairs = packed.shape[2] - 1

    def body(first):
        at = rows_at(first, 2 * pairs)
        pack_rows(packed, first, *pair_rows(gates[layer, at] * adjoint[at], 2 * pairs))

    each_group(pairs, body)


def retreat_layer(turn, layers, source, target, packs, weights, kernels, damping, gates):
    channels = source.shape[-1]
    pairs = packs[0].shape[2] - 1
    side = 2 * pairs
    layer = layers - 1 - turn
    now, later = packs[turn % 2], packs[(turn + 1) % 2]
    fill_weights(weights, tap_of(kernels, layer, channels), True)
    decay = damping[layer, :].reshape(1, 1, channels)
    state = source if turn == 0 else target

    def body(first):
        at = rows_at(first, side)
        outs = convolve(now, weights, first, GROUP, side, True)
        nexts = []
        for out, current in zip(outs, pair_rows(state[at], side)):
            nexts.append(current - STEP * decay * current + out)
        target[at] = flat_rows(*nexts)
        if layer > 0:
            scaled = [gate * moved for gate, moved in zip(pair_rows(gates[layer - 1, at], side), nexts)]
            pack_rows(later, first, *scaled)

    each_group(pairs, body)


def run_backward(source, target, packs, weights, kernels, damping, gates):
    layers = gates.shape[0]
    pack_scaled(packs[0], gates, layers - 1, source)
    for turn in range(layers):
        retreat_layer(turn, layers, source, target, packs, weights, kernels, damping, gates)


def gradient(packed, kept, layer, grads):
    channels = packed.shape[-1]
    pairs = packed.shape[2] - 1
    pixels = pairs * packed.shape[3]
    left = jnp.concatenate([kept[layer, row].reshape(pixels, channels) for row in range(2)], axis=1)
    for col in range(3):
        parts = []
        for parity, ahead in ((1, 0), (0, 1), (0, 0), (1, 1)):
            parts.append(packed[col, parity, pl.ds(ahead, pairs)].reshape(pixels, channels))
        out = lax.dot_general(
            left, jnp.concatenate(parts, axis=1), (((0,), (0,)), ((), ())), preferred_element_type=F32
        )

        def block(row, offset):
            place = OFFSETS.index(offset)
            return out[row * channels : (row + 1) * channels, place * channels : (place + 1) * channels]

        for tap in range(3):
            total = block(0, 1 - tap) + block(1, 2 - tap)
            index = tap * 3 + (2 - col)
            grads[layer, pl.ds(index * channels, channels), :] = total


def rows_times(source, packed_matrix, transposed, put):
    parts = 7
    size = source.shape[0] // parts

    def body(index, carry):
        at = pl.ds(pl.multiple_of(index * size, 8), size)
        put(at, times(source[at], packed_matrix, transposed))
        return carry

    lax.fori_loop(0, parts, body, 0, unroll=True)


def choose_rows(flag, chosen, target):
    @pl.when(flag)
    def _():
        target[...] = chosen[...]


def final_kernel(
    ring, tops, kernels, damping, matrix, back_hbm, gates_hbm, kept_hbm,
    start_hbm, coarse_hbm, grads_hbm,
    pack_a, pack_b, weights, back_offset, gates, kept, start, coarse_start, local, total, landed,
    reduce_send, reduce_recv, gather_send, gather_recv, load_sems, store_sems,
):
    layers = kernels.shape[0]
    me = lax.axis_index("dp")
    neighbours = (lax.rem(me + 1, ring), lax.rem(me + ring - 1, ring))
    barrier = pltpu.get_barrier_semaphore()
    for neighbour in neighbours:
        pl.semaphore_signal(barrier, inc=1, device_id={"dp": neighbour}, device_id_type=MESH)

    loads = []
    for layer in reversed(range(layers)):
        loads.append(pltpu.make_async_copy(gates_hbm.at[layer], gates.at[layer], load_sems.at[2 * layer]))
        loads.append(pltpu.make_async_copy(kept_hbm.at[layer], kept.at[layer], load_sems.at[2 * layer + 1]))
    loads.append(pltpu.make_async_copy(back_hbm, back_offset, load_sems.at[2 * layers]))
    for load in loads:
        load.start()
    streams = 4
    size = kernels.shape[1] // (streams * ring)

    def rows_of(way, step):
        chunk = lax.rem(me + (2 * ring - step if way % 2 == 0 else step + ring), ring)
        return pl.ds(pl.multiple_of((way * ring + chunk) * size, 8), size)

    def reduce_copy(layer, way, step):
        slot = (layer * streams + way) * (ring - 1) + step
        return pltpu.make_async_remote_copy(
            src_ref=local.at[layer, rows_of(way, step)],
            dst_ref=landed.at[slot],
            send_sem=reduce_send.at[slot],
            recv_sem=reduce_recv.at[slot],
            device_id={"dp": neighbours[way % 2]},
            device_id_type=MESH,
        )

    def gather_copy(layer, way, step):
        slot = (layer * streams + way) * (ring - 1) + step
        rows = rows_of(way, step - 1)
        return pltpu.make_async_remote_copy(
            src_ref=total.at[layer, rows],
            dst_ref=total.at[layer, rows],
            send_sem=gather_send.at[slot],
            recv_sem=gather_recv.at[slot],
            device_id={"dp": neighbours[way % 2]},
            device_id_type=MESH,
        )

    def advance_ring(layer, stage):
        last = ring - 1
        for way in range(streams):
            if 1 <= stage <= last:
                slot = (layer * streams + way) * last + stage - 1
                reduce_copy(layer, way, stage - 1).wait_recv()
                rows = rows_of(way, stage)
                value = local[layer, rows] + landed[slot]
                if stage < last:
                    local[layer, rows] = value
                else:
                    total[layer, rows] = value
            elif stage > last:
                gather_copy(layer, way, stage - last - 1).wait_recv()
            if stage < last:
                reduce_copy(layer, way, stage).start()
            elif stage < 2 * last:
                gather_copy(layer, way, stage - last).start()

    packs = (pack_a, pack_b)
    for packed in packs:
        clear_edges(packed)
    packed_transposed = pack_matrix(matrix[...], True)

    def put(at, value):
        coarse_start[at] = value + back_offset[at]

    stages = 2 * (ring - 1) + 1
    reached = [0] * layers

    def forward_rings(count):
        for other in reversed(range(count)):
            layer = layers - 1 - other
            advance_ring(layer, reached[layer])
            reached[layer] += 1

    loads[0].wait()
    pack_scaled(pack_a, gates, layers - 1, tops)
    for turn in range(layers):
        layer = layers - 1 - turn
        loads[2 * turn + 1].wait()
        gradient(packs[turn % 2], kept, layer, local)
        if turn == 0:
            pl.semaphore_wait(barrier, 2)
        forward_rings(turn + 1)
        if layer > 0:
            loads[2 * turn + 2].wait()
        retreat_layer(turn, layers, tops, start, packs, weights, kernels, damping, gates)
        if turn + 1 < layers:
            forward_rings(turn + 1)
    stores = [pltpu.make_async_copy(start, start_hbm, store_sems.at[layers])]
    stores[0].start()
    forward_rings(layers)
    loads[2 * layers].wait()
    rows_times(tops, packed_transposed, True, put)
    stores.append(pltpu.make_async_copy(coarse_start, coarse_hbm, store_sems.at[layers + 1]))
    stores[1].start()
    while min(reached) < stages:
        for layer in range(layers):
            if reached[layer] < stages:
                advance_ring(layer, reached[layer])
                reached[layer] += 1
                if reached[layer] == stages:
                    store = pltpu.make_async_copy(total.at[layer], grads_hbm.at[layer], store_sems.at[layer])
                    store.start()
                    stores.append(store)
    for layer in range(layers):
        for way in range(streams):
            for step in range(ring - 1):
                reduce_copy(layer, way, step).wait_send()
                gather_copy(layer, way, step).wait_send()
    for store in stores:
        store.wait()


def in_vmem(count, scalars=0):
    return [pl.BlockSpec(memory_space=pltpu.SMEM)] * scalars + [
        pl.BlockSpec(memory_space=pltpu.VMEM)
    ] * count


def nothing():
    pass


def chain_steps(
    chips, backward, window, seed, terms, matrices, out, scratch, pair_ready=nothing, all_ready=nothing
):
    (
        partner_terms, composed, inbox, outbox, returned, handed, partner_out, packs,
        pair_send, pair_recv, in_send, in_recv, back_send, back_recv, out_send, out_recv,
    ) = scratch
    me = lax.axis_index("layer")
    chip = me // 2
    core = me % 2
    partner = me + 1 - 2 * core
    half = terms.shape[0] // 2
    lead = 1 if backward else 0
    is_lead = core == lead
    tiles = half // 8

    def start_of(other):
        return pl.multiple_of((other * tiles) // chips * 8, 8)

    def own_rows(other):
        return pl.ds(pl.multiple_of(core * half + start_of(other), 8), window)

    def other_rows(other):
        return pl.ds(pl.multiple_of((1 - core) * half + start_of(other), 8), window)

    def turned(step):
        return lax.rem(chip + step, chips)

    def pair_copy(other):
        return pltpu.make_async_remote_copy(
            src_ref=terms.at[other_rows(other)],
            dst_ref=partner_terms.at[other],
            send_sem=pair_send.at[other],
            recv_sem=pair_recv.at[other],
            device_id={"layer": partner},
            device_id_type=MESH,
        )

    def send_pair(step, carry):
        pair_copy(turned(step)).start()
        return carry

    lax.fori_loop(1, chips + 1, send_pair, 0)

    lead_slab = 2 * chip + lead
    next_slab = 2 * chip + 1 - lead
    pair_ready()
    packs[next_slab] = pack_matrix(matrices[next_slab], backward)

    def in_copy(other):
        return pltpu.make_async_remote_copy(
            src_ref=composed.at[other],
            dst_ref=inbox.at[chip],
            send_sem=in_send.at[other],
            recv_sem=in_recv.at[chip],
            device_id={"layer": other * 2 + core},
            device_id_type=MESH,
        )

    def in_arrival(other):
        return pltpu.make_async_remote_copy(
            src_ref=composed.at[other],
            dst_ref=inbox.at[other],
            send_sem=in_send.at[other],
            recv_sem=in_recv.at[other],
            device_id={"layer": other * 2 + core},
            device_id_type=MESH,
        )

    def compose(other):
        pair_copy(other).wait_recv()
        own, theirs = terms[own_rows(other)], partner_terms[other]
        led = jnp.where(is_lead, own, theirs)
        following = jnp.where(is_lead, theirs, own)
        return times(led, packs[next_slab], backward) + following

    def compose_send(step, carry):
        other = turned(step)
        composed[other] = compose(other)
        in_copy(other).start()
        return carry

    lax.fori_loop(1, chips, compose_send, 0)
    inbox[chip] = compose(chip)

    all_ready()

    def prepare(index, carry):
        packs[index] = pack_matrix(matrices[index], backward)
        return carry

    lax.fori_loop(0, 2 * chips, prepare, 0, unroll=4)

    def back_copy(other):
        return pltpu.make_async_remote_copy(
            src_ref=outbox.at[other],
            dst_ref=returned.at[chip],
            send_sem=back_send.at[other],
            recv_sem=back_recv.at[chip],
            device_id={"layer": other * 2 + core},
            device_id_type=MESH,
        )

    def back_arrival(other):
        return pltpu.make_async_remote_copy(
            src_ref=outbox.at[other],
            dst_ref=returned.at[other],
            send_sem=back_send.at[other],
            recv_sem=back_recv.at[other],
            device_id={"layer": other * 2 + core},
            device_id_type=MESH,
        )

    rows = seed[own_rows(chip)]
    group = 4
    for first in range(0, chips, group):
        steps = range(first, min(first + group, chips))
        order = [chips - 1 - step if backward else step for step in steps]
        for at in order:

            @pl.when(chip != at)
            def _():
                in_arrival(at).wait_recv()

        for step, at in zip(steps, order):
            outbox[at] = rows
            if step < chips - 1:
                rows = times(rows, packs[2 * at + lead], backward)
                rows = times(rows, packs[2 * at + 1 - lead], backward) + inbox[at]
        for at in order:

            @pl.when(chip != at)
            def _():
                back_copy(at).start()

    def hand_copy(other):
        return pltpu.make_async_remote_copy(
            src_ref=handed.at[other],
            dst_ref=partner_out.at[other],
            send_sem=out_send.at[other],
            recv_sem=out_recv.at[other],
            device_id={"layer": partner},
            device_id_type=MESH,
        )

    def finish(other, led):
        lead_terms = jnp.where(is_lead, terms[own_rows(other)], partner_terms[other])
        following = times(led, packs[lead_slab], backward) + lead_terms
        out[own_rows(other)] = jnp.where(is_lead, led, following)
        handed[other] = jnp.where(is_lead, following, led)
        hand_copy(other).start()

    finish(chip, outbox[chip])

    def finish_next(step, carry):
        other = turned(step)
        back_arrival(other).wait_recv()
        finish(other, returned[other])
        return carry

    lax.fori_loop(1, chips, finish_next, 0)

    def drain(step, carry):
        in_copy(turned(step)).wait_send()
        back_copy(turned(step)).wait_send()
        return carry

    lax.fori_loop(1, chips, drain, 0)

    def collect(step, carry):
        other = turned(step)
        pair_copy(other).wait_send()
        hand_copy(other).wait()
        out[other_rows(other)] = partner_out[other]
        return carry

    lax.fori_loop(0, chips, collect, 0)

def chain_scratch(rows, slabs, channels):
    chips = slabs // 2
    window = -(-(rows // 16) // chips) * 8
    blocks = pltpu.VMEM((chips, window, channels), F32)
    packs = pltpu.VMEM((slabs, 2 * channels, 2 * channels), BF16)
    return window, [blocks] * 7 + [packs] + [pltpu.SemaphoreType.DMA((chips,))] * 8


def greet_chain(chips):
    me = lax.axis_index("layer")
    barrier = pltpu.get_barrier_semaphore()
    pl.semaphore_signal(barrier, inc=1, device_id={"layer": me + 1 - 2 * (me % 2)}, device_id_type=MESH)

    def greet(step, carry):
        other = lax.rem(me // 2 + step, chips) * 2 + me % 2
        pl.semaphore_signal(barrier, inc=1, device_id={"layer": other}, device_id_type=MESH)
        return carry

    lax.fori_loop(1, chips, greet, 0)


def middle_kernel(
    chips, window, begins, kernels, damping, damp_after, matrix,
    offsets_hbm, after_hbm, cot_hbm, matrices_hbm,
    slab_hbm, coarse_hbm, back_hbm, gates_hbm, kept_hbm, tops,
    offsets, after, cotangent, matrices, slab_end, coarse_end, back_offset, gates, kept,
    gates_after, state, pack_a, pack_b, weights, weights_back, load_sems, store_sems, *chain,
):
    slabs = 2 * chips
    layers = kernels.shape[0]
    greet_chain(chips)
    sources = (offsets_hbm, after_hbm, cot_hbm, matrices_hbm)
    loads = [
        pltpu.make_async_copy(source, target, load_sems.at[place])
        for place, (source, target) in enumerate(zip(sources, (offsets, after, cotangent, matrices)))
    ]
    for load in loads:
        load.start()
    stores = []

    def keep(source, target):
        stores.append(pltpu.make_async_copy(source, target, store_sems.at[len(stores)]))
        stores[-1].start()

    packs = (pack_a, pack_b)
    for packed in packs:
        clear_edges(packed)
    packed_matrix = pack_matrix(matrix[...], False)
    packed_transposed = pack_matrix(matrix[...], True)
    pack_field(pack_a, begins)
    for layer in range(layers):
        advance_layer(layer, layers, begins, slab_end, packs, weights, kernels, damping, gates, kept)
        keep(gates.at[layer], gates_hbm.at[layer])
        keep(kept.at[layer], kept_hbm.at[layer])
    keep(slab_end, slab_hbm)
    loads[0].wait()

    def put(at, value):
        coarse_end[at] = value + offsets[at]

    rows_times(begins, packed_matrix, False, put)
    keep(coarse_end, coarse_hbm)
    loads[1].wait()
    pack_field(pack_a, coarse_end)
    run_forward(coarse_end, state, packs, weights, after, damp_after, gates_after)
    loads[2].wait()
    run_backward(cotangent, state, packs, weights_back, after, damp_after, gates_after)
    choose_rows(lax.axis_index("layer") == slabs - 1, cotangent, state)
    run_backward(state, back_offset, packs, weights_back, kernels, damping, gates)

    def put_back(at, value):
        back_offset[at] = back_offset[at] - value

    rows_times(state, packed_transposed, True, put_back)
    keep(back_offset, back_hbm)
    loads[3].wait()
    pl.semaphore_wait(pltpu.get_barrier_semaphore(), chips)
    chain_steps(chips, True, window, cotangent, back_offset, matrices, tops, chain)
    for store in stores:
        store.wait()


def run_middle(begins, kernels, damping, damp_after, matrix, offsets, after, cotangent, matrices, packed, weights):
    layers, depth, channels = kernels.shape
    slabs = matrices.shape[0]
    pairs = packed[0].shape[2] - 1
    window, chain = chain_scratch(begins.shape[0], slabs, channels)
    field = jax.ShapeDtypeStruct(begins.shape, F32)
    gates = jax.ShapeDtypeStruct((layers,) + begins.shape, F32)
    kept = jax.ShapeDtypeStruct((layers, 2, pairs, 2 * pairs, channels), BF16)
    anywhere = pl.BlockSpec(memory_space=pl.ANY)
    dma = pltpu.SemaphoreType.DMA
    flat = pltpu.VMEM(begins.shape, F32)
    return pl.pallas_call(
        functools.partial(middle_kernel, slabs // 2, window),
        out_shape=(field, field, field, gates, kept, field),
        in_specs=in_vmem(5) + [anywhere] * 4,
        out_specs=(anywhere,) * 5 + tuple(in_vmem(1)),
        scratch_shapes=[
            flat,
            pltpu.VMEM(kernels.shape, F32),
            flat,
            pltpu.VMEM(matrices.shape, F32),
            flat,
            flat,
            flat,
            pltpu.VMEM(gates.shape, F32),
            pltpu.VMEM(kept.shape, BF16),
            pltpu.VMEM(gates.shape, F32),
            flat,
        ]
        + packed
        + weights
        + [dma((4,)), dma((2 * layers + 3,))]
        + chain,
        compiler_params=pltpu.CompilerParams(
            vmem_limit_bytes=VMEM_BYTES, collective_id=2, has_side_effects=True
        ),
        name="middle",
    )(begins, kernels, damping, damp_after, matrix, offsets, after, cotangent, matrices)


def forward_kernel(
    chips, ring, window, images, kernels, damping,
    begins, offsets_hbm, after_hbm, damp_after, matrices_hbm, own_matrix,
    offsets, after, matrices,
    wide, damp_wide, before, damp_before, quarter, start, pack_a, pack_b, weights, store_sems,
    full_send, full_recv, part_send, part_recv, direct_send, direct_recv, relay_send, relay_recv,
    next_send, next_recv, damp_send, damp_recv, far_send, far_recv, pair_send, pair_recv,
    after_send, after_recv, back_send, back_recv, *chain,
):
    layers, depth, channels = kernels.shape
    share = depth // ring
    slabs = 2 * chips
    me = lax.axis_index("layer")
    line = lax.axis_index("dp")
    chip = me // 2
    core = me % 2
    partner = me + 1 - 2 * core
    across = (core == 1) & (me < slabs - 1)
    from_across = (core == 0) & (me > 0)

    def turned(step):
        return lax.rem(chip + step, chips)

    barrier = pltpu.get_barrier_semaphore()
    greet_chain(chips)
    for step in range(1, ring):
        pl.semaphore_signal(barrier, inc=1, device_id={"dp": lax.rem(line + step, ring)}, device_id_type=MESH)

    @pl.when(across)
    def _():
        pl.semaphore_signal(barrier, inc=1, device_id={"layer": me + 1}, device_id_type=MESH)

    @pl.when(from_across)
    def _():
        pl.semaphore_signal(barrier, inc=1, device_id={"layer": me - 1}, device_id_type=MESH)

    wide[...] = kernels[...].astype(F32)
    damp_wide[...] = jnp.zeros_like(damp_wide)
    damp_wide[pl.ds(0, layers)] = damping[...]
    packs = (pack_a, pack_b)
    for packed in packs:
        clear_edges(packed)
    pl.semaphore_wait(barrier, chips + ring - 1 + across.astype(jnp.int32) + from_across.astype(jnp.int32))

    own_share = pl.ds(pl.multiple_of(line * share, 8), share)

    def to(source, target, send, recv, device):
        return pltpu.make_async_remote_copy(
            src_ref=source, dst_ref=target, send_sem=send, recv_sem=recv, device_id=device, device_id_type=MESH
        )

    after_slab = {"layer": lax.rem(me + 1, slabs)}
    before_slab = {"layer": lax.rem(me + slabs - 1, slabs)}

    def full_copy(layer):
        return to(wide.at[layer], before.at[layer], full_send.at[layer], full_recv.at[layer], after_slab)

    def part_copy(layer):
        return to(
            wide.at[layer, own_share], before.at[layer, own_share], part_send.at[layer], part_recv.at[layer], after_slab
        )

    far_line = lax.rem(line + 2, ring)

    def direct_copy(layer):
        rows = pl.ds(pl.multiple_of(far_line * share + share // 2, 8), share // 2)
        return to(
            wide.at[layer, rows], before.at[layer, rows],
            direct_send.at[layer], direct_recv.at[layer], after_slab,
        )

    def damp_copy(way, target, device):
        return to(damp_wide, target, damp_send.at[way], damp_recv.at[way], device)

    def next_copy():
        return to(wide.at[:, own_share], quarter, next_send, next_recv, before_slab)

    def back_copy():
        return to(wide, after, back_send, back_recv, before_slab)

    damp_up = damp_copy(0, damp_before, after_slab)
    damp_down = damp_copy(1, damp_after, before_slab)

    @pl.when(core == 0)
    def _():
        damp_up.start()
        for layer in range(layers):
            full_copy(layer).start()

    @pl.when(across)
    def _():
        damp_up.start()
        for layer in range(layers):
            part_copy(layer).start()
            direct_copy(layer).start()

    @pl.when(me > 0)
    def _():
        damp_down.start()

    @pl.when(from_across)
    def _():
        next_copy().start()

    @pl.when(core == 1)
    def _():
        back_copy().start()

    pack_field(pack_a, images)

    taps = wide[0].reshape(depth // channels, channels, channels)
    tap_sum = taps[0]
    for tap in range(1, depth // channels):
        tap_sum = tap_sum + taps[tap]
    scale = layers * STEP
    line_at = lax.broadcasted_iota(jnp.int32, (channels, channels), 0)
    col_at = lax.broadcasted_iota(jnp.int32, (channels, channels), 1)
    decay = jnp.broadcast_to((1.0 - scale * damping[0, :]).reshape(1, channels), (channels, channels))
    matrix = jnp.where(line_at == col_at, decay, 0.0) + scale * tap_sum
    own_matrix[...] = matrix
    matrices[me] = matrix

    def far_copy(other):
        return to(
            own_matrix, matrices.at[me], far_send.at[other], far_recv.at[chip], {"layer": other * 2 + core}
        )

    def far_arrival(other):
        return to(
            own_matrix, matrices.at[other * 2 + core], far_send.at[other], far_recv.at[other],
            {"layer": other * 2 + core},
        )

    def pair_copy(other):
        slab = other * 2 + core
        return to(matrices.at[slab], matrices.at[slab], pair_send.at[other], pair_recv.at[other], {"layer": partner})

    def pair_arrival(other):
        slab = other * 2 + 1 - core
        return to(matrices.at[slab], matrices.at[slab], pair_send.at[other], pair_recv.at[other], {"layer": partner})

    def send_far(step, carry):
        far_copy(turned(step)).start()
        return carry

    def relay_copy(layer, step):
        rows = pl.ds(pl.multiple_of(line * share, 8), share // 2 if step == 2 else share)
        return to(
            before.at[layer, rows], before.at[layer, rows],
            relay_send.at[layer * ring + step], relay_recv.at[layer * ring + step],
            {"dp": lax.rem(line + step, ring)},
        )

    def relay_arrival(layer, step):
        size = share // 2 if step == 2 else share
        rows = pl.ds(pl.multiple_of(lax.rem(line + ring - step, ring) * share, 8), size)
        return to(
            before.at[layer, rows], before.at[layer, rows],
            relay_send.at[layer * ring + step], relay_recv.at[layer * ring + step],
            {"dp": lax.rem(line + step, ring)},
        )

    @pl.when(from_across)
    def _():
        for layer in range(layers):
            part_copy(layer).wait_recv()
            for step in range(1, ring):
                relay_copy(layer, step).start()

    pair_copy(chip).start()

    @pl.when(me == 0)
    def _():
        before[...] = jnp.zeros_like(before)
        damp_before[...] = jnp.zeros_like(damp_before)

    @pl.when(me > 0)
    def _():
        damp_up.wait_recv()

    for layer in range(layers):

        @pl.when(from_across)
        def _():
            direct_copy(layer).wait_recv()
            for step in range(1, ring):
                relay_arrival(layer, step).wait_recv()

        @pl.when(core == 1)
        def _():
            full_copy(layer).wait_recv()

        if layer == 1:
            lax.fori_loop(1, chips, send_far, 0)
        advance_layer(layer, layers, images, start, packs, weights, before, damp_before)

    choose_rows(me == 0, images, start)

    def after_rows(step):
        return pl.ds(pl.multiple_of(lax.rem(line + ring - step, ring) * share, 8), share)

    def after_copy(step):
        return to(
            quarter, after.at[:, own_share], after_send.at[step - 1], after_recv.at[step - 1],
            {"dp": lax.rem(line + step, ring)},
        )

    def after_arrival(step):
        return to(
            quarter, after.at[:, after_rows(step)], after_send.at[step - 1], after_recv.at[step - 1],
            {"dp": lax.rem(line + step, ring)},
        )

    @pl.when(across)
    def _():
        next_copy().wait_recv()
        for step in range(1, ring):
            after_copy(step).start()
        after[:, own_share] = quarter[...]

    pack_field(pack_a, start)
    run_forward(start, offsets, packs, weights, kernels, damping)
    packed_matrix = pack_matrix(matrix, False)

    def put(at, value):
        offsets[at] = offsets[at] - value

    rows_times(start, packed_matrix, False, put)
    stores = [pltpu.make_async_copy(offsets, offsets_hbm, store_sems.at[0])]
    stores[0].start()

    def pass_on(step, carry):
        other = turned(step)
        far_arrival(other).wait_recv()
        pair_copy(other).start()
        return carry

    def pair_ready():
        pair_arrival(chip).wait_recv()

    def all_ready():
        lax.fori_loop(1, chips, pass_on, 0)

        def arrived(step, carry):
            pair_arrival(turned(step)).wait_recv()
            return carry

        lax.fori_loop(1, chips, arrived, 0)
        stores.append(pltpu.make_async_copy(matrices, matrices_hbm, store_sems.at[1]))
        stores[1].start()

        @pl.when(me == slabs - 1)
        def _():
            after[...] = jnp.zeros_like(after)

        @pl.when(core == 0)
        def _():
            back_copy().wait_recv()

        @pl.when(across)
        def _():
            for step in range(1, ring):
                after_arrival(step).wait_recv()

        stores.append(pltpu.make_async_copy(after, after_hbm, store_sems.at[2]))
        stores[2].start()

    chain_steps(chips, False, window, images, offsets, matrices, begins, chain, pair_ready, all_ready)

    @pl.when(from_across)
    def _():
        for layer in range(layers):
            for step in range(1, ring):
                relay_copy(layer, step).wait_send()

    @pl.when(me > 0)
    def _():
        damp_down.wait_send()

    @pl.when(from_across)
    def _():
        next_copy().wait_send()

    @pl.when(core == 1)
    def _():
        back_copy().wait_send()

    @pl.when(me < slabs - 1)
    def _():
        damp_up.wait_send()
        damp_down.wait_recv()

    @pl.when(me == slabs - 1)
    def _():
        damp_after[...] = jnp.zeros_like(damp_after)

    @pl.when(core == 0)
    def _():
        for layer in range(layers):
            full_copy(layer).wait_send()

    @pl.when(across)
    def _():
        for layer in range(layers):
            part_copy(layer).wait_send()
            direct_copy(layer).wait_send()

    def settle(step, carry):
        far_copy(turned(step)).wait_send()
        return carry

    lax.fori_loop(1, chips, settle, 0)

    def settle_pair(step, carry):
        pair_copy(turned(step)).wait_send()
        return carry

    lax.fori_loop(0, chips, settle_pair, 0)

    @pl.when(across)
    def _():
        for step in range(1, ring):
            after_copy(step).wait_send()

    for store in stores:
        store.wait()


def run_forward_kernel(images, kernels, damping, slabs, ring, packed, weights):
    chips = slabs // 2
    layers, depth, channels = kernels.shape
    dma = pltpu.SemaphoreType.DMA
    window, chain = chain_scratch(images.shape[0], slabs, channels)
    field = jax.ShapeDtypeStruct(images.shape, F32)
    outs = (
        field,
        field,
        jax.ShapeDtypeStruct(kernels.shape, F32),
        jax.ShapeDtypeStruct((8, channels), F32),
        jax.ShapeDtypeStruct((slabs, channels, channels), F32),
        jax.ShapeDtypeStruct((channels, channels), F32),
    )
    anywhere = pl.BlockSpec(memory_space=pl.ANY)
    (vmem,) = in_vmem(1)
    return pl.pallas_call(
        functools.partial(forward_kernel, chips, ring, window),
        out_shape=outs,
        in_specs=in_vmem(3),
        out_specs=(vmem, anywhere, anywhere, vmem, anywhere, vmem),
        scratch_shapes=[
            pltpu.VMEM(images.shape, F32),
            pltpu.VMEM(kernels.shape, F32),
            pltpu.VMEM((slabs, channels, channels), F32),
            pltpu.VMEM(kernels.shape, F32),
            pltpu.VMEM((8, channels), F32),
            pltpu.VMEM(kernels.shape, F32),
            pltpu.VMEM((8, channels), F32),
            pltpu.VMEM((layers, depth // ring, channels), F32),
            pltpu.VMEM(images.shape, F32),
        ]
        + packed
        + weights
        + [dma((3,))]
        + [dma((layers,))] * 6
        + [dma((layers * ring,))] * 2
        + [dma, dma, dma((2,)), dma((2,))]
        + [dma((chips,))] * 4
        + [dma((ring - 1,))] * 2
        + [dma] * 2
        + chain,
        compiler_params=pltpu.CompilerParams(
            vmem_limit_bytes=VMEM_BYTES, collective_id=1, has_side_effects=True
        ),
        name="forward",
    )(images, kernels, damping)


def place_kernel(*refs):
    half = len(refs) // 2
    for source, target in zip(refs[:half], refs[half:]):
        target[...] = source[...]


def place(*arrays):
    parts = 2

    def specs():
        return [pl.BlockSpec((a.shape[0] // parts, a.shape[1]), lambda i: (i, 0)) for a in arrays]

    return pl.pallas_call(
        place_kernel,
        grid=(parts,),
        out_shape=[jax.ShapeDtypeStruct(a.shape, a.dtype) for a in arrays],
        in_specs=specs(),
        out_specs=specs(),
        compiler_params=pltpu.CompilerParams(vmem_limit_bytes=VMEM_BYTES),
        name="place",
    )(*arrays)


def run_final(tops, kernels, damping, matrix, back_offsets, gates, kept, ring, packed, weights):
    layers, depth, channels = kernels.shape
    moves = layers * 4 * (ring - 1)
    dma = pltpu.SemaphoreType.DMA
    state = jax.ShapeDtypeStruct(tops.shape, F32)
    anywhere = pl.BlockSpec(memory_space=pl.ANY)
    return pl.pallas_call(
        functools.partial(final_kernel, ring),
        out_shape=(state, state, jax.ShapeDtypeStruct(kernels.shape, F32)),
        in_specs=in_vmem(4) + [anywhere] * 3,
        out_specs=(anywhere,) * 3,
        scratch_shapes=packed
        + weights
        + [
            pltpu.VMEM(tops.shape, F32),
            pltpu.VMEM(gates.shape, F32),
            pltpu.VMEM(kept.shape, BF16),
            pltpu.VMEM(tops.shape, F32),
            pltpu.VMEM(tops.shape, F32),
            pltpu.VMEM(kernels.shape, F32),
            pltpu.VMEM(kernels.shape, F32),
            pltpu.VMEM((moves, depth // (4 * ring), channels), F32),
        ]
        + [dma((moves,))] * 4
        + [dma((2 * layers + 1,)), dma((layers + 2,))],
        compiler_params=pltpu.CompilerParams(
            vmem_limit_bytes=VMEM_BYTES, collective_id=4, has_side_effects=True
        ),
        name="final",
    )(tops, kernels, damping, matrix, back_offsets, gates, kept)


def per_device(images, kernels, damping, cotangent):
    slab, depth, channels = kernels.shape
    side = images.shape[1]
    slabs = lax.axis_size("layer")
    ring = lax.axis_size("dp")
    pairs = side // 2
    flat = (side * side, channels)
    images_flat, cot_flat = images.reshape(flat), cotangent.reshape(flat)
    packed = [pltpu.VMEM((3, 2, pairs + 1, side, channels), BF16)] * 2
    weights = [pltpu.VMEM((12 * channels, 2 * channels), BF16)]
    weights_back = [pltpu.VMEM((2 * channels, 12 * channels), BF16)]

    begins, offsets, after, damp_after, matrices, matrix = run_forward_kernel(
        images_flat, kernels, damping, slabs, ring, packed, weights
    )
    slab_end, coarse_end, back_offsets, gates, kept, tops = run_middle(
        begins, kernels, damping, damp_after, matrix, offsets, after, cot_flat, matrices, packed, weights + weights_back
    )
    adjoint_start, adjoint_coarse, grads = run_final(
        tops, kernels, damping, matrix, back_offsets, gates, kept, ring, packed, weights_back
    )
    slab_end, coarse_end, adjoint_start, adjoint_coarse, grads = place(
        slab_end, coarse_end, adjoint_start, adjoint_coarse, grads.reshape(slab * depth, channels)
    )
    full = (1,) + images.shape
    return (
        slab_end.reshape(full),
        coarse_end.reshape(full),
        adjoint_start.reshape(full),
        adjoint_coarse.reshape(full),
        grads.reshape(kernels.shape),
    )


def solution(mesh):
    in_specs = (
        P("dp", None, None, None),
        P("layer", None, None),
        P("layer", None),
        P("dp", None, None, None),
    )
    out_specs = (
        P("layer", "dp", None, None, None),
        P("layer", "dp", None, None, None),
        P("layer", "dp", None, None, None),
        P("layer", "dp", None, None, None),
        P("layer", None, None),
    )
    return jax.shard_map(
        per_device, mesh=mesh, in_specs=in_specs, out_specs=out_specs, check_vma=False
    )
```

```python
import functools

import jax
import jax.numpy as jnp
from jax import lax
from jax.experimental import pallas as pl
from jax.experimental.pallas import tpu as pltpu
from jax.sharding import PartitionSpec as P

STEP = 0.125
F32 = jnp.float32
BF16 = jnp.bfloat16
MESH = pl.DeviceIdType.MESH
VMEM_BYTES = 60 * 1024 * 1024
GROUP = 7


def split(value):
    high = value.astype(BF16)
    return high, (value - high.astype(F32)).astype(BF16)


def pack_matrix(matrix, transposed):
    high, low = split(matrix)
    if transposed:
        top = jnp.concatenate([high, high], axis=1)
        bottom = jnp.concatenate([low, jnp.zeros_like(low)], axis=1)
    else:
        top = jnp.concatenate([high, low], axis=1)
        bottom = jnp.concatenate([high, jnp.zeros_like(low)], axis=1)
    return jnp.concatenate([top, bottom], axis=0)


def times(rows, packed, transposed):
    channels = rows.shape[1]
    both = jnp.concatenate(split(rows), axis=1)
    dims = (((1,), (1 if transposed else 0,)), ((), ()))
    result = lax.dot_general(both, packed, dims, preferred_element_type=F32)
    return result[:, :channels] + result[:, channels:]


def clear_edges(packed):
    zeros = jnp.zeros(packed.shape[3:], packed.dtype)
    for col in range(3):
        packed[col, 0, 0] = zeros
        packed[col, 1, packed.shape[2] - 1] = zeros


def pack_rows(packed, first, even, odd):
    count, side, channels = even.shape
    column = lax.broadcasted_iota(jnp.int32, even.shape, 1)
    for parity, value in ((1, even), (0, odd)):
        start = first if parity == 1 else first + 1
        left = jnp.where(column == 0, 0.0, pltpu.roll(value, 1, 1))
        right = jnp.where(column == side - 1, 0.0, pltpu.roll(value, side - 1, 1))
        for col, moved in enumerate((left, value, right)):
            packed[col, parity, pl.ds(start, count)] = moved.astype(BF16)


def pieces(packed, first, count):
    channels = packed.shape[-1]
    rows = count * packed.shape[3]
    out = []
    for col in range(3):
        for parity, ahead in ((1, 0), (0, 1), (0, 0), (1, 1)):
            out.append(packed[col, parity, pl.ds(first + ahead, count)].reshape(rows, channels))
    return out


OFFSETS = (0, 1, -1, 2)


def fill_weights(weights, kernel, backward):
    channels = weights.shape[1] // 2 if not backward else weights.shape[0] // 2
    zero = jnp.zeros((channels, channels), BF16)
    for col in range(3):
        for place, offset in enumerate(OFFSETS):
            at = pl.ds((col * 4 + place) * channels, channels)
            for row in range(2):
                tap = offset - row + 1
                if 0 <= tap <= 2:
                    index = tap * 3 + col
                    block = kernel(8 - index if backward else index).astype(BF16)
                else:
                    block = zero
                out = pl.ds(row * channels, channels)
                if backward:
                    weights[out, at] = block
                else:
                    weights[at, out] = block


def convolve(packed, weights, first, count, side, backward):
    left = jnp.concatenate(pieces(packed, first, count), axis=1)
    dims = (((1,), (1 if backward else 0,)), ((), ()))
    result = lax.dot_general(left, weights[...], dims, preferred_element_type=F32)
    channels = result.shape[1] // 2
    result = result.reshape(count, side, 2 * channels)
    return result[:, :, :channels], result[:, :, channels:]


def each_group(pairs, body):
    def step(index, carry):
        body(index * GROUP)
        return carry

    lax.fori_loop(0, pairs // GROUP, step, 0, unroll=True)


def rows_at(first, side):
    return pl.ds(pl.multiple_of(first * 2 * side, 8), GROUP * 2 * side)


def pair_rows(value, side):
    value = value.reshape(GROUP, 2, side, value.shape[-1])
    return value[:, 0], value[:, 1]


def flat_rows(even, odd):
    return jnp.stack([even, odd], axis=1).reshape(-1, even.shape[-1])


def pack_field(packed, field):
    pairs = packed.shape[2] - 1

    def body(first):
        even, odd = pair_rows(field[rows_at(first, 2 * pairs)], 2 * pairs)
        pack_rows(packed, first, even, odd)

    each_group(pairs, body)


def tap_of(ref, layer, channels):
    return lambda tap: ref[layer, pl.ds(tap * channels, channels), :]


def advance_layer(layer, layers, source, target, packs, weights, kernels, damping, gates=None, kept=None):
    channels = source.shape[-1]
    pairs = packs[0].shape[2] - 1
    side = 2 * pairs
    now, later = packs[layer % 2], packs[(layer + 1) % 2]
    weights = weights[layer % 2]
    fill_weights(weights, tap_of(kernels, layer, channels), False)
    decay = damping[layer, :].reshape(1, 1, channels)
    state = source if layer == 0 else target

    def body(first):
        at = rows_at(first, side)
        outs = convolve(now, weights, first, GROUP, side, False)
        nexts, slopes = [], []
        for out, current in zip(outs, pair_rows(state[at], side)):
            act = jnp.tanh(out)
            slopes.append(STEP * (1.0 - act * act))
            nexts.append(current + STEP * (act - decay * current))
        target[at] = flat_rows(*nexts)
        if gates is not None:
            gates[layer, at] = flat_rows(*slopes)
        if kept is not None:
            kept[layer, 0, pl.ds(first, GROUP)] = now[1, 1, pl.ds(first, GROUP)]
            kept[layer, 1, pl.ds(first, GROUP)] = now[1, 0, pl.ds(first + 1, GROUP)]
        if layer + 1 < layers:
            pack_rows(later, first, *nexts)

    each_group(pairs, body)


def run_forward(source, target, packs, weights, kernels, damping, gates=None, kept=None):
    layers = kernels.shape[0]
    for layer in range(layers):
        advance_layer(layer, layers, source, target, packs, weights, kernels, damping, gates, kept)


def pack_scaled(packed, gates, layer, adjoint):
    pairs = packed.shape[2] - 1

    def body(first):
        at = rows_at(first, 2 * pairs)
        pack_rows(packed, first, *pair_rows(gates[layer, at] * adjoint[at], 2 * pairs))

    each_group(pairs, body)


def retreat_layer(turn, layers, source, target, packs, weights, kernels, damping, gates):
    channels = source.shape[-1]
    pairs = packs[0].shape[2] - 1
    side = 2 * pairs
    layer = layers - 1 - turn
    now, later = packs[turn % 2], packs[(turn + 1) % 2]
    weights = weights[turn % 2]
    fill_weights(weights, tap_of(kernels, layer, channels), True)
    decay = damping[layer, :].reshape(1, 1, channels)
    state = source if turn == 0 else target

    def body(first):
        at = rows_at(first, side)
        outs = convolve(now, weights, first, GROUP, side, True)
        nexts = []
        for out, current in zip(outs, pair_rows(state[at], side)):
            nexts.append(current - STEP * decay * current + out)
        target[at] = flat_rows(*nexts)
        if layer > 0:
            scaled = [gate * moved for gate, moved in zip(pair_rows(gates[layer - 1, at], side), nexts)]
            pack_rows(later, first, *scaled)

    each_group(pairs, body)


def run_backward(source, target, packs, weights, kernels, damping, gates):
    layers = gates.shape[0]
    pack_scaled(packs[0], gates, layers - 1, source)
    for turn in range(layers):
        retreat_layer(turn, layers, source, target, packs, weights, kernels, damping, gates)


def gradient(packed, kept, layer, grads):
    channels = packed.shape[-1]
    pairs = packed.shape[2] - 1
    pixels = pairs * packed.shape[3]
    left = jnp.concatenate([kept[layer, row].reshape(pixels, channels) for row in range(2)], axis=1)
    for col in range(3):
        parts = []
        for parity, ahead in ((1, 0), (0, 1), (0, 0), (1, 1)):
            parts.append(packed[col, parity, pl.ds(ahead, pairs)].reshape(pixels, channels))
        out = lax.dot_general(
            left, jnp.concatenate(parts, axis=1), (((0,), (0,)), ((), ())), preferred_element_type=F32
        )

        def block(row, offset):
            place = OFFSETS.index(offset)
            return out[row * channels : (row + 1) * channels, place * channels : (place + 1) * channels]

        for tap in range(3):
            total = block(0, 1 - tap) + block(1, 2 - tap)
            index = tap * 3 + (2 - col)
            grads[layer, pl.ds(index * channels, channels), :] = total


def rows_times(source, packed_matrix, transposed, put):
    parts = 7
    size = source.shape[0] // parts

    def body(index, carry):
        at = pl.ds(pl.multiple_of(index * size, 8), size)
        put(at, times(source[at], packed_matrix, transposed))
        return carry

    lax.fori_loop(0, parts, body, 0, unroll=True)


def choose_rows(flag, chosen, target):
    @pl.when(flag)
    def _():
        target[...] = chosen[...]


def final_kernel(
    ring, tops, kernels, damping, matrix, back_hbm, gates_hbm, kept_hbm,
    start_hbm, coarse_hbm, grads_hbm,
    pack_a, pack_b, weights_a, weights_b, back_offset, gates, kept, start, coarse_start, local, total, landed,
    reduce_send, reduce_recv, gather_send, gather_recv, load_sems, store_sems,
):
    layers = kernels.shape[0]
    me = lax.axis_index("dp")
    neighbours = (lax.rem(me + 1, ring), lax.rem(me + ring - 1, ring))
    barrier = pltpu.get_barrier_semaphore()
    for neighbour in neighbours:
        pl.semaphore_signal(barrier, inc=1, device_id={"dp": neighbour}, device_id_type=MESH)

    loads = []
    for layer in reversed(range(layers)):
        loads.append(pltpu.make_async_copy(gates_hbm.at[layer], gates.at[layer], load_sems.at[2 * layer]))
        loads.append(pltpu.make_async_copy(kept_hbm.at[layer], kept.at[layer], load_sems.at[2 * layer + 1]))
    loads.append(pltpu.make_async_copy(back_hbm, back_offset, load_sems.at[2 * layers]))
    for load in loads:
        load.start()
    streams = 2
    size = kernels.shape[1] // (streams * ring)

    def rows_of(way, step):
        chunk = lax.rem(me + (2 * ring - step if way % 2 == 0 else step + ring), ring)
        return pl.ds(pl.multiple_of((way * ring + chunk) * size, 8), size)

    def reduce_copy(layer, way, step):
        slot = (layer * streams + way) * (ring - 1) + step
        return pltpu.make_async_remote_copy(
            src_ref=local.at[layer, rows_of(way, step)],
            dst_ref=landed.at[slot],
            send_sem=reduce_send.at[slot],
            recv_sem=reduce_recv.at[slot],
            device_id={"dp": neighbours[way % 2]},
            device_id_type=MESH,
        )

    def gather_copy(layer, way, step):
        slot = (layer * streams + way) * (ring - 1) + step
        rows = rows_of(way, step - 1)
        return pltpu.make_async_remote_copy(
            src_ref=total.at[layer, rows],
            dst_ref=total.at[layer, rows],
            send_sem=gather_send.at[slot],
            recv_sem=gather_recv.at[slot],
            device_id={"dp": neighbours[way % 2]},
            device_id_type=MESH,
        )

    def advance_ring(layer, stage):
        last = ring - 1
        for way in range(streams):
            if 1 <= stage <= last:
                slot = (layer * streams + way) * last + stage - 1
                reduce_copy(layer, way, stage - 1).wait_recv()
                rows = rows_of(way, stage)
                value = local[layer, rows] + landed[slot]
                if stage < last:
                    local[layer, rows] = value
                else:
                    total[layer, rows] = value
            elif stage > last:
                gather_copy(layer, way, stage - last - 1).wait_recv()
            if stage < last:
                reduce_copy(layer, way, stage).start()
            elif stage < 2 * last:
                gather_copy(layer, way, stage - last).start()

    packs = (pack_a, pack_b)
    weights = (weights_a, weights_b)
    for packed in packs:
        clear_edges(packed)
    packed_transposed = pack_matrix(matrix[...], True)

    def put(at, value):
        coarse_start[at] = value + back_offset[at]

    stages = 2 * (ring - 1) + 1
    reached = [0] * layers
    stores = []

    def forward_rings(order):
        for layer in order:
            if layer < layers and reached[layer] < stages:
                advance_ring(layer, reached[layer])
                reached[layer] += 1
                if reached[layer] == stages:
                    store = pltpu.make_async_copy(total.at[layer], grads_hbm.at[layer], store_sems.at[layer])
                    store.start()
                    stores.append(store)

    loads[0].wait()
    pack_scaled(pack_a, gates, layers - 1, tops)
    for turn in range(layers):
        layer = layers - 1 - turn
        loads[2 * turn + 1].wait()
        gradient(packs[turn % 2], kept, layer, local)
        if turn == 0:
            pl.semaphore_wait(barrier, 2)
        forward_rings(range(layer, layers))
        if layer > 0:
            loads[2 * turn + 2].wait()
        retreat_layer(turn, layers, tops, start, packs, weights, kernels, damping, gates)
    stores.append(pltpu.make_async_copy(start, start_hbm, store_sems.at[layers]))
    stores[-1].start()
    forward_rings((0, 1))
    loads[2 * layers].wait()
    rows_times(tops, packed_transposed, True, put)
    stores.append(pltpu.make_async_copy(coarse_start, coarse_hbm, store_sems.at[layers + 1]))
    stores[-1].start()
    forward_rings((0, 2, 1, 0, 2, 0, 1, 0, 2, 1, 0, 2, 1))
    while min(reached) < stages:
        forward_rings(range(layers))
    for layer in range(layers):
        for way in range(streams):
            for step in range(ring - 1):
                reduce_copy(layer, way, step).wait_send()
                gather_copy(layer, way, step).wait_send()
    for store in stores:
        store.wait()


def in_vmem(count, scalars=0):
    return [pl.BlockSpec(memory_space=pltpu.SMEM)] * scalars + [
        pl.BlockSpec(memory_space=pltpu.VMEM)
    ] * count


def nothing():
    pass


def chain_steps(
    chips, backward, window, seed, terms, matrices, out, scratch, pair_ready=nothing, all_ready=nothing
):
    (
        partner_terms, composed, inbox, outbox, returned, handed, partner_out, packs,
        pair_send, pair_recv, in_send, in_recv, back_send, back_recv, out_send, out_recv,
    ) = scratch
    me = lax.axis_index("layer")
    chip = me // 2
    core = me % 2
    partner = me + 1 - 2 * core
    half = terms.shape[0] // 2
    lead = 1 if backward else 0
    is_lead = core == lead
    tiles = half // 8

    def start_of(other):
        return pl.multiple_of((other * tiles) // chips * 8, 8)

    def own_rows(other):
        return pl.ds(pl.multiple_of(core * half + start_of(other), 8), window)

    def other_rows(other):
        return pl.ds(pl.multiple_of((1 - core) * half + start_of(other), 8), window)

    def turned(step):
        return lax.rem(chip + step, chips)

    def pair_copy(other):
        return pltpu.make_async_remote_copy(
            src_ref=terms.at[other_rows(other)],
            dst_ref=partner_terms.at[other],
            send_sem=pair_send.at[other],
            recv_sem=pair_recv.at[other],
            device_id={"layer": partner},
            device_id_type=MESH,
        )

    def send_pair(step, carry):
        pair_copy(turned(step)).start()
        return carry

    lax.fori_loop(1, chips + 1, send_pair, 0)

    lead_slab = 2 * chip + lead
    next_slab = 2 * chip + 1 - lead
    pair_ready()
    packs[next_slab] = pack_matrix(matrices[next_slab], backward)

    def in_copy(other):
        return pltpu.make_async_remote_copy(
            src_ref=composed.at[other],
            dst_ref=inbox.at[chip],
            send_sem=in_send.at[other],
            recv_sem=in_recv.at[chip],
            device_id={"layer": other * 2 + core},
            device_id_type=MESH,
        )

    def in_arrival(other):
        return pltpu.make_async_remote_copy(
            src_ref=composed.at[other],
            dst_ref=inbox.at[other],
            send_sem=in_send.at[other],
            recv_sem=in_recv.at[other],
            device_id={"layer": other * 2 + core},
            device_id_type=MESH,
        )

    def compose(other):
        pair_copy(other).wait_recv()
        own, theirs = terms[own_rows(other)], partner_terms[other]
        led = jnp.where(is_lead, own, theirs)
        following = jnp.where(is_lead, theirs, own)
        return times(led, packs[next_slab], backward) + following

    def compose_send(step, carry):
        other = turned(step)
        composed[other] = compose(other)
        in_copy(other).start()
        return carry

    lax.fori_loop(1, chips, compose_send, 0)
    inbox[chip] = compose(chip)

    all_ready()

    def prepare(index, carry):
        packs[index] = pack_matrix(matrices[index], backward)
        return carry

    lax.fori_loop(0, 2 * chips, prepare, 0, unroll=4)

    def back_copy(other):
        return pltpu.make_async_remote_copy(
            src_ref=outbox.at[other],
            dst_ref=returned.at[chip],
            send_sem=back_send.at[other],
            recv_sem=back_recv.at[chip],
            device_id={"layer": other * 2 + core},
            device_id_type=MESH,
        )

    def back_arrival(other):
        return pltpu.make_async_remote_copy(
            src_ref=outbox.at[other],
            dst_ref=returned.at[other],
            send_sem=back_send.at[other],
            recv_sem=back_recv.at[other],
            device_id={"layer": other * 2 + core},
            device_id_type=MESH,
        )

    rows = seed[own_rows(chip)]
    group = 4
    for first in range(0, chips, group):
        steps = range(first, min(first + group, chips))
        order = [chips - 1 - step if backward else step for step in steps]
        for at in order:

            @pl.when(chip != at)
            def _():
                in_arrival(at).wait_recv()

        for step, at in zip(steps, order):
            outbox[at] = rows
            if step < chips - 1:
                rows = times(rows, packs[2 * at + lead], backward)
                rows = times(rows, packs[2 * at + 1 - lead], backward) + inbox[at]
        for at in order:

            @pl.when(chip != at)
            def _():
                back_copy(at).start()

    def hand_copy(other):
        return pltpu.make_async_remote_copy(
            src_ref=handed.at[other],
            dst_ref=partner_out.at[other],
            send_sem=out_send.at[other],
            recv_sem=out_recv.at[other],
            device_id={"layer": partner},
            device_id_type=MESH,
        )

    def finish(other, led):
        lead_terms = jnp.where(is_lead, terms[own_rows(other)], partner_terms[other])
        following = times(led, packs[lead_slab], backward) + lead_terms
        out[own_rows(other)] = jnp.where(is_lead, led, following)
        handed[other] = jnp.where(is_lead, following, led)
        hand_copy(other).start()

    finish(chip, outbox[chip])

    def finish_next(step, carry):
        other = turned(step)
        back_arrival(other).wait_recv()
        finish(other, returned[other])
        return carry

    lax.fori_loop(1, chips, finish_next, 0)

    def drain(step, carry):
        in_copy(turned(step)).wait_send()
        back_copy(turned(step)).wait_send()
        return carry

    lax.fori_loop(1, chips, drain, 0)

    def collect(step, carry):
        other = turned(step)
        pair_copy(other).wait_send()
        hand_copy(other).wait()
        out[other_rows(other)] = partner_out[other]
        return carry

    lax.fori_loop(0, chips, collect, 0)

def chain_scratch(rows, slabs, channels):
    chips = slabs // 2
    window = -(-(rows // 16) // chips) * 8
    blocks = pltpu.VMEM((chips, window, channels), F32)
    packs = pltpu.VMEM((slabs, 2 * channels, 2 * channels), BF16)
    return window, [blocks] * 7 + [packs] + [pltpu.SemaphoreType.DMA((chips,))] * 8


def greet_chain(chips):
    me = lax.axis_index("layer")
    barrier = pltpu.get_barrier_semaphore()
    pl.semaphore_signal(barrier, inc=1, device_id={"layer": me + 1 - 2 * (me % 2)}, device_id_type=MESH)

    def greet(step, carry):
        other = lax.rem(me // 2 + step, chips) * 2 + me % 2
        pl.semaphore_signal(barrier, inc=1, device_id={"layer": other}, device_id_type=MESH)
        return carry

    lax.fori_loop(1, chips, greet, 0)


def middle_kernel(
    chips, window, begins, kernels, damping, damp_after, matrix,
    offsets_hbm, after_hbm, cot_hbm, matrices_hbm,
    slab_hbm, coarse_hbm, back_hbm, gates_hbm, kept_hbm, tops,
    offsets, after, cotangent, matrices, slab_end, coarse_end, back_offset, gates, kept,
    gates_after, state, pack_a, pack_b, weights_a, weights_b, back_a, back_b, load_sems, store_sems, *chain,
):
    slabs = 2 * chips
    layers = kernels.shape[0]
    greet_chain(chips)
    sources = (offsets_hbm, after_hbm, cot_hbm, matrices_hbm)
    loads = [
        pltpu.make_async_copy(source, target, load_sems.at[place])
        for place, (source, target) in enumerate(zip(sources, (offsets, after, cotangent, matrices)))
    ]
    for load in loads:
        load.start()
    stores = []

    def keep(source, target):
        stores.append(pltpu.make_async_copy(source, target, store_sems.at[len(stores)]))
        stores[-1].start()

    packs = (pack_a, pack_b)
    weights = (weights_a, weights_b)
    for packed in packs:
        clear_edges(packed)
    weights_back = (back_a, back_b)
    packed_matrix = pack_matrix(matrix[...], False)
    packed_transposed = pack_matrix(matrix[...], True)
    pack_field(pack_a, begins)
    for layer in range(layers):
        advance_layer(layer, layers, begins, slab_end, packs, weights, kernels, damping, gates, kept)
        keep(gates.at[layer], gates_hbm.at[layer])
        keep(kept.at[layer], kept_hbm.at[layer])
    keep(slab_end, slab_hbm)
    loads[0].wait()

    def put(at, value):
        coarse_end[at] = value + offsets[at]

    rows_times(begins, packed_matrix, False, put)
    keep(coarse_end, coarse_hbm)
    loads[1].wait()
    pack_field(pack_a, coarse_end)
    run_forward(coarse_end, state, packs, weights, after, damp_after, gates_after)
    loads[2].wait()
    run_backward(cotangent, state, packs, weights_back, after, damp_after, gates_after)
    choose_rows(lax.axis_index("layer") == slabs - 1, cotangent, state)
    run_backward(state, back_offset, packs, weights_back, kernels, damping, gates)

    def put_back(at, value):
        back_offset[at] = back_offset[at] - value

    rows_times(state, packed_transposed, True, put_back)
    keep(back_offset, back_hbm)
    loads[3].wait()
    pl.semaphore_wait(pltpu.get_barrier_semaphore(), chips)
    chain_steps(chips, True, window, cotangent, back_offset, matrices, tops, chain)
    for store in stores:
        store.wait()


def run_middle(begins, kernels, damping, damp_after, matrix, offsets, after, cotangent, matrices, packed, weights):
    layers, depth, channels = kernels.shape
    slabs = matrices.shape[0]
    pairs = packed[0].shape[2] - 1
    window, chain = chain_scratch(begins.shape[0], slabs, channels)
    field = jax.ShapeDtypeStruct(begins.shape, F32)
    gates = jax.ShapeDtypeStruct((layers,) + begins.shape, F32)
    kept = jax.ShapeDtypeStruct((layers, 2, pairs, 2 * pairs, channels), BF16)
    anywhere = pl.BlockSpec(memory_space=pl.ANY)
    dma = pltpu.SemaphoreType.DMA
    flat = pltpu.VMEM(begins.shape, F32)
    return pl.pallas_call(
        functools.partial(middle_kernel, slabs // 2, window),
        out_shape=(field, field, field, gates, kept, field),
        in_specs=in_vmem(5) + [anywhere] * 4,
        out_specs=(anywhere,) * 5 + tuple(in_vmem(1)),
        scratch_shapes=[
            flat,
            pltpu.VMEM(kernels.shape, F32),
            flat,
            pltpu.VMEM(matrices.shape, F32),
            flat,
            flat,
            flat,
            pltpu.VMEM(gates.shape, F32),
            pltpu.VMEM(kept.shape, BF16),
            pltpu.VMEM(gates.shape, F32),
            flat,
        ]
        + packed
        + weights
        + [dma((4,)), dma((2 * layers + 3,))]
        + chain,
        compiler_params=pltpu.CompilerParams(
            vmem_limit_bytes=VMEM_BYTES, collective_id=2, has_side_effects=True
        ),
        name="middle",
    )(begins, kernels, damping, damp_after, matrix, offsets, after, cotangent, matrices)


def forward_kernel(
    chips, ring, window, images, kernels, damping,
    begins, offsets_hbm, after_hbm, damp_after, matrices_hbm, own_matrix,
    offsets, after, matrices,
    wide, damp_wide, before, damp_before, quarter, start, pack_a, pack_b, weights_a, weights_b, store_sems,
    full_send, full_recv, part_send, part_recv, direct_send, direct_recv, relay_send, relay_recv,
    next_send, next_recv, damp_send, damp_recv, far_send, far_recv, pair_send, pair_recv,
    after_send, after_recv, back_send, back_recv, *chain,
):
    layers, depth, channels = kernels.shape
    share = depth // ring
    slabs = 2 * chips
    me = lax.axis_index("layer")
    line = lax.axis_index("dp")
    chip = me // 2
    core = me % 2
    partner = me + 1 - 2 * core
    across = (core == 1) & (me < slabs - 1)
    from_across = (core == 0) & (me > 0)

    def turned(step):
        return lax.rem(chip + step, chips)

    barrier = pltpu.get_barrier_semaphore()
    greet_chain(chips)
    for step in range(1, ring):
        pl.semaphore_signal(barrier, inc=1, device_id={"dp": lax.rem(line + step, ring)}, device_id_type=MESH)

    @pl.when(across)
    def _():
        pl.semaphore_signal(barrier, inc=1, device_id={"layer": me + 1}, device_id_type=MESH)

    @pl.when(from_across)
    def _():
        pl.semaphore_signal(barrier, inc=1, device_id={"layer": me - 1}, device_id_type=MESH)

    wide[...] = kernels[...].astype(F32)
    damp_wide[...] = jnp.zeros_like(damp_wide)
    damp_wide[pl.ds(0, layers)] = damping[...]
    packs = (pack_a, pack_b)
    weights = (weights_a, weights_b)
    for packed in packs:
        clear_edges(packed)
    pl.semaphore_wait(barrier, chips + ring - 1 + across.astype(jnp.int32) + from_across.astype(jnp.int32))

    own_share = pl.ds(pl.multiple_of(line * share, 8), share)

    def to(source, target, send, recv, device):
        return pltpu.make_async_remote_copy(
            src_ref=source, dst_ref=target, send_sem=send, recv_sem=recv, device_id=device, device_id_type=MESH
        )

    after_slab = {"layer": lax.rem(me + 1, slabs)}
    before_slab = {"layer": lax.rem(me + slabs - 1, slabs)}

    def full_copy(layer):
        return to(wide.at[layer], before.at[layer], full_send.at[layer], full_recv.at[layer], after_slab)

    def part_copy(layer):
        return to(
            wide.at[layer, own_share], before.at[layer, own_share], part_send.at[layer], part_recv.at[layer], after_slab
        )

    far_line = lax.rem(line + 2, ring)

    def direct_copy(layer):
        rows = pl.ds(pl.multiple_of(far_line * share + share // 2, 8), share // 2)
        return to(
            wide.at[layer, rows], before.at[layer, rows],
            direct_send.at[layer], direct_recv.at[layer], after_slab,
        )

    def damp_copy(way, target, device):
        return to(damp_wide, target, damp_send.at[way], damp_recv.at[way], device)

    def next_copy():
        return to(wide.at[:, own_share], quarter, next_send, next_recv, before_slab)

    def back_copy():
        return to(wide, after, back_send, back_recv, before_slab)

    damp_up = damp_copy(0, damp_before, after_slab)
    damp_down = damp_copy(1, damp_after, before_slab)

    @pl.when(core == 0)
    def _():
        damp_up.start()
        for layer in range(layers):
            full_copy(layer).start()

    @pl.when(across)
    def _():
        damp_up.start()
        for layer in range(layers):
            part_copy(layer).start()
            direct_copy(layer).start()

    @pl.when(me > 0)
    def _():
        damp_down.start()

    @pl.when(from_across)
    def _():
        next_copy().start()

    @pl.when(core == 1)
    def _():
        back_copy().start()

    pack_field(pack_a, images)

    taps = wide[0].reshape(depth // channels, channels, channels)
    tap_sum = taps[0]
    for tap in range(1, depth // channels):
        tap_sum = tap_sum + taps[tap]
    scale = layers * STEP
    line_at = lax.broadcasted_iota(jnp.int32, (channels, channels), 0)
    col_at = lax.broadcasted_iota(jnp.int32, (channels, channels), 1)
    decay = jnp.broadcast_to((1.0 - scale * damping[0, :]).reshape(1, channels), (channels, channels))
    matrix = jnp.where(line_at == col_at, decay, 0.0) + scale * tap_sum
    own_matrix[...] = matrix
    matrices[me] = matrix

    def far_copy(other):
        return to(
            own_matrix, matrices.at[me], far_send.at[other], far_recv.at[chip], {"layer": other * 2 + core}
        )

    def far_arrival(other):
        return to(
            own_matrix, matrices.at[other * 2 + core], far_send.at[other], far_recv.at[other],
            {"layer": other * 2 + core},
        )

    def pair_copy(other):
        slab = other * 2 + core
        return to(matrices.at[slab], matrices.at[slab], pair_send.at[other], pair_recv.at[other], {"layer": partner})

    def pair_arrival(other):
        slab = other * 2 + 1 - core
        return to(matrices.at[slab], matrices.at[slab], pair_send.at[other], pair_recv.at[other], {"layer": partner})

    def send_far(step, carry):
        far_copy(turned(step)).start()
        return carry

    def relay_copy(layer, step):
        rows = pl.ds(pl.multiple_of(line * share, 8), share // 2 if step == 2 else share)
        return to(
            before.at[layer, rows], before.at[layer, rows],
            relay_send.at[layer * ring + step], relay_recv.at[layer * ring + step],
            {"dp": lax.rem(line + step, ring)},
        )

    def relay_arrival(layer, step):
        size = share // 2 if step == 2 else share
        rows = pl.ds(pl.multiple_of(lax.rem(line + ring - step, ring) * share, 8), size)
        return to(
            before.at[layer, rows], before.at[layer, rows],
            relay_send.at[layer * ring + step], relay_recv.at[layer * ring + step],
            {"dp": lax.rem(line + step, ring)},
        )

    @pl.when(from_across)
    def _():
        for layer in range(layers):
            part_copy(layer).wait_recv()
            for step in range(1, ring):
                relay_copy(layer, step).start()

    pair_copy(chip).start()

    @pl.when(me == 0)
    def _():
        before[...] = jnp.zeros_like(before)
        damp_before[...] = jnp.zeros_like(damp_before)

    @pl.when(me > 0)
    def _():
        damp_up.wait_recv()

    for layer in range(layers):

        @pl.when(from_across)
        def _():
            direct_copy(layer).wait_recv()
            for step in range(1, ring):
                relay_arrival(layer, step).wait_recv()

        @pl.when(core == 1)
        def _():
            full_copy(layer).wait_recv()

        advance_layer(layer, layers, images, start, packs, weights, before, damp_before)

    lax.fori_loop(1, chips, send_far, 0)
    choose_rows(me == 0, images, start)

    def after_rows(step):
        return pl.ds(pl.multiple_of(lax.rem(line + ring - step, ring) * share, 8), share)

    def after_copy(step):
        return to(
            quarter, after.at[:, own_share], after_send.at[step - 1], after_recv.at[step - 1],
            {"dp": lax.rem(line + step, ring)},
        )

    def after_arrival(step):
        return to(
            quarter, after.at[:, after_rows(step)], after_send.at[step - 1], after_recv.at[step - 1],
            {"dp": lax.rem(line + step, ring)},
        )

    @pl.when(across)
    def _():
        next_copy().wait_recv()
        for step in range(1, ring):
            after_copy(step).start()
        after[:, own_share] = quarter[...]

    pack_field(pack_a, start)
    run_forward(start, offsets, packs, weights, kernels, damping)
    packed_matrix = pack_matrix(matrix, False)

    def put(at, value):
        offsets[at] = offsets[at] - value

    rows_times(start, packed_matrix, False, put)
    stores = [pltpu.make_async_copy(offsets, offsets_hbm, store_sems.at[0])]
    stores[0].start()

    def pass_on(step, carry):
        other = turned(step)
        far_arrival(other).wait_recv()
        pair_copy(other).start()
        return carry

    def pair_ready():
        pair_arrival(chip).wait_recv()

    def all_ready():
        lax.fori_loop(1, chips, pass_on, 0)

        def arrived(step, carry):
            pair_arrival(turned(step)).wait_recv()
            return carry

        lax.fori_loop(1, chips, arrived, 0)
        stores.append(pltpu.make_async_copy(matrices, matrices_hbm, store_sems.at[1]))
        stores[1].start()

        @pl.when(me == slabs - 1)
        def _():
            after[...] = jnp.zeros_like(after)

        @pl.when(core == 0)
        def _():
            back_copy().wait_recv()

        @pl.when(across)
        def _():
            for step in range(1, ring):
                after_arrival(step).wait_recv()

        stores.append(pltpu.make_async_copy(after, after_hbm, store_sems.at[2]))
        stores[2].start()

    chain_steps(chips, False, window, images, offsets, matrices, begins, chain, pair_ready, all_ready)

    @pl.when(from_across)
    def _():
        for layer in range(layers):
            for step in range(1, ring):
                relay_copy(layer, step).wait_send()

    @pl.when(me > 0)
    def _():
        damp_down.wait_send()

    @pl.when(from_across)
    def _():
        next_copy().wait_send()

    @pl.when(core == 1)
    def _():
        back_copy().wait_send()

    @pl.when(me < slabs - 1)
    def _():
        damp_up.wait_send()
        damp_down.wait_recv()

    @pl.when(me == slabs - 1)
    def _():
        damp_after[...] = jnp.zeros_like(damp_after)

    @pl.when(core == 0)
    def _():
        for layer in range(layers):
            full_copy(layer).wait_send()

    @pl.when(across)
    def _():
        for layer in range(layers):
            part_copy(layer).wait_send()
            direct_copy(layer).wait_send()

    def settle(step, carry):
        far_copy(turned(step)).wait_send()
        return carry

    lax.fori_loop(1, chips, settle, 0)

    def settle_pair(step, carry):
        pair_copy(turned(step)).wait_send()
        return carry

    lax.fori_loop(0, chips, settle_pair, 0)

    @pl.when(across)
    def _():
        for step in range(1, ring):
            after_copy(step).wait_send()

    for store in stores:
        store.wait()


def run_forward_kernel(images, kernels, damping, slabs, ring, packed, weights):
    chips = slabs // 2
    layers, depth, channels = kernels.shape
    dma = pltpu.SemaphoreType.DMA
    window, chain = chain_scratch(images.shape[0], slabs, channels)
    field = jax.ShapeDtypeStruct(images.shape, F32)
    outs = (
        field,
        field,
        jax.ShapeDtypeStruct(kernels.shape, F32),
        jax.ShapeDtypeStruct((8, channels), F32),
        jax.ShapeDtypeStruct((slabs, channels, channels), F32),
        jax.ShapeDtypeStruct((channels, channels), F32),
    )
    anywhere = pl.BlockSpec(memory_space=pl.ANY)
    (vmem,) = in_vmem(1)
    return pl.pallas_call(
        functools.partial(forward_kernel, chips, ring, window),
        out_shape=outs,
        in_specs=in_vmem(3),
        out_specs=(vmem, anywhere, anywhere, vmem, anywhere, vmem),
        scratch_shapes=[
            pltpu.VMEM(images.shape, F32),
            pltpu.VMEM(kernels.shape, F32),
            pltpu.VMEM((slabs, channels, channels), F32),
            pltpu.VMEM(kernels.shape, F32),
            pltpu.VMEM((8, channels), F32),
            pltpu.VMEM(kernels.shape, F32),
            pltpu.VMEM((8, channels), F32),
            pltpu.VMEM((layers, depth // ring, channels), F32),
            pltpu.VMEM(images.shape, F32),
        ]
        + packed
        + weights
        + [dma((3,))]
        + [dma((layers,))] * 6
        + [dma((layers * ring,))] * 2
        + [dma, dma, dma((2,)), dma((2,))]
        + [dma((chips,))] * 4
        + [dma((ring - 1,))] * 2
        + [dma] * 2
        + chain,
        compiler_params=pltpu.CompilerParams(
            vmem_limit_bytes=VMEM_BYTES, collective_id=1, has_side_effects=True
        ),
        name="forward",
    )(images, kernels, damping)


def place_kernel(*refs):
    half = len(refs) // 2
    for source, target in zip(refs[:half], refs[half:]):
        target[...] = source[...]


def place(*arrays):
    parts = 2

    def specs():
        return [pl.BlockSpec((a.shape[0] // parts, a.shape[1]), lambda i: (i, 0)) for a in arrays]

    return pl.pallas_call(
        place_kernel,
        grid=(parts,),
        out_shape=[jax.ShapeDtypeStruct(a.shape, a.dtype) for a in arrays],
        in_specs=specs(),
        out_specs=specs(),
        compiler_params=pltpu.CompilerParams(vmem_limit_bytes=VMEM_BYTES),
        name="place",
    )(*arrays)


def run_final(tops, kernels, damping, matrix, back_offsets, gates, kept, ring, packed, weights):
    layers, depth, channels = kernels.shape
    moves = layers * 2 * (ring - 1)
    dma = pltpu.SemaphoreType.DMA
    state = jax.ShapeDtypeStruct(tops.shape, F32)
    anywhere = pl.BlockSpec(memory_space=pl.ANY)
    return pl.pallas_call(
        functools.partial(final_kernel, ring),
        out_shape=(state, state, jax.ShapeDtypeStruct(kernels.shape, F32)),
        in_specs=in_vmem(4) + [anywhere] * 3,
        out_specs=(anywhere,) * 3,
        scratch_shapes=packed
        + weights
        + [
            pltpu.VMEM(tops.shape, F32),
            pltpu.VMEM(gates.shape, F32),
            pltpu.VMEM(kept.shape, BF16),
            pltpu.VMEM(tops.shape, F32),
            pltpu.VMEM(tops.shape, F32),
            pltpu.VMEM(kernels.shape, F32),
            pltpu.VMEM(kernels.shape, F32),
            pltpu.VMEM((moves, depth // (2 * ring), channels), F32),
        ]
        + [dma((moves,))] * 4
        + [dma((2 * layers + 1,)), dma((layers + 2,))],
        compiler_params=pltpu.CompilerParams(
            vmem_limit_bytes=VMEM_BYTES, collective_id=4, has_side_effects=True
        ),
        name="final",
    )(tops, kernels, damping, matrix, back_offsets, gates, kept)


def per_device(images, kernels, damping, cotangent):
    slab, depth, channels = kernels.shape
    side = images.shape[1]
    slabs = lax.axis_size("layer")
    ring = lax.axis_size("dp")
    pairs = side // 2
    flat = (side * side, channels)
    images_flat, cot_flat = images.reshape(flat), cotangent.reshape(flat)
    packed = [pltpu.VMEM((3, 2, pairs + 1, side, channels), BF16)] * 2
    weights = [pltpu.VMEM((12 * channels, 2 * channels), BF16)] * 2
    weights_back = [pltpu.VMEM((2 * channels, 12 * channels), BF16)] * 2

    begins, offsets, after, damp_after, matrices, matrix = run_forward_kernel(
        images_flat, kernels, damping, slabs, ring, packed, weights
    )
    slab_end, coarse_end, back_offsets, gates, kept, tops = run_middle(
        begins, kernels, damping, damp_after, matrix, offsets, after, cot_flat, matrices, packed, weights + weights_back
    )
    adjoint_start, adjoint_coarse, grads = run_final(
        tops, kernels, damping, matrix, back_offsets, gates, kept, ring, packed, weights_back
    )
    slab_end, coarse_end, adjoint_start, adjoint_coarse, grads = place(
        slab_end, coarse_end, adjoint_start, adjoint_coarse, grads.reshape(slab * depth, channels)
    )
    full = (1,) + images.shape
    return (
        slab_end.reshape(full),
        coarse_end.reshape(full),
        adjoint_start.reshape(full),
        adjoint_coarse.reshape(full),
        grads.reshape(kernels.shape),
    )


def solution(mesh):
    in_specs = (
        P("dp", None, None, None),
        P("layer", None, None),
        P("layer", None),
        P("dp", None, None, None),
    )
    out_specs = (
        P("layer", "dp", None, None, None),
        P("layer", "dp", None, None, None),
        P("layer", "dp", None, None, None),
        P("layer", "dp", None, None, None),
        P("layer", None, None),
    )
    return jax.shard_map(
        per_device, mesh=mesh, in_specs=in_specs, out_specs=out_specs, check_vma=False
    )
```

```python
import functools

import jax
import jax.numpy as jnp
from jax import lax
from jax.experimental import pallas as pl
from jax.experimental.pallas import tpu as pltpu
from jax.sharding import PartitionSpec as P

STEP = 0.125
F32 = jnp.float32
BF16 = jnp.bfloat16
MESH = pl.DeviceIdType.MESH
VMEM_BYTES = 60 * 1024 * 1024
LINE = 4
GROUP = 7


def split(value):
    high = value.astype(BF16)
    return high, (value - high.astype(F32)).astype(BF16)


def pack_matrix(matrix, transposed):
    high, low = split(matrix)
    if transposed:
        top = jnp.concatenate([high, high], axis=1)
        bottom = jnp.concatenate([low, jnp.zeros_like(low)], axis=1)
    else:
        top = jnp.concatenate([high, low], axis=1)
        bottom = jnp.concatenate([high, jnp.zeros_like(low)], axis=1)
    return jnp.concatenate([top, bottom], axis=0)


def times(rows, packed, transposed):
    channels = rows.shape[1]
    both = jnp.concatenate(split(rows), axis=1)
    dims = (((1,), (1 if transposed else 0,)), ((), ()))
    result = lax.dot_general(both, packed, dims, preferred_element_type=F32)
    return result[:, :channels] + result[:, channels:]


def clear_edges(packed):
    zeros = jnp.zeros(packed.shape[3:], packed.dtype)
    for col in range(3):
        packed[col, 0, 0] = zeros
        packed[col, 1, packed.shape[2] - 1] = zeros


def pack_rows(packed, first, even, odd):
    count, side, channels = even.shape
    column = lax.broadcasted_iota(jnp.int32, even.shape, 1)
    for parity, value in ((1, even), (0, odd)):
        start = first if parity == 1 else first + 1
        left = jnp.where(column == 0, 0.0, pltpu.roll(value, 1, 1))
        right = jnp.where(column == side - 1, 0.0, pltpu.roll(value, side - 1, 1))
        for col, moved in enumerate((left, value, right)):
            packed[col, parity, pl.ds(start, count)] = moved.astype(BF16)


def pieces(packed, first, count):
    channels = packed.shape[-1]
    rows = count * packed.shape[3]
    out = []
    for col in range(3):
        for parity, ahead in ((1, 0), (0, 1), (0, 0), (1, 1)):
            out.append(packed[col, parity, pl.ds(first + ahead, count)].reshape(rows, channels))
    return out


OFFSETS = (0, 1, -1, 2)


def fill_weights(weights, kernel, backward):
    channels = weights.shape[1] // 2 if not backward else weights.shape[0] // 2
    zero = jnp.zeros((channels, channels), BF16)
    for col in range(3):
        for place, offset in enumerate(OFFSETS):
            at = pl.ds((col * 4 + place) * channels, channels)
            for row in range(2):
                tap = offset - row + 1
                if 0 <= tap <= 2:
                    index = tap * 3 + col
                    block = kernel(8 - index if backward else index).astype(BF16)
                else:
                    block = zero
                out = pl.ds(row * channels, channels)
                if backward:
                    weights[out, at] = block
                else:
                    weights[at, out] = block


def convolve(packed, weights, first, count, side, backward):
    left = jnp.concatenate(pieces(packed, first, count), axis=1)
    dims = (((1,), (1 if backward else 0,)), ((), ()))
    result = lax.dot_general(left, weights[...], dims, preferred_element_type=F32)
    channels = result.shape[1] // 2
    result = result.reshape(count, side, 2 * channels)
    return result[:, :, :channels], result[:, :, channels:]


def each_group(pairs, body):
    def step(index, carry):
        body(index * GROUP)
        return carry

    lax.fori_loop(0, pairs // GROUP, step, 0, unroll=True)


def rows_at(first, side):
    return pl.ds(pl.multiple_of(first * 2 * side, 8), GROUP * 2 * side)


def pair_rows(value, side):
    value = value.reshape(GROUP, 2, side, value.shape[-1])
    return value[:, 0], value[:, 1]


def flat_rows(even, odd):
    return jnp.stack([even, odd], axis=1).reshape(-1, even.shape[-1])


def pack_field(packed, field):
    pairs = packed.shape[2] - 1

    def body(first):
        even, odd = pair_rows(field[rows_at(first, 2 * pairs)], 2 * pairs)
        pack_rows(packed, first, even, odd)

    each_group(pairs, body)


def tap_of(ref, layer, channels):
    return lambda tap: ref[layer, pl.ds(tap * channels, channels), :]


def advance_layer(layer, layers, source, target, packs, weights, kernels, damping, gates=None, kept=None):
    channels = source.shape[-1]
    pairs = packs[0].shape[2] - 1
    side = 2 * pairs
    now, later = packs[layer % 2], packs[(layer + 1) % 2]
    weights = weights[layer % 2]
    fill_weights(weights, tap_of(kernels, layer, channels), False)
    decay = damping[layer, :].reshape(1, 1, channels)
    state = source if layer == 0 else target

    def body(first):
        at = rows_at(first, side)
        outs = convolve(now, weights, first, GROUP, side, False)
        nexts, slopes = [], []
        for out, current in zip(outs, pair_rows(state[at], side)):
            act = jnp.tanh(out)
            slopes.append(STEP * (1.0 - act * act))
            nexts.append(current + STEP * (act - decay * current))
        target[at] = flat_rows(*nexts)
        if gates is not None:
            gates[layer, at] = flat_rows(*slopes)
        if kept is not None:
            kept[layer, 0, pl.ds(first, GROUP)] = now[1, 1, pl.ds(first, GROUP)]
            kept[layer, 1, pl.ds(first, GROUP)] = now[1, 0, pl.ds(first + 1, GROUP)]
        if layer + 1 < layers:
            pack_rows(later, first, *nexts)

    each_group(pairs, body)


def run_forward(source, target, packs, weights, kernels, damping, gates=None, kept=None):
    layers = kernels.shape[0]
    for layer in range(layers):
        advance_layer(layer, layers, source, target, packs, weights, kernels, damping, gates, kept)


def pack_scaled(packed, gates, layer, adjoint):
    pairs = packed.shape[2] - 1

    def body(first):
        at = rows_at(first, 2 * pairs)
        pack_rows(packed, first, *pair_rows(gates[layer, at] * adjoint[at], 2 * pairs))

    each_group(pairs, body)


def retreat_layer(turn, layers, source, target, packs, weights, kernels, damping, gates):
    channels = source.shape[-1]
    pairs = packs[0].shape[2] - 1
    side = 2 * pairs
    layer = layers - 1 - turn
    now, later = packs[turn % 2], packs[(turn + 1) % 2]
    weights = weights[turn % 2]
    fill_weights(weights, tap_of(kernels, layer, channels), True)
    decay = damping[layer, :].reshape(1, 1, channels)
    state = source if turn == 0 else target

    def body(first):
        at = rows_at(first, side)
        outs = convolve(now, weights, first, GROUP, side, True)
        nexts = []
        for out, current in zip(outs, pair_rows(state[at], side)):
            nexts.append(current - STEP * decay * current + out)
        target[at] = flat_rows(*nexts)
        if layer > 0:
            scaled = [gate * moved for gate, moved in zip(pair_rows(gates[layer - 1, at], side), nexts)]
            pack_rows(later, first, *scaled)

    each_group(pairs, body)


def run_backward(source, target, packs, weights, kernels, damping, gates):
    layers = gates.shape[0]
    pack_scaled(packs[0], gates, layers - 1, source)
    for turn in range(layers):
        retreat_layer(turn, layers, source, target, packs, weights, kernels, damping, gates)


def gradient(packed, kept, layer, grads):
    channels = packed.shape[-1]
    pairs = packed.shape[2] - 1
    pixels = pairs * packed.shape[3]
    left = jnp.concatenate([kept[layer, row].reshape(pixels, channels) for row in range(2)], axis=1)
    for col in range(3):
        parts = []
        for parity, ahead in ((1, 0), (0, 1), (0, 0), (1, 1)):
            parts.append(packed[col, parity, pl.ds(ahead, pairs)].reshape(pixels, channels))
        out = lax.dot_general(
            left, jnp.concatenate(parts, axis=1), (((0,), (0,)), ((), ())), preferred_element_type=F32
        )

        def block(row, offset):
            place = OFFSETS.index(offset)
            return out[row * channels : (row + 1) * channels, place * channels : (place + 1) * channels]

        for tap in range(3):
            total = block(0, 1 - tap) + block(1, 2 - tap)
            index = tap * 3 + (2 - col)
            grads[layer, pl.ds(index * channels, channels), :] = total


def rows_times(source, packed_matrix, transposed, put):
    parts = 7
    size = source.shape[0] // parts

    def body(index, carry):
        at = pl.ds(pl.multiple_of(index * size, 8), size)
        put(at, times(source[at], packed_matrix, transposed))
        return carry

    lax.fori_loop(0, parts, body, 0, unroll=True)


def choose_rows(flag, chosen, target):
    @pl.when(flag)
    def _():
        target[...] = chosen[...]


def final_kernel(
    ring, tops, kernels, damping, matrix, back_hbm, gates_hbm, kept_hbm,
    start_hbm, coarse_hbm, grads_hbm,
    pack_a, pack_b, weights_a, weights_b, back_offset, gates, kept, start, coarse_start, local, total, landed,
    reduce_send, reduce_recv, gather_send, gather_recv, load_sems, store_sems,
):
    layers = kernels.shape[0]
    me = lax.axis_index("dp")
    neighbours = (lax.rem(me + 1, ring), lax.rem(me + ring - 1, ring))
    barrier = pltpu.get_barrier_semaphore()
    for neighbour in neighbours:
        pl.semaphore_signal(barrier, inc=1, device_id={"dp": neighbour}, device_id_type=MESH)

    loads = []
    for layer in reversed(range(layers)):
        loads.append(pltpu.make_async_copy(gates_hbm.at[layer], gates.at[layer], load_sems.at[2 * layer]))
        loads.append(pltpu.make_async_copy(kept_hbm.at[layer], kept.at[layer], load_sems.at[2 * layer + 1]))
    loads.append(pltpu.make_async_copy(back_hbm, back_offset, load_sems.at[2 * layers]))
    for load in loads:
        load.start()
    streams = 2
    size = kernels.shape[1] // (streams * ring)

    def rows_of(way, step):
        chunk = lax.rem(me + (2 * ring - step if way % 2 == 0 else step + ring), ring)
        return pl.ds(pl.multiple_of((way * ring + chunk) * size, 8), size)

    def reduce_copy(layer, way, step):
        slot = (layer * streams + way) * (ring - 1) + step
        return pltpu.make_async_remote_copy(
            src_ref=local.at[layer, rows_of(way, step)],
            dst_ref=landed.at[slot],
            send_sem=reduce_send.at[slot],
            recv_sem=reduce_recv.at[slot],
            device_id={"dp": neighbours[way % 2]},
            device_id_type=MESH,
        )

    def gather_copy(layer, way, step):
        slot = (layer * streams + way) * (ring - 1) + step
        rows = rows_of(way, step - 1)
        return pltpu.make_async_remote_copy(
            src_ref=total.at[layer, rows],
            dst_ref=total.at[layer, rows],
            send_sem=gather_send.at[slot],
            recv_sem=gather_recv.at[slot],
            device_id={"dp": neighbours[way % 2]},
            device_id_type=MESH,
        )

    def advance_ring(layer, stage):
        last = ring - 1
        for way in range(streams):
            if 1 <= stage <= last:
                slot = (layer * streams + way) * last + stage - 1
                reduce_copy(layer, way, stage - 1).wait_recv()
                rows = rows_of(way, stage)
                value = local[layer, rows] + landed[slot]
                if stage < last:
                    local[layer, rows] = value
                else:
                    total[layer, rows] = value
            elif stage > last:
                gather_copy(layer, way, stage - last - 1).wait_recv()
            if stage < last:
                reduce_copy(layer, way, stage).start()
            elif stage < 2 * last:
                gather_copy(layer, way, stage - last).start()

    packs = (pack_a, pack_b)
    weights = (weights_a, weights_b)
    for packed in packs:
        clear_edges(packed)
    packed_transposed = pack_matrix(matrix[...], True)

    def put(at, value):
        coarse_start[at] = value + back_offset[at]

    stages = 2 * (ring - 1) + 1
    reached = [0] * layers
    stores = []

    def forward_rings(order):
        for layer in order:
            if layer < layers and reached[layer] < stages:
                advance_ring(layer, reached[layer])
                reached[layer] += 1
                if reached[layer] == stages:
                    store = pltpu.make_async_copy(total.at[layer], grads_hbm.at[layer], store_sems.at[layer])
                    store.start()
                    stores.append(store)

    loads[0].wait()
    pack_scaled(pack_a, gates, layers - 1, tops)
    for turn in range(layers):
        layer = layers - 1 - turn
        loads[2 * turn + 1].wait()
        gradient(packs[turn % 2], kept, layer, local)
        if turn == 0:
            pl.semaphore_wait(barrier, 2)
        forward_rings(range(layer, layers))
        if layer > 0:
            loads[2 * turn + 2].wait()
        retreat_layer(turn, layers, tops, start, packs, weights, kernels, damping, gates)
    stores.append(pltpu.make_async_copy(start, start_hbm, store_sems.at[layers]))
    stores[-1].start()
    forward_rings((0, 1))
    loads[2 * layers].wait()
    rows_times(tops, packed_transposed, True, put)
    stores.append(pltpu.make_async_copy(coarse_start, coarse_hbm, store_sems.at[layers + 1]))
    stores[-1].start()
    forward_rings((0, 2, 1, 0, 2, 0, 1, 0, 2, 1, 0, 2, 1))
    while min(reached) < stages:
        forward_rings(range(layers))
    for layer in range(layers):
        for way in range(streams):
            for step in range(ring - 1):
                reduce_copy(layer, way, step).wait_send()
                gather_copy(layer, way, step).wait_send()
    for store in stores:
        store.wait()


def in_vmem(count, scalars=0):
    return [pl.BlockSpec(memory_space=pltpu.SMEM)] * scalars + [
        pl.BlockSpec(memory_space=pltpu.VMEM)
    ] * count


def nothing():
    pass


def chain_steps(
    chips, backward, window, seed, terms, matrices, out, scratch, pair_ready=nothing, all_ready=nothing
):
    (
        partner_terms, composed, inbox, outbox, returned, handed, partner_out, packs,
        pair_send, pair_recv, in_send, in_recv, back_send, back_recv, out_send, out_recv,
    ) = scratch
    me = lax.axis_index("layer")
    chip = me // 2
    core = me % 2
    partner = me + 1 - 2 * core
    half = terms.shape[0] // 2
    lead = 1 if backward else 0
    is_lead = core == lead
    tiles = half // 8

    def start_of(other):
        return pl.multiple_of((other * tiles) // chips * 8, 8)

    def own_rows(other):
        return pl.ds(pl.multiple_of(core * half + start_of(other), 8), window)

    def other_rows(other):
        return pl.ds(pl.multiple_of((1 - core) * half + start_of(other), 8), window)

    def turned(step):
        return lax.rem(chip + step, chips)

    def pair_copy(other):
        return pltpu.make_async_remote_copy(
            src_ref=terms.at[other_rows(other)],
            dst_ref=partner_terms.at[other],
            send_sem=pair_send.at[other],
            recv_sem=pair_recv.at[other],
            device_id={"layer": partner},
            device_id_type=MESH,
        )

    def send_pair(step, carry):
        pair_copy(turned(step)).start()
        return carry

    lax.fori_loop(1, chips + 1, send_pair, 0)

    lead_slab = 2 * chip + lead
    next_slab = 2 * chip + 1 - lead
    pair_ready()
    packs[next_slab] = pack_matrix(matrices[next_slab], backward)

    def in_copy(other):
        return pltpu.make_async_remote_copy(
            src_ref=composed.at[other],
            dst_ref=inbox.at[chip],
            send_sem=in_send.at[other],
            recv_sem=in_recv.at[chip],
            device_id={"layer": other * 2 + core},
            device_id_type=MESH,
        )

    def in_arrival(other):
        return pltpu.make_async_remote_copy(
            src_ref=composed.at[other],
            dst_ref=inbox.at[other],
            send_sem=in_send.at[other],
            recv_sem=in_recv.at[other],
            device_id={"layer": other * 2 + core},
            device_id_type=MESH,
        )

    def compose(other):
        pair_copy(other).wait_recv()
        own, theirs = terms[own_rows(other)], partner_terms[other]
        led = jnp.where(is_lead, own, theirs)
        following = jnp.where(is_lead, theirs, own)
        return times(led, packs[next_slab], backward) + following

    def compose_send(step, carry):
        other = turned(step)
        composed[other] = compose(other)
        in_copy(other).start()
        return carry

    lax.fori_loop(1, chips, compose_send, 0)
    inbox[chip] = compose(chip)

    all_ready()

    def prepare(index, carry):
        packs[index] = pack_matrix(matrices[index], backward)
        return carry

    lax.fori_loop(0, 2 * chips, prepare, 0, unroll=4)

    def back_copy(other):
        return pltpu.make_async_remote_copy(
            src_ref=outbox.at[other],
            dst_ref=returned.at[chip],
            send_sem=back_send.at[other],
            recv_sem=back_recv.at[chip],
            device_id={"layer": other * 2 + core},
            device_id_type=MESH,
        )

    def back_arrival(other):
        return pltpu.make_async_remote_copy(
            src_ref=outbox.at[other],
            dst_ref=returned.at[other],
            send_sem=back_send.at[other],
            recv_sem=back_recv.at[other],
            device_id={"layer": other * 2 + core},
            device_id_type=MESH,
        )

    rows = seed[own_rows(chip)]
    group = 4
    for first in range(0, chips, group):
        steps = range(first, min(first + group, chips))
        order = [chips - 1 - step if backward else step for step in steps]
        for at in order:

            @pl.when(chip != at)
            def _():
                in_arrival(at).wait_recv()

        for step, at in zip(steps, order):
            outbox[at] = rows
            if step < chips - 1:
                rows = times(rows, packs[2 * at + lead], backward)
                rows = times(rows, packs[2 * at + 1 - lead], backward) + inbox[at]
        for at in order:

            @pl.when(chip != at)
            def _():
                back_copy(at).start()

    def hand_copy(other):
        return pltpu.make_async_remote_copy(
            src_ref=handed.at[other],
            dst_ref=partner_out.at[other],
            send_sem=out_send.at[other],
            recv_sem=out_recv.at[other],
            device_id={"layer": partner},
            device_id_type=MESH,
        )

    def finish(other, led):
        lead_terms = jnp.where(is_lead, terms[own_rows(other)], partner_terms[other])
        following = times(led, packs[lead_slab], backward) + lead_terms
        out[own_rows(other)] = jnp.where(is_lead, led, following)
        handed[other] = jnp.where(is_lead, following, led)
        hand_copy(other).start()

    finish(chip, outbox[chip])

    def finish_next(step, carry):
        other = turned(step)
        back_arrival(other).wait_recv()
        finish(other, returned[other])
        return carry

    lax.fori_loop(1, chips, finish_next, 0)

    def drain(step, carry):
        in_copy(turned(step)).wait_send()
        back_copy(turned(step)).wait_send()
        return carry

    lax.fori_loop(1, chips, drain, 0)

    def collect(step, carry):
        other = turned(step)
        pair_copy(other).wait_send()
        hand_copy(other).wait()
        out[other_rows(other)] = partner_out[other]
        return carry

    lax.fori_loop(0, chips, collect, 0)

def chain_scratch(rows, slabs, channels):
    chips = slabs // 2
    window = -(-(rows // 16) // chips) * 8
    blocks = pltpu.VMEM((chips, window, channels), F32)
    packs = pltpu.VMEM((slabs, 2 * channels, 2 * channels), BF16)
    return window, [blocks] * 7 + [packs] + [pltpu.SemaphoreType.DMA((chips,))] * 8


def greet_chain(chips):
    me = lax.axis_index("layer")
    barrier = pltpu.get_barrier_semaphore()
    pl.semaphore_signal(barrier, inc=1, device_id={"layer": me + 1 - 2 * (me % 2)}, device_id_type=MESH)

    def greet(step, carry):
        other = lax.rem(me // 2 + step, chips) * 2 + me % 2
        pl.semaphore_signal(barrier, inc=1, device_id={"layer": other}, device_id_type=MESH)
        return carry

    lax.fori_loop(1, chips, greet, 0)


def middle_kernel(
    chips, window, begins, kernels, damping, damp_after, matrix,
    offsets_hbm, after_hbm, cot_hbm, matrices_hbm,
    slab_hbm, coarse_hbm, back_hbm, gates_hbm, kept_hbm, tops,
    offsets, after, cotangent, matrices, slab_end, coarse_end, back_offset, gates, kept,
    gates_after, state, pack_a, pack_b, weights_a, weights_b, back_a, back_b, load_sems, store_sems, *chain,
):
    slabs = 2 * chips
    layers = kernels.shape[0]
    greet_chain(chips)
    sources = (offsets_hbm, after_hbm, cot_hbm, matrices_hbm)
    loads = [
        pltpu.make_async_copy(source, target, load_sems.at[place])
        for place, (source, target) in enumerate(zip(sources, (offsets, after, cotangent, matrices)))
    ]
    for load in loads:
        load.start()
    stores = []

    def keep(source, target):
        stores.append(pltpu.make_async_copy(source, target, store_sems.at[len(stores)]))
        stores[-1].start()

    packs = (pack_a, pack_b)
    weights = (weights_a, weights_b)
    for packed in packs:
        clear_edges(packed)
    weights_back = (back_a, back_b)
    packed_matrix = pack_matrix(matrix[...], False)
    packed_transposed = pack_matrix(matrix[...], True)
    pack_field(pack_a, begins)
    for layer in range(layers):
        advance_layer(layer, layers, begins, slab_end, packs, weights, kernels, damping, gates, kept)
        keep(gates.at[layer], gates_hbm.at[layer])
        keep(kept.at[layer], kept_hbm.at[layer])
    keep(slab_end, slab_hbm)
    loads[0].wait()

    def put(at, value):
        coarse_end[at] = value + offsets[at]

    rows_times(begins, packed_matrix, False, put)
    keep(coarse_end, coarse_hbm)
    loads[1].wait()
    pack_field(pack_a, coarse_end)
    run_forward(coarse_end, state, packs, weights, after, damp_after, gates_after)
    loads[2].wait()
    run_backward(cotangent, state, packs, weights_back, after, damp_after, gates_after)
    choose_rows(lax.axis_index("layer") == slabs - 1, cotangent, state)
    run_backward(state, back_offset, packs, weights_back, kernels, damping, gates)

    def put_back(at, value):
        back_offset[at] = back_offset[at] - value

    rows_times(state, packed_transposed, True, put_back)
    keep(back_offset, back_hbm)
    loads[3].wait()
    pl.semaphore_wait(pltpu.get_barrier_semaphore(), chips)
    chain_steps(chips, True, window, cotangent, back_offset, matrices, tops, chain)
    for store in stores:
        store.wait()


def run_middle(begins, kernels, damping, damp_after, matrix, offsets, after, cotangent, matrices, packed, weights):
    layers, depth, channels = kernels.shape
    slabs = matrices.shape[0]
    pairs = packed[0].shape[2] - 1
    window, chain = chain_scratch(begins.shape[0], slabs, channels)
    field = jax.ShapeDtypeStruct(begins.shape, F32)
    gates = jax.ShapeDtypeStruct((layers,) + begins.shape, F32)
    kept = jax.ShapeDtypeStruct((layers, 2, pairs, 2 * pairs, channels), BF16)
    anywhere = pl.BlockSpec(memory_space=pl.ANY)
    dma = pltpu.SemaphoreType.DMA
    flat = pltpu.VMEM(begins.shape, F32)
    return pl.pallas_call(
        functools.partial(middle_kernel, slabs // 2, window),
        out_shape=(field, field, field, gates, kept, field),
        in_specs=in_vmem(5) + [anywhere] * 4,
        out_specs=(anywhere,) * 5 + tuple(in_vmem(1)),
        scratch_shapes=[
            flat,
            pltpu.VMEM(kernels.shape, F32),
            flat,
            pltpu.VMEM(matrices.shape, F32),
            flat,
            flat,
            flat,
            pltpu.VMEM(gates.shape, F32),
            pltpu.VMEM(kept.shape, BF16),
            pltpu.VMEM(gates.shape, F32),
            flat,
        ]
        + packed
        + weights
        + [dma((4,)), dma((2 * layers + 3,))]
        + chain,
        compiler_params=pltpu.CompilerParams(
            vmem_limit_bytes=VMEM_BYTES, collective_id=2, has_side_effects=True
        ),
        name="middle",
    )(begins, kernels, damping, damp_after, matrix, offsets, after, cotangent, matrices)


def forward_kernel(
    chips, ring, window, images, kernels, damping,
    begins, offsets_hbm, after_hbm, damp_after, matrices_hbm, own_matrix,
    offsets, after, matrices,
    wide, damp_wide, before, damp_before, quarter, start, pack_a, pack_b, weights_a, weights_b, store_sems,
    full_send, full_recv, part_send, part_recv, direct_send, direct_recv, relay_send, relay_recv,
    next_send, next_recv, damp_send, damp_recv, far_send, far_recv, pair_send, pair_recv, spread_send,
    after_send, after_recv, back_send, back_recv, *chain,
):
    layers, depth, channels = kernels.shape
    share = depth // ring
    slabs = 2 * chips
    me = lax.axis_index("layer")
    line = lax.axis_index("dp")
    chip = me // 2
    core = me % 2
    partner = me + 1 - 2 * core
    across = (core == 1) & (me < slabs - 1)
    from_across = (core == 0) & (me > 0)

    def turned(step):
        return lax.rem(chip + step, chips)

    barrier = pltpu.get_barrier_semaphore()
    greet_chain(chips)
    for step in range(1, ring):
        pl.semaphore_signal(barrier, inc=1, device_id={"dp": lax.rem(line + step, ring)}, device_id_type=MESH)

    @pl.when(across)
    def _():
        pl.semaphore_signal(barrier, inc=1, device_id={"layer": me + 1}, device_id_type=MESH)

    @pl.when(from_across)
    def _():
        pl.semaphore_signal(barrier, inc=1, device_id={"layer": me - 1}, device_id_type=MESH)

    wide[...] = kernels[...].astype(F32)
    damp_wide[...] = jnp.zeros_like(damp_wide)
    damp_wide[pl.ds(0, layers)] = damping[...]
    packs = (pack_a, pack_b)
    weights = (weights_a, weights_b)
    for packed in packs:
        clear_edges(packed)
    pl.semaphore_wait(barrier, chips + ring - 1 + across.astype(jnp.int32) + from_across.astype(jnp.int32))

    own_share = pl.ds(pl.multiple_of(line * share, 8), share)

    def to(source, target, send, recv, device):
        return pltpu.make_async_remote_copy(
            src_ref=source, dst_ref=target, send_sem=send, recv_sem=recv, device_id=device, device_id_type=MESH
        )

    after_slab = {"layer": lax.rem(me + 1, slabs)}
    before_slab = {"layer": lax.rem(me + slabs - 1, slabs)}

    def full_copy(layer):
        return to(wide.at[layer], before.at[layer], full_send.at[layer], full_recv.at[layer], after_slab)

    def part_copy(layer):
        return to(
            wide.at[layer, own_share], before.at[layer, own_share], part_send.at[layer], part_recv.at[layer], after_slab
        )

    far_line = lax.rem(line + 2, ring)

    def direct_copy(layer):
        rows = pl.ds(pl.multiple_of(far_line * share + share // 2, 8), share // 2)
        return to(
            wide.at[layer, rows], before.at[layer, rows],
            direct_send.at[layer], direct_recv.at[layer], after_slab,
        )

    def damp_copy(way, target, device):
        return to(damp_wide, target, damp_send.at[way], damp_recv.at[way], device)

    def next_copy():
        return to(wide.at[:, own_share], quarter, next_send, next_recv, before_slab)

    def back_copy():
        return to(wide, after, back_send, back_recv, before_slab)

    damp_up = damp_copy(0, damp_before, after_slab)
    damp_down = damp_copy(1, damp_after, before_slab)

    @pl.when(core == 0)
    def _():
        damp_up.start()
        for layer in range(layers):
            full_copy(layer).start()

    @pl.when(across)
    def _():
        damp_up.start()
        for layer in range(layers):
            part_copy(layer).start()
            direct_copy(layer).start()

    @pl.when(me > 0)
    def _():
        damp_down.start()

    @pl.when(from_across)
    def _():
        next_copy().start()

    @pl.when(core == 1)
    def _():
        back_copy().start()

    pack_field(pack_a, images)

    taps = wide[0].reshape(depth // channels, channels, channels)
    tap_sum = taps[0]
    for tap in range(1, depth // channels):
        tap_sum = tap_sum + taps[tap]
    scale = layers * STEP
    line_at = lax.broadcasted_iota(jnp.int32, (channels, channels), 0)
    col_at = lax.broadcasted_iota(jnp.int32, (channels, channels), 1)
    decay = jnp.broadcast_to((1.0 - scale * damping[0, :]).reshape(1, channels), (channels, channels))
    matrix = jnp.where(line_at == col_at, decay, 0.0) + scale * tap_sum
    own_matrix[...] = matrix
    matrices[me] = matrix

    def far_copy(other):
        return to(
            own_matrix, matrices.at[me], far_send.at[other], far_recv.at[chip], {"layer": other * 2 + core}
        )

    def far_arrival(other):
        return to(
            own_matrix, matrices.at[other * 2 + core], far_send.at[other], far_recv.at[other],
            {"layer": other * 2 + core},
        )

    def pair_copy(other):
        slab = other * 2 + core
        return to(matrices.at[slab], matrices.at[slab], pair_send.at[other], pair_recv.at[other], {"layer": partner})

    def pair_arrival(other):
        slab = other * 2 + 1 - core
        return to(matrices.at[slab], matrices.at[slab], pair_send.at[other], pair_recv.at[other], {"layer": partner})

    line_at, column_at = chip // LINE, chip % LINE
    lines = chips // LINE

    def row_chip(step):
        return line_at * LINE + lax.rem(column_at + step, LINE)

    def spread_copy(step, jump):
        slab = row_chip(step) * 2 + core
        target = lax.rem(line_at + jump, lines) * LINE + column_at
        return to(
            matrices.at[slab], matrices.at[slab],
            spread_send.at[step * (lines - 1) + jump - 1], far_recv.at[row_chip(step)],
            {"layer": target * 2 + core},
        )

    for step in range(1, LINE):
        far_copy(row_chip(step)).start()
    def relay_copy(layer, step):
        rows = pl.ds(pl.multiple_of(line * share, 8), share // 2 if step == 2 else share)
        return to(
            before.at[layer, rows], before.at[layer, rows],
            relay_send.at[layer * ring + step], relay_recv.at[layer * ring + step],
            {"dp": lax.rem(line + step, ring)},
        )

    def relay_arrival(layer, step):
        size = share // 2 if step == 2 else share
        rows = pl.ds(pl.multiple_of(lax.rem(line + ring - step, ring) * share, 8), size)
        return to(
            before.at[layer, rows], before.at[layer, rows],
            relay_send.at[layer * ring + step], relay_recv.at[layer * ring + step],
            {"dp": lax.rem(line + step, ring)},
        )

    def relay_layer(layer):
        @pl.when(from_across)
        def _():
            part_copy(layer).wait_recv()
            for step in range(1, ring):
                relay_copy(layer, step).start()

    relay_layer(0)
    for step in range(LINE):
        if step > 0:
            far_arrival(row_chip(step)).wait_recv()
        pair_copy(row_chip(step)).start()
        for jump in range(1, lines):
            spread_copy(step, jump).start()
    for layer in range(1, layers):
        relay_layer(layer)


    @pl.when(me == 0)
    def _():
        before[...] = jnp.zeros_like(before)
        damp_before[...] = jnp.zeros_like(damp_before)

    @pl.when(me > 0)
    def _():
        damp_up.wait_recv()

    for layer in range(layers):

        @pl.when(from_across)
        def _():
            direct_copy(layer).wait_recv()
            for step in range(1, ring):
                relay_arrival(layer, step).wait_recv()

        @pl.when(core == 1)
        def _():
            full_copy(layer).wait_recv()

        advance_layer(layer, layers, images, start, packs, weights, before, damp_before)

    choose_rows(me == 0, images, start)

    def after_rows(step):
        return pl.ds(pl.multiple_of(lax.rem(line + ring - step, ring) * share, 8), share)

    def after_copy(step):
        return to(
            quarter, after.at[:, own_share], after_send.at[step - 1], after_recv.at[step - 1],
            {"dp": lax.rem(line + step, ring)},
        )

    def after_arrival(step):
        return to(
            quarter, after.at[:, after_rows(step)], after_send.at[step - 1], after_recv.at[step - 1],
            {"dp": lax.rem(line + step, ring)},
        )

    @pl.when(across)
    def _():
        next_copy().wait_recv()
        for step in range(1, ring):
            after_copy(step).start()
        after[:, own_share] = quarter[...]

    pack_field(pack_a, start)
    run_forward(start, offsets, packs, weights, kernels, damping)
    packed_matrix = pack_matrix(matrix, False)

    def put(at, value):
        offsets[at] = offsets[at] - value

    rows_times(start, packed_matrix, False, put)
    stores = [pltpu.make_async_copy(offsets, offsets_hbm, store_sems.at[0])]
    stores[0].start()

    def pass_on(step, carry):
        other = lax.rem(line_at + step // LINE, lines) * LINE + lax.rem(column_at + step % LINE, LINE)
        far_arrival(other).wait_recv()
        pair_copy(other).start()
        return carry

    def pair_ready():
        pair_arrival(chip).wait_recv()

    def all_ready():
        lax.fori_loop(LINE, chips, pass_on, 0)

        def arrived(step, carry):
            pair_arrival(turned(step)).wait_recv()
            return carry

        lax.fori_loop(1, chips, arrived, 0)
        stores.append(pltpu.make_async_copy(matrices, matrices_hbm, store_sems.at[1]))
        stores[1].start()

        @pl.when(me == slabs - 1)
        def _():
            after[...] = jnp.zeros_like(after)

        @pl.when(core == 0)
        def _():
            back_copy().wait_recv()

        @pl.when(across)
        def _():
            for step in range(1, ring):
                after_arrival(step).wait_recv()

        stores.append(pltpu.make_async_copy(after, after_hbm, store_sems.at[2]))
        stores[2].start()

    chain_steps(chips, False, window, images, offsets, matrices, begins, chain, pair_ready, all_ready)

    @pl.when(from_across)
    def _():
        for layer in range(layers):
            for step in range(1, ring):
                relay_copy(layer, step).wait_send()

    @pl.when(me > 0)
    def _():
        damp_down.wait_send()

    @pl.when(from_across)
    def _():
        next_copy().wait_send()

    @pl.when(core == 1)
    def _():
        back_copy().wait_send()

    @pl.when(me < slabs - 1)
    def _():
        damp_up.wait_send()
        damp_down.wait_recv()

    @pl.when(me == slabs - 1)
    def _():
        damp_after[...] = jnp.zeros_like(damp_after)

    @pl.when(core == 0)
    def _():
        for layer in range(layers):
            full_copy(layer).wait_send()

    @pl.when(across)
    def _():
        for layer in range(layers):
            part_copy(layer).wait_send()
            direct_copy(layer).wait_send()

    for step in range(LINE):
        if step > 0:
            far_copy(row_chip(step)).wait_send()
        for jump in range(1, lines):
            spread_copy(step, jump).wait_send()

    def settle_pair(step, carry):
        pair_copy(turned(step)).wait_send()
        return carry

    lax.fori_loop(0, chips, settle_pair, 0)

    @pl.when(across)
    def _():
        for step in range(1, ring):
            after_copy(step).wait_send()

    for store in stores:
        store.wait()


def run_forward_kernel(images, kernels, damping, slabs, ring, packed, weights):
    chips = slabs // 2
    layers, depth, channels = kernels.shape
    dma = pltpu.SemaphoreType.DMA
    window, chain = chain_scratch(images.shape[0], slabs, channels)
    field = jax.ShapeDtypeStruct(images.shape, F32)
    outs = (
        field,
        field,
        jax.ShapeDtypeStruct(kernels.shape, F32),
        jax.ShapeDtypeStruct((8, channels), F32),
        jax.ShapeDtypeStruct((slabs, channels, channels), F32),
        jax.ShapeDtypeStruct((channels, channels), F32),
    )
    anywhere = pl.BlockSpec(memory_space=pl.ANY)
    (vmem,) = in_vmem(1)
    return pl.pallas_call(
        functools.partial(forward_kernel, chips, ring, window),
        out_shape=outs,
        in_specs=in_vmem(3),
        out_specs=(vmem, anywhere, anywhere, vmem, anywhere, vmem),
        scratch_shapes=[
            pltpu.VMEM(images.shape, F32),
            pltpu.VMEM(kernels.shape, F32),
            pltpu.VMEM((slabs, channels, channels), F32),
            pltpu.VMEM(kernels.shape, F32),
            pltpu.VMEM((8, channels), F32),
            pltpu.VMEM(kernels.shape, F32),
            pltpu.VMEM((8, channels), F32),
            pltpu.VMEM((layers, depth // ring, channels), F32),
            pltpu.VMEM(images.shape, F32),
        ]
        + packed
        + weights
        + [dma((3,))]
        + [dma((layers,))] * 6
        + [dma((layers * ring,))] * 2
        + [dma, dma, dma((2,)), dma((2,))]
        + [dma((chips,))] * 4
        + [dma((LINE * (chips // LINE - 1),))]
        + [dma((ring - 1,))] * 2
        + [dma] * 2
        + chain,
        compiler_params=pltpu.CompilerParams(
            vmem_limit_bytes=VMEM_BYTES, collective_id=1, has_side_effects=True
        ),
        name="forward",
    )(images, kernels, damping)


def place_kernel(*refs):
    half = len(refs) // 2
    for source, target in zip(refs[:half], refs[half:]):
        target[...] = source[...]


def place(*arrays):
    parts = 2

    def specs():
        return [pl.BlockSpec((a.shape[0] // parts, a.shape[1]), lambda i: (i, 0)) for a in arrays]

    return pl.pallas_call(
        place_kernel,
        grid=(parts,),
        out_shape=[jax.ShapeDtypeStruct(a.shape, a.dtype) for a in arrays],
        in_specs=specs(),
        out_specs=specs(),
        compiler_params=pltpu.CompilerParams(vmem_limit_bytes=VMEM_BYTES),
        name="place",
    )(*arrays)


def run_final(tops, kernels, damping, matrix, back_offsets, gates, kept, ring, packed, weights):
    layers, depth, channels = kernels.shape
    moves = layers * 2 * (ring - 1)
    dma = pltpu.SemaphoreType.DMA
    state = jax.ShapeDtypeStruct(tops.shape, F32)
    anywhere = pl.BlockSpec(memory_space=pl.ANY)
    return pl.pallas_call(
        functools.partial(final_kernel, ring),
        out_shape=(state, state, jax.ShapeDtypeStruct(kernels.shape, F32)),
        in_specs=in_vmem(4) + [anywhere] * 3,
        out_specs=(anywhere,) * 3,
        scratch_shapes=packed
        + weights
        + [
            pltpu.VMEM(tops.shape, F32),
            pltpu.VMEM(gates.shape, F32),
            pltpu.VMEM(kept.shape, BF16),
            pltpu.VMEM(tops.shape, F32),
            pltpu.VMEM(tops.shape, F32),
            pltpu.VMEM(kernels.shape, F32),
            pltpu.VMEM(kernels.shape, F32),
            pltpu.VMEM((moves, depth // (2 * ring), channels), F32),
        ]
        + [dma((moves,))] * 4
        + [dma((2 * layers + 1,)), dma((layers + 2,))],
        compiler_params=pltpu.CompilerParams(
            vmem_limit_bytes=VMEM_BYTES, collective_id=4, has_side_effects=True
        ),
        name="final",
    )(tops, kernels, damping, matrix, back_offsets, gates, kept)


def per_device(images, kernels, damping, cotangent):
    slab, depth, channels = kernels.shape
    side = images.shape[1]
    slabs = lax.axis_size("layer")
    ring = lax.axis_size("dp")
    pairs = side // 2
    flat = (side * side, channels)
    images_flat, cot_flat = images.reshape(flat), cotangent.reshape(flat)
    packed = [pltpu.VMEM((3, 2, pairs + 1, side, channels), BF16)] * 2
    weights = [pltpu.VMEM((12 * channels, 2 * channels), BF16)] * 2
    weights_back = [pltpu.VMEM((2 * channels, 12 * channels), BF16)] * 2

    begins, offsets, after, damp_after, matrices, matrix = run_forward_kernel(
        images_flat, kernels, damping, slabs, ring, packed, weights
    )
    slab_end, coarse_end, back_offsets, gates, kept, tops = run_middle(
        begins, kernels, damping, damp_after, matrix, offsets, after, cot_flat, matrices, packed, weights + weights_back
    )
    adjoint_start, adjoint_coarse, grads = run_final(
        tops, kernels, damping, matrix, back_offsets, gates, kept, ring, packed, weights_back
    )
    slab_end, coarse_end, adjoint_start, adjoint_coarse, grads = place(
        slab_end, coarse_end, adjoint_start, adjoint_coarse, grads.reshape(slab * depth, channels)
    )
    full = (1,) + images.shape
    return (
        slab_end.reshape(full),
        coarse_end.reshape(full),
        adjoint_start.reshape(full),
        adjoint_coarse.reshape(full),
        grads.reshape(kernels.shape),
    )


def solution(mesh):
    in_specs = (
        P("dp", None, None, None),
        P("layer", None, None),
        P("layer", None),
        P("dp", None, None, None),
    )
    out_specs = (
        P("layer", "dp", None, None, None),
        P("layer", "dp", None, None, None),
        P("layer", "dp", None, None, None),
        P("layer", "dp", None, None, None),
        P("layer", None, None),
    )
    return jax.shard_map(
        per_device, mesh=mesh, in_specs=in_specs, out_specs=out_specs, check_vma=False
    )
```

```python
import functools

import jax
import jax.numpy as jnp
from jax import lax
from jax.experimental import pallas as pl
from jax.experimental.pallas import tpu as pltpu
from jax.sharding import PartitionSpec as P

STEP = 0.125
F32 = jnp.float32
BF16 = jnp.bfloat16
MESH = pl.DeviceIdType.MESH
VMEM_BYTES = 60 * 1024 * 1024
GROUP = 7


def split(value):
    high = value.astype(BF16)
    return high, (value - high.astype(F32)).astype(BF16)


def pack_matrix(matrix, transposed):
    high, low = split(matrix)
    if transposed:
        top = jnp.concatenate([high, high], axis=1)
        bottom = jnp.concatenate([low, jnp.zeros_like(low)], axis=1)
    else:
        top = jnp.concatenate([high, low], axis=1)
        bottom = jnp.concatenate([high, jnp.zeros_like(low)], axis=1)
    return jnp.concatenate([top, bottom], axis=0)


def times(rows, packed, transposed):
    channels = rows.shape[1]
    both = jnp.concatenate(split(rows), axis=1)
    dims = (((1,), (1 if transposed else 0,)), ((), ()))
    result = lax.dot_general(both, packed, dims, preferred_element_type=F32)
    return result[:, :channels] + result[:, channels:]


def clear_edges(packed):
    zeros = jnp.zeros(packed.shape[3:], packed.dtype)
    for col in range(3):
        packed[col, 0, 0] = zeros
        packed[col, 1, packed.shape[2] - 1] = zeros


def pack_rows(packed, first, even, odd):
    count, side, channels = even.shape
    column = lax.broadcasted_iota(jnp.int32, even.shape, 1)
    for parity, value in ((1, even), (0, odd)):
        start = first if parity == 1 else first + 1
        left = jnp.where(column == 0, 0.0, pltpu.roll(value, 1, 1))
        right = jnp.where(column == side - 1, 0.0, pltpu.roll(value, side - 1, 1))
        for col, moved in enumerate((left, value, right)):
            packed[col, parity, pl.ds(start, count)] = moved.astype(BF16)


def pieces(packed, first, count):
    channels = packed.shape[-1]
    rows = count * packed.shape[3]
    out = []
    for col in range(3):
        for parity, ahead in ((1, 0), (0, 1), (0, 0), (1, 1)):
            out.append(packed[col, parity, pl.ds(first + ahead, count)].reshape(rows, channels))
    return out


OFFSETS = (0, 1, -1, 2)


def fill_weights(weights, kernel, backward):
    channels = weights.shape[1] // 2 if not backward else weights.shape[0] // 2
    zero = jnp.zeros((channels, channels), BF16)
    for col in range(3):
        for place, offset in enumerate(OFFSETS):
            at = pl.ds((col * 4 + place) * channels, channels)
            for row in range(2):
                tap = offset - row + 1
                if 0 <= tap <= 2:
                    index = tap * 3 + col
                    block = kernel(8 - index if backward else index).astype(BF16)
                else:
                    block = zero
                out = pl.ds(row * channels, channels)
                if backward:
                    weights[out, at] = block
                else:
                    weights[at, out] = block


def convolve(packed, weights, first, count, side, backward):
    left = jnp.concatenate(pieces(packed, first, count), axis=1)
    dims = (((1,), (1 if backward else 0,)), ((), ()))
    result = lax.dot_general(left, weights[...], dims, preferred_element_type=F32)
    channels = result.shape[1] // 2
    result = result.reshape(count, side, 2 * channels)
    return result[:, :, :channels], result[:, :, channels:]


def each_group(pairs, body):
    def step(index, carry):
        body(index * GROUP)
        return carry

    lax.fori_loop(0, pairs // GROUP, step, 0, unroll=True)


def rows_at(first, side):
    return pl.ds(pl.multiple_of(first * 2 * side, 8), GROUP * 2 * side)


def pair_rows(value, side):
    value = value.reshape(GROUP, 2, side, value.shape[-1])
    return value[:, 0], value[:, 1]


def flat_rows(even, odd):
    return jnp.stack([even, odd], axis=1).reshape(-1, even.shape[-1])


def pack_field(packed, field):
    pairs = packed.shape[2] - 1

    def body(first):
        even, odd = pair_rows(field[rows_at(first, 2 * pairs)], 2 * pairs)
        pack_rows(packed, first, even, odd)

    each_group(pairs, body)


def tap_of(ref, layer, channels):
    return lambda tap: ref[layer, pl.ds(tap * channels, channels), :]


def advance_layer(layer, layers, source, target, packs, weights, kernels, damping, gates=None, kept=None):
    channels = source.shape[-1]
    pairs = packs[0].shape[2] - 1
    side = 2 * pairs
    now, later = packs[layer % 2], packs[(layer + 1) % 2]
    fill_weights(weights, tap_of(kernels, layer, channels), False)
    decay = damping[layer, :].reshape(1, 1, channels)
    state = source if layer == 0 else target

    def body(first):
        at = rows_at(first, side)
        outs = convolve(now, weights, first, GROUP, side, False)
        nexts, slopes = [], []
        for out, current in zip(outs, pair_rows(state[at], side)):
            act = jnp.tanh(out)
            slopes.append(STEP * (1.0 - act * act))
            nexts.append(current + STEP * (act - decay * current))
        target[at] = flat_rows(*nexts)
        if gates is not None:
            gates[layer, at] = flat_rows(*slopes)
        if kept is not None:
            kept[layer, 0, pl.ds(first, GROUP)] = now[1, 1, pl.ds(first, GROUP)]
            kept[layer, 1, pl.ds(first, GROUP)] = now[1, 0, pl.ds(first + 1, GROUP)]
        if layer + 1 < layers:
            pack_rows(later, first, *nexts)

    each_group(pairs, body)


def run_forward(source, target, packs, weights, kernels, damping, gates=None, kept=None):
    layers = kernels.shape[0]
    for layer in range(layers):
        advance_layer(layer, layers, source, target, packs, weights, kernels, damping, gates, kept)


def pack_scaled(packed, gates, layer, adjoint):
    pairs = packed.shape[2] - 1

    def body(first):
        at = rows_at(first, 2 * pairs)
        pack_rows(packed, first, *pair_rows(gates[layer, at] * adjoint[at], 2 * pairs))

    each_group(pairs, body)


def retreat_layer(turn, layers, source, target, packs, weights, kernels, damping, gates):
    channels = source.shape[-1]
    pairs = packs[0].shape[2] - 1
    side = 2 * pairs
    layer = layers - 1 - turn
    now, later = packs[turn % 2], packs[(turn + 1) % 2]
    fill_weights(weights, tap_of(kernels, layer, channels), True)
    decay = damping[layer, :].reshape(1, 1, channels)
    state = source if turn == 0 else target

    def body(first):
        at = rows_at(first, side)
        outs = convolve(now, weights, first, GROUP, side, True)
        nexts = []
        for out, current in zip(outs, pair_rows(state[at], side)):
            nexts.append(current - STEP * decay * current + out)
        target[at] = flat_rows(*nexts)
        if layer > 0:
            scaled = [gate * moved for gate, moved in zip(pair_rows(gates[layer - 1, at], side), nexts)]
            pack_rows(later, first, *scaled)

    each_group(pairs, body)


def run_backward(source, target, packs, weights, kernels, damping, gates):
    layers = gates.shape[0]
    pack_scaled(packs[0], gates, layers - 1, source)
    for turn in range(layers):
        retreat_layer(turn, layers, source, target, packs, weights, kernels, damping, gates)


def gradient(packed, kept, layer, grads):
    channels = packed.shape[-1]
    pairs = packed.shape[2] - 1
    pixels = pairs * packed.shape[3]
    left = jnp.concatenate([kept[layer, row].reshape(pixels, channels) for row in range(2)], axis=1)
    for col in range(3):
        parts = []
        for parity, ahead in ((1, 0), (0, 1), (0, 0), (1, 1)):
            parts.append(packed[col, parity, pl.ds(ahead, pairs)].reshape(pixels, channels))
        out = lax.dot_general(
            left, jnp.concatenate(parts, axis=1), (((0,), (0,)), ((), ())), preferred_element_type=F32
        )

        def block(row, offset):
            place = OFFSETS.index(offset)
            return out[row * channels : (row + 1) * channels, place * channels : (place + 1) * channels]

        for tap in range(3):
            total = block(0, 1 - tap) + block(1, 2 - tap)
            index = tap * 3 + (2 - col)
            grads[layer, pl.ds(index * channels, channels), :] = total


def rows_times(source, packed_matrix, transposed, put):
    parts = 7
    size = source.shape[0] // parts

    def body(index, carry):
        at = pl.ds(pl.multiple_of(index * size, 8), size)
        put(at, times(source[at], packed_matrix, transposed))
        return carry

    lax.fori_loop(0, parts, body, 0, unroll=True)


def choose_rows(flag, chosen, target):
    @pl.when(flag)
    def _():
        target[...] = chosen[...]


def final_kernel(
    ring, tops, kernels, damping, matrix, back_hbm, gates_hbm, kept_hbm,
    start_hbm, coarse_hbm, grads_hbm,
    pack_a, pack_b, weights, back_offset, gates, kept, start, coarse_start, local, total, landed,
    reduce_send, reduce_recv, gather_send, gather_recv, load_sems, store_sems,
):
    layers = kernels.shape[0]
    me = lax.axis_index("dp")
    neighbours = (lax.rem(me + 1, ring), lax.rem(me + ring - 1, ring))
    barrier = pltpu.get_barrier_semaphore()
    for neighbour in neighbours:
        pl.semaphore_signal(barrier, inc=1, device_id={"dp": neighbour}, device_id_type=MESH)

    loads = []
    for layer in reversed(range(layers)):
        loads.append(pltpu.make_async_copy(gates_hbm.at[layer], gates.at[layer], load_sems.at[2 * layer]))
        loads.append(pltpu.make_async_copy(kept_hbm.at[layer], kept.at[layer], load_sems.at[2 * layer + 1]))
    loads.append(pltpu.make_async_copy(back_hbm, back_offset, load_sems.at[2 * layers]))
    for load in loads:
        load.start()
    streams = 2
    size = kernels.shape[1] // (streams * ring)

    def rows_of(way, step):
        chunk = lax.rem(me + (2 * ring - step if way % 2 == 0 else step + ring), ring)
        return pl.ds(pl.multiple_of((way * ring + chunk) * size, 8), size)

    def reduce_copy(layer, way, step):
        slot = (layer * streams + way) * (ring - 1) + step
        return pltpu.make_async_remote_copy(
            src_ref=local.at[layer, rows_of(way, step)],
            dst_ref=landed.at[slot],
            send_sem=reduce_send.at[slot],
            recv_sem=reduce_recv.at[slot],
            device_id={"dp": neighbours[way % 2]},
            device_id_type=MESH,
        )

    def gather_copy(layer, way, step):
        slot = (layer * streams + way) * (ring - 1) + step
        rows = rows_of(way, step - 1)
        return pltpu.make_async_remote_copy(
            src_ref=total.at[layer, rows],
            dst_ref=total.at[layer, rows],
            send_sem=gather_send.at[slot],
            recv_sem=gather_recv.at[slot],
            device_id={"dp": neighbours[way % 2]},
            device_id_type=MESH,
        )

    def advance_ring(layer, stage):
        last = ring - 1
        for way in range(streams):
            if 1 <= stage <= last:
                slot = (layer * streams + way) * last + stage - 1
                reduce_copy(layer, way, stage - 1).wait_recv()
                rows = rows_of(way, stage)
                value = local[layer, rows] + landed[slot]
                if stage < last:
                    local[layer, rows] = value
                else:
                    total[layer, rows] = value
            elif stage > last:
                gather_copy(layer, way, stage - last - 1).wait_recv()
            if stage < last:
                reduce_copy(layer, way, stage).start()
            elif stage < 2 * last:
                gather_copy(layer, way, stage - last).start()

    packs = (pack_a, pack_b)
    for packed in packs:
        clear_edges(packed)
    packed_transposed = pack_matrix(matrix[...], True)

    def put(at, value):
        coarse_start[at] = value + back_offset[at]

    stages = 2 * (ring - 1) + 1
    reached = [0] * layers
    stores = []

    def forward_rings(order):
        for layer in order:
            if layer < layers and reached[layer] < stages:
                advance_ring(layer, reached[layer])
                reached[layer] += 1
                if reached[layer] == stages:
                    store = pltpu.make_async_copy(total.at[layer], grads_hbm.at[layer], store_sems.at[layer])
                    store.start()
                    stores.append(store)

    loads[0].wait()
    pack_scaled(pack_a, gates, layers - 1, tops)
    for turn in range(layers):
        layer = layers - 1 - turn
        loads[2 * turn + 1].wait()
        gradient(packs[turn % 2], kept, layer, local)
        if turn == 0:
            pl.semaphore_wait(barrier, 2)
        forward_rings(range(layer, layers))
        if layer > 0:
            loads[2 * turn + 2].wait()
        retreat_layer(turn, layers, tops, start, packs, weights, kernels, damping, gates)
    stores.append(pltpu.make_async_copy(start, start_hbm, store_sems.at[layers]))
    stores[-1].start()
    forward_rings((0, 1))
    loads[2 * layers].wait()
    rows_times(tops, packed_transposed, True, put)
    stores.append(pltpu.make_async_copy(coarse_start, coarse_hbm, store_sems.at[layers + 1]))
    stores[-1].start()
    forward_rings((0, 2, 1, 0, 2, 0, 1, 0, 2, 1, 0, 2, 1))
    while min(reached) < stages:
        forward_rings(range(layers))
    for layer in range(layers):
        for way in range(streams):
            for step in range(ring - 1):
                reduce_copy(layer, way, step).wait_send()
                gather_copy(layer, way, step).wait_send()
    for store in stores:
        store.wait()


def in_vmem(count, scalars=0):
    return [pl.BlockSpec(memory_space=pltpu.SMEM)] * scalars + [
        pl.BlockSpec(memory_space=pltpu.VMEM)
    ] * count


def nothing():
    pass


def chain_steps(
    chips, backward, window, seed, terms, matrices, out, scratch, pair_ready=nothing, all_ready=nothing
):
    (
        partner_terms, composed, inbox, outbox, returned, handed, partner_out, packs,
        pair_send, pair_recv, in_send, in_recv, back_send, back_recv, out_send, out_recv,
    ) = scratch
    me = lax.axis_index("layer")
    chip = me // 2
    core = me % 2
    partner = me + 1 - 2 * core
    half = terms.shape[0] // 2
    lead = 1 if backward else 0
    is_lead = core == lead
    tiles = half // 8

    def start_of(other):
        return pl.multiple_of((other * tiles) // chips * 8, 8)

    def own_rows(other):
        return pl.ds(pl.multiple_of(core * half + start_of(other), 8), window)

    def other_rows(other):
        return pl.ds(pl.multiple_of((1 - core) * half + start_of(other), 8), window)

    def turned(step):
        return lax.rem(chip + step, chips)

    def pair_copy(other):
        return pltpu.make_async_remote_copy(
            src_ref=terms.at[other_rows(other)],
            dst_ref=partner_terms.at[other],
            send_sem=pair_send.at[other],
            recv_sem=pair_recv.at[other],
            device_id={"layer": partner},
            device_id_type=MESH,
        )

    def send_pair(step, carry):
        pair_copy(turned(step)).start()
        return carry

    lax.fori_loop(1, chips + 1, send_pair, 0)

    lead_slab = 2 * chip + lead
    next_slab = 2 * chip + 1 - lead
    pair_ready()
    packs[next_slab] = pack_matrix(matrices[next_slab], backward)

    def in_copy(other):
        return pltpu.make_async_remote_copy(
            src_ref=composed.at[other],
            dst_ref=inbox.at[chip],
            send_sem=in_send.at[other],
            recv_sem=in_recv.at[chip],
            device_id={"layer": other * 2 + core},
            device_id_type=MESH,
        )

    def in_arrival(other):
        return pltpu.make_async_remote_copy(
            src_ref=composed.at[other],
            dst_ref=inbox.at[other],
            send_sem=in_send.at[other],
            recv_sem=in_recv.at[other],
            device_id={"layer": other * 2 + core},
            device_id_type=MESH,
        )

    def compose(other):
        pair_copy(other).wait_recv()
        own, theirs = terms[own_rows(other)], partner_terms[other]
        led = jnp.where(is_lead, own, theirs)
        following = jnp.where(is_lead, theirs, own)
        return times(led, packs[next_slab], backward) + following

    def compose_send(step, carry):
        other = turned(step)
        composed[other] = compose(other)
        in_copy(other).start()
        return carry

    lax.fori_loop(1, chips, compose_send, 0)
    inbox[chip] = compose(chip)

    all_ready()

    def prepare(index, carry):
        packs[index] = pack_matrix(matrices[index], backward)
        return carry

    lax.fori_loop(0, 2 * chips, prepare, 0, unroll=4)

    def back_copy(other):
        return pltpu.make_async_remote_copy(
            src_ref=outbox.at[other],
            dst_ref=returned.at[chip],
            send_sem=back_send.at[other],
            recv_sem=back_recv.at[chip],
            device_id={"layer": other * 2 + core},
            device_id_type=MESH,
        )

    def back_arrival(other):
        return pltpu.make_async_remote_copy(
            src_ref=outbox.at[other],
            dst_ref=returned.at[other],
            send_sem=back_send.at[other],
            recv_sem=back_recv.at[other],
            device_id={"layer": other * 2 + core},
            device_id_type=MESH,
        )

    rows = seed[own_rows(chip)]
    group = 4
    for first in range(0, chips, group):
        steps = range(first, min(first + group, chips))
        order = [chips - 1 - step if backward else step for step in steps]
        for at in order:

            @pl.when(chip != at)
            def _():
                in_arrival(at).wait_recv()

        for step, at in zip(steps, order):
            outbox[at] = rows
            if step < chips - 1:
                rows = times(rows, packs[2 * at + lead], backward)
                rows = times(rows, packs[2 * at + 1 - lead], backward) + inbox[at]
        for at in order:

            @pl.when(chip != at)
            def _():
                back_copy(at).start()

    def hand_copy(other):
        return pltpu.make_async_remote_copy(
            src_ref=handed.at[other],
            dst_ref=partner_out.at[other],
            send_sem=out_send.at[other],
            recv_sem=out_recv.at[other],
            device_id={"layer": partner},
            device_id_type=MESH,
        )

    def finish(other, led):
        lead_terms = jnp.where(is_lead, terms[own_rows(other)], partner_terms[other])
        following = times(led, packs[lead_slab], backward) + lead_terms
        out[own_rows(other)] = jnp.where(is_lead, led, following)
        handed[other] = jnp.where(is_lead, following, led)
        hand_copy(other).start()

    finish(chip, outbox[chip])

    def finish_next(step, carry):
        other = turned(step)
        back_arrival(other).wait_recv()
        finish(other, returned[other])
        return carry

    lax.fori_loop(1, chips, finish_next, 0)

    def drain(step, carry):
        in_copy(turned(step)).wait_send()
        back_copy(turned(step)).wait_send()
        return carry

    lax.fori_loop(1, chips, drain, 0)

    def collect(step, carry):
        other = turned(step)
        pair_copy(other).wait_send()
        hand_copy(other).wait()
        out[other_rows(other)] = partner_out[other]
        return carry

    lax.fori_loop(0, chips, collect, 0)

def chain_scratch(rows, slabs, channels):
    chips = slabs // 2
    window = -(-(rows // 16) // chips) * 8
    blocks = pltpu.VMEM((chips, window, channels), F32)
    packs = pltpu.VMEM((slabs, 2 * channels, 2 * channels), BF16)
    return window, [blocks] * 7 + [packs] + [pltpu.SemaphoreType.DMA((chips,))] * 8


def greet_chain(chips):
    me = lax.axis_index("layer")
    barrier = pltpu.get_barrier_semaphore()
    pl.semaphore_signal(barrier, inc=1, device_id={"layer": me + 1 - 2 * (me % 2)}, device_id_type=MESH)

    def greet(step, carry):
        other = lax.rem(me // 2 + step, chips) * 2 + me % 2
        pl.semaphore_signal(barrier, inc=1, device_id={"layer": other}, device_id_type=MESH)
        return carry

    lax.fori_loop(1, chips, greet, 0)


def middle_kernel(
    chips, window, begins, kernels, damping, damp_after, matrix,
    offsets_hbm, after_hbm, cot_hbm, matrices_hbm,
    slab_hbm, coarse_hbm, back_hbm, gates_hbm, kept_hbm, tops,
    offsets, after, cotangent, matrices, slab_end, coarse_end, back_offset, gates, kept,
    gates_after, state, pack_a, pack_b, weights, weights_back, load_sems, store_sems, *chain,
):
    slabs = 2 * chips
    layers = kernels.shape[0]
    greet_chain(chips)
    sources = (offsets_hbm, after_hbm, cot_hbm, matrices_hbm)
    loads = [
        pltpu.make_async_copy(source, target, load_sems.at[place])
        for place, (source, target) in enumerate(zip(sources, (offsets, after, cotangent, matrices)))
    ]
    for load in loads:
        load.start()
    stores = []

    def keep(source, target):
        stores.append(pltpu.make_async_copy(source, target, store_sems.at[len(stores)]))
        stores[-1].start()

    packs = (pack_a, pack_b)
    for packed in packs:
        clear_edges(packed)
    packed_matrix = pack_matrix(matrix[...], False)
    packed_transposed = pack_matrix(matrix[...], True)
    pack_field(pack_a, begins)
    for layer in range(layers):
        advance_layer(layer, layers, begins, slab_end, packs, weights, kernels, damping, gates, kept)
        keep(gates.at[layer], gates_hbm.at[layer])
        keep(kept.at[layer], kept_hbm.at[layer])
    keep(slab_end, slab_hbm)
    loads[0].wait()

    def put(at, value):
        coarse_end[at] = value + offsets[at]

    rows_times(begins, packed_matrix, False, put)
    keep(coarse_end, coarse_hbm)
    loads[1].wait()
    pack_field(pack_a, coarse_end)
    run_forward(coarse_end, state, packs, weights, after, damp_after, gates_after)
    loads[2].wait()
    run_backward(cotangent, state, packs, weights_back, after, damp_after, gates_after)
    choose_rows(lax.axis_index("layer") == slabs - 1, cotangent, state)
    run_backward(state, back_offset, packs, weights_back, kernels, damping, gates)

    def put_back(at, value):
        back_offset[at] = back_offset[at] - value

    rows_times(state, packed_transposed, True, put_back)
    keep(back_offset, back_hbm)
    loads[3].wait()
    pl.semaphore_wait(pltpu.get_barrier_semaphore(), chips)
    chain_steps(chips, True, window, cotangent, back_offset, matrices, tops, chain)
    for store in stores:
        store.wait()


def run_middle(begins, kernels, damping, damp_after, matrix, offsets, after, cotangent, matrices, packed, weights):
    layers, depth, channels = kernels.shape
    slabs = matrices.shape[0]
    pairs = packed[0].shape[2] - 1
    window, chain = chain_scratch(begins.shape[0], slabs, channels)
    field = jax.ShapeDtypeStruct(begins.shape, F32)
    gates = jax.ShapeDtypeStruct((layers,) + begins.shape, F32)
    kept = jax.ShapeDtypeStruct((layers, 2, pairs, 2 * pairs, channels), BF16)
    anywhere = pl.BlockSpec(memory_space=pl.ANY)
    dma = pltpu.SemaphoreType.DMA
    flat = pltpu.VMEM(begins.shape, F32)
    return pl.pallas_call(
        functools.partial(middle_kernel, slabs // 2, window),
        out_shape=(field, field, field, gates, kept, field),
        in_specs=in_vmem(5) + [anywhere] * 4,
        out_specs=(anywhere,) * 5 + tuple(in_vmem(1)),
        scratch_shapes=[
            flat,
            pltpu.VMEM(kernels.shape, F32),
            flat,
            pltpu.VMEM(matrices.shape, F32),
            flat,
            flat,
            flat,
            pltpu.VMEM(gates.shape, F32),
            pltpu.VMEM(kept.shape, BF16),
            pltpu.VMEM(gates.shape, F32),
            flat,
        ]
        + packed
        + weights
        + [dma((4,)), dma((2 * layers + 3,))]
        + chain,
        compiler_params=pltpu.CompilerParams(
            vmem_limit_bytes=VMEM_BYTES, collective_id=2, has_side_effects=True
        ),
        name="middle",
    )(begins, kernels, damping, damp_after, matrix, offsets, after, cotangent, matrices)


def forward_kernel(
    chips, ring, window, images, kernels, damping,
    begins, offsets_hbm, after_hbm, damp_after, matrices_hbm, own_matrix,
    offsets, after, matrices,
    wide, damp_wide, before, damp_before, quarter, start, pack_a, pack_b, weights, store_sems,
    full_send, full_recv, part_send, part_recv, direct_send, direct_recv, relay_send, relay_recv,
    next_send, next_recv, damp_send, damp_recv, far_send, far_recv, pair_send, pair_recv,
    after_send, after_recv, back_send, back_recv, *chain,
):
    layers, depth, channels = kernels.shape
    share = depth // ring
    slabs = 2 * chips
    me = lax.axis_index("layer")
    line = lax.axis_index("dp")
    chip = me // 2
    core = me % 2
    partner = me + 1 - 2 * core
    across = (core == 1) & (me < slabs - 1)
    from_across = (core == 0) & (me > 0)

    def turned(step):
        return lax.rem(chip + step, chips)

    barrier = pltpu.get_barrier_semaphore()
    greet_chain(chips)
    for step in range(1, ring):
        pl.semaphore_signal(barrier, inc=1, device_id={"dp": lax.rem(line + step, ring)}, device_id_type=MESH)

    @pl.when(across)
    def _():
        pl.semaphore_signal(barrier, inc=1, device_id={"layer": me + 1}, device_id_type=MESH)

    @pl.when(from_across)
    def _():
        pl.semaphore_signal(barrier, inc=1, device_id={"layer": me - 1}, device_id_type=MESH)

    wide[...] = kernels[...].astype(F32)
    damp_wide[...] = jnp.zeros_like(damp_wide)
    damp_wide[pl.ds(0, layers)] = damping[...]
    packs = (pack_a, pack_b)
    for packed in packs:
        clear_edges(packed)
    pl.semaphore_wait(barrier, chips + ring - 1 + across.astype(jnp.int32) + from_across.astype(jnp.int32))

    own_share = pl.ds(pl.multiple_of(line * share, 8), share)

    def to(source, target, send, recv, device):
        return pltpu.make_async_remote_copy(
            src_ref=source, dst_ref=target, send_sem=send, recv_sem=recv, device_id=device, device_id_type=MESH
        )

    after_slab = {"layer": lax.rem(me + 1, slabs)}
    before_slab = {"layer": lax.rem(me + slabs - 1, slabs)}

    def full_copy(layer):
        return to(wide.at[layer], before.at[layer], full_send.at[layer], full_recv.at[layer], after_slab)

    def part_copy(layer):
        return to(
            wide.at[layer, own_share], before.at[layer, own_share], part_send.at[layer], part_recv.at[layer], after_slab
        )

    far_line = lax.rem(line + 2, ring)

    def direct_copy(layer):
        rows = pl.ds(pl.multiple_of(far_line * share + share // 2, 8), share // 2)
        return to(
            wide.at[layer, rows], before.at[layer, rows],
            direct_send.at[layer], direct_recv.at[layer], after_slab,
        )

    def damp_copy(way, target, device):
        return to(damp_wide, target, damp_send.at[way], damp_recv.at[way], device)

    def next_copy():
        return to(wide.at[:, own_share], quarter, next_send, next_recv, before_slab)

    def back_copy():
        return to(wide, after, back_send, back_recv, before_slab)

    damp_up = damp_copy(0, damp_before, after_slab)
    damp_down = damp_copy(1, damp_after, before_slab)

    @pl.when(core == 0)
    def _():
        damp_up.start()
        for layer in range(layers):
            full_copy(layer).start()

    @pl.when(across)
    def _():
        damp_up.start()
        for layer in range(layers):
            part_copy(layer).start()
            direct_copy(layer).start()

    @pl.when(me > 0)
    def _():
        damp_down.start()

    @pl.when(from_across)
    def _():
        next_copy().start()

    @pl.when(core == 1)
    def _():
        back_copy().start()

    pack_field(pack_a, images)

    taps = wide[0].reshape(depth // channels, channels, channels)
    tap_sum = taps[0]
    for tap in range(1, depth // channels):
        tap_sum = tap_sum + taps[tap]
    scale = layers * STEP
    line_at = lax.broadcasted_iota(jnp.int32, (channels, channels), 0)
    col_at = lax.broadcasted_iota(jnp.int32, (channels, channels), 1)
    decay = jnp.broadcast_to((1.0 - scale * damping[0, :]).reshape(1, channels), (channels, channels))
    matrix = jnp.where(line_at == col_at, decay, 0.0) + scale * tap_sum
    own_matrix[...] = matrix
    matrices[me] = matrix

    def far_copy(other):
        return to(
            own_matrix, matrices.at[me], far_send.at[other], far_recv.at[chip], {"layer": other * 2 + core}
        )

    def far_arrival(other):
        return to(
            own_matrix, matrices.at[other * 2 + core], far_send.at[other], far_recv.at[other],
            {"layer": other * 2 + core},
        )

    def pair_copy(other):
        slab = other * 2 + core
        return to(matrices.at[slab], matrices.at[slab], pair_send.at[other], pair_recv.at[other], {"layer": partner})

    def pair_arrival(other):
        slab = other * 2 + 1 - core
        return to(matrices.at[slab], matrices.at[slab], pair_send.at[other], pair_recv.at[other], {"layer": partner})

    def send_far(step, carry):
        far_copy(turned(step)).start()
        return carry

    def relay_copy(layer, step):
        rows = pl.ds(pl.multiple_of(line * share, 8), share // 2 if step == 2 else share)
        return to(
            before.at[layer, rows], before.at[layer, rows],
            relay_send.at[layer * ring + step], relay_recv.at[layer * ring + step],
            {"dp": lax.rem(line + step, ring)},
        )

    def relay_arrival(layer, step):
        size = share // 2 if step == 2 else share
        rows = pl.ds(pl.multiple_of(lax.rem(line + ring - step, ring) * share, 8), size)
        return to(
            before.at[layer, rows], before.at[layer, rows],
            relay_send.at[layer * ring + step], relay_recv.at[layer * ring + step],
            {"dp": lax.rem(line + step, ring)},
        )

    @pl.when(from_across)
    def _():
        for layer in range(layers):
            part_copy(layer).wait_recv()
            for step in range(1, ring):
                relay_copy(layer, step).start()

    pair_copy(chip).start()

    @pl.when(me == 0)
    def _():
        before[...] = jnp.zeros_like(before)
        damp_before[...] = jnp.zeros_like(damp_before)

    @pl.when(me > 0)
    def _():
        damp_up.wait_recv()

    for layer in range(layers):

        @pl.when(from_across)
        def _():
            direct_copy(layer).wait_recv()
            for step in range(1, ring):
                relay_arrival(layer, step).wait_recv()

        @pl.when(core == 1)
        def _():
            full_copy(layer).wait_recv()

        if layer == 1:
            lax.fori_loop(1, chips, send_far, 0)
        advance_layer(layer, layers, images, start, packs, weights, before, damp_before)

    choose_rows(me == 0, images, start)

    def after_rows(step):
        return pl.ds(pl.multiple_of(lax.rem(line + ring - step, ring) * share, 8), share)

    def after_copy(step):
        return to(
            quarter, after.at[:, own_share], after_send.at[step - 1], after_recv.at[step - 1],
            {"dp": lax.rem(line + step, ring)},
        )

    def after_arrival(step):
        return to(
            quarter, after.at[:, after_rows(step)], after_send.at[step - 1], after_recv.at[step - 1],
            {"dp": lax.rem(line + step, ring)},
        )

    @pl.when(across)
    def _():
        next_copy().wait_recv()
        for step in range(1, ring):
            after_copy(step).start()
        after[:, own_share] = quarter[...]

    pack_field(pack_a, start)
    run_forward(start, offsets, packs, weights, kernels, damping)
    packed_matrix = pack_matrix(matrix, False)

    def put(at, value):
        offsets[at] = offsets[at] - value

    rows_times(start, packed_matrix, False, put)
    stores = [pltpu.make_async_copy(offsets, offsets_hbm, store_sems.at[0])]
    stores[0].start()

    def pass_on(step, carry):
        other = turned(step)
        far_arrival(other).wait_recv()
        pair_copy(other).start()
        return carry

    def pair_ready():
        pair_arrival(chip).wait_recv()

    def all_ready():
        lax.fori_loop(1, chips, pass_on, 0)

        def arrived(step, carry):
            pair_arrival(turned(step)).wait_recv()
            return carry

        lax.fori_loop(1, chips, arrived, 0)
        stores.append(pltpu.make_async_copy(matrices, matrices_hbm, store_sems.at[1]))
        stores[1].start()

        @pl.when(me == slabs - 1)
        def _():
            after[...] = jnp.zeros_like(after)

        @pl.when(core == 0)
        def _():
            back_copy().wait_recv()

        @pl.when(across)
        def _():
            for step in range(1, ring):
                after_arrival(step).wait_recv()

        stores.append(pltpu.make_async_copy(after, after_hbm, store_sems.at[2]))
        stores[2].start()

    chain_steps(chips, False, window, images, offsets, matrices, begins, chain, pair_ready, all_ready)

    @pl.when(from_across)
    def _():
        for layer in range(layers):
            for step in range(1, ring):
                relay_copy(layer, step).wait_send()

    @pl.when(me > 0)
    def _():
        damp_down.wait_send()

    @pl.when(from_across)
    def _():
        next_copy().wait_send()

    @pl.when(core == 1)
    def _():
        back_copy().wait_send()

    @pl.when(me < slabs - 1)
    def _():
        damp_up.wait_send()
        damp_down.wait_recv()

    @pl.when(me == slabs - 1)
    def _():
        damp_after[...] = jnp.zeros_like(damp_after)

    @pl.when(core == 0)
    def _():
        for layer in range(layers):
            full_copy(layer).wait_send()

    @pl.when(across)
    def _():
        for layer in range(layers):
            part_copy(layer).wait_send()
            direct_copy(layer).wait_send()

    def settle(step, carry):
        far_copy(turned(step)).wait_send()
        return carry

    lax.fori_loop(1, chips, settle, 0)

    def settle_pair(step, carry):
        pair_copy(turned(step)).wait_send()
        return carry

    lax.fori_loop(0, chips, settle_pair, 0)

    @pl.when(across)
    def _():
        for step in range(1, ring):
            after_copy(step).wait_send()

    for store in stores:
        store.wait()


def run_forward_kernel(images, kernels, damping, slabs, ring, packed, weights):
    chips = slabs // 2
    layers, depth, channels = kernels.shape
    dma = pltpu.SemaphoreType.DMA
    window, chain = chain_scratch(images.shape[0], slabs, channels)
    field = jax.ShapeDtypeStruct(images.shape, F32)
    outs = (
        field,
        field,
        jax.ShapeDtypeStruct(kernels.shape, F32),
        jax.ShapeDtypeStruct((8, channels), F32),
        jax.ShapeDtypeStruct((slabs, channels, channels), F32),
        jax.ShapeDtypeStruct((channels, channels), F32),
    )
    anywhere = pl.BlockSpec(memory_space=pl.ANY)
    (vmem,) = in_vmem(1)
    return pl.pallas_call(
        functools.partial(forward_kernel, chips, ring, window),
        out_shape=outs,
        in_specs=in_vmem(3),
        out_specs=(vmem, anywhere, anywhere, vmem, anywhere, vmem),
        scratch_shapes=[
            pltpu.VMEM(images.shape, F32),
            pltpu.VMEM(kernels.shape, F32),
            pltpu.VMEM((slabs, channels, channels), F32),
            pltpu.VMEM(kernels.shape, F32),
            pltpu.VMEM((8, channels), F32),
            pltpu.VMEM(kernels.shape, F32),
            pltpu.VMEM((8, channels), F32),
            pltpu.VMEM((layers, depth // ring, channels), F32),
            pltpu.VMEM(images.shape, F32),
        ]
        + packed
        + weights
        + [dma((3,))]
        + [dma((layers,))] * 6
        + [dma((layers * ring,))] * 2
        + [dma, dma, dma((2,)), dma((2,))]
        + [dma((chips,))] * 4
        + [dma((ring - 1,))] * 2
        + [dma] * 2
        + chain,
        compiler_params=pltpu.CompilerParams(
            vmem_limit_bytes=VMEM_BYTES, collective_id=1, has_side_effects=True
        ),
        name="forward",
    )(images, kernels, damping)


def place_kernel(*refs):
    half = len(refs) // 2
    for source, target in zip(refs[:half], refs[half:]):
        target[...] = source[...]


def place(*arrays):
    parts = 2

    def specs():
        return [pl.BlockSpec((a.shape[0] // parts, a.shape[1]), lambda i: (i, 0)) for a in arrays]

    return pl.pallas_call(
        place_kernel,
        grid=(parts,),
        out_shape=[jax.ShapeDtypeStruct(a.shape, a.dtype) for a in arrays],
        in_specs=specs(),
        out_specs=specs(),
        compiler_params=pltpu.CompilerParams(vmem_limit_bytes=VMEM_BYTES),
        name="place",
    )(*arrays)


def run_final(tops, kernels, damping, matrix, back_offsets, gates, kept, ring, packed, weights):
    layers, depth, channels = kernels.shape
    moves = layers * 2 * (ring - 1)
    dma = pltpu.SemaphoreType.DMA
    state = jax.ShapeDtypeStruct(tops.shape, F32)
    anywhere = pl.BlockSpec(memory_space=pl.ANY)
    return pl.pallas_call(
        functools.partial(final_kernel, ring),
        out_shape=(state, state, jax.ShapeDtypeStruct(kernels.shape, F32)),
        in_specs=in_vmem(4) + [anywhere] * 3,
        out_specs=(anywhere,) * 3,
        scratch_shapes=packed
        + weights
        + [
            pltpu.VMEM(tops.shape, F32),
            pltpu.VMEM(gates.shape, F32),
            pltpu.VMEM(kept.shape, BF16),
            pltpu.VMEM(tops.shape, F32),
            pltpu.VMEM(tops.shape, F32),
            pltpu.VMEM(kernels.shape, F32),
            pltpu.VMEM(kernels.shape, F32),
            pltpu.VMEM((moves, depth // (2 * ring), channels), F32),
        ]
        + [dma((moves,))] * 4
        + [dma((2 * layers + 1,)), dma((layers + 2,))],
        compiler_params=pltpu.CompilerParams(
            vmem_limit_bytes=VMEM_BYTES, collective_id=4, has_side_effects=True
        ),
        name="final",
    )(tops, kernels, damping, matrix, back_offsets, gates, kept)


def per_device(images, kernels, damping, cotangent):
    slab, depth, channels = kernels.shape
    side = images.shape[1]
    slabs = lax.axis_size("layer")
    ring = lax.axis_size("dp")
    pairs = side // 2
    flat = (side * side, channels)
    images_flat, cot_flat = images.reshape(flat), cotangent.reshape(flat)
    packed = [pltpu.VMEM((3, 2, pairs + 1, side, channels), BF16)] * 2
    weights = [pltpu.VMEM((12 * channels, 2 * channels), BF16)]
    weights_back = [pltpu.VMEM((2 * channels, 12 * channels), BF16)]

    begins, offsets, after, damp_after, matrices, matrix = run_forward_kernel(
        images_flat, kernels, damping, slabs, ring, packed, weights
    )
    slab_end, coarse_end, back_offsets, gates, kept, tops = run_middle(
        begins, kernels, damping, damp_after, matrix, offsets, after, cot_flat, matrices, packed, weights + weights_back
    )
    adjoint_start, adjoint_coarse, grads = run_final(
        tops, kernels, damping, matrix, back_offsets, gates, kept, ring, packed, weights_back
    )
    slab_end, coarse_end, adjoint_start, adjoint_coarse, grads = place(
        slab_end, coarse_end, adjoint_start, adjoint_coarse, grads.reshape(slab * depth, channels)
    )
    full = (1,) + images.shape
    return (
        slab_end.reshape(full),
        coarse_end.reshape(full),
        adjoint_start.reshape(full),
        adjoint_coarse.reshape(full),
        grads.reshape(kernels.shape),
    )


def solution(mesh):
    in_specs = (
        P("dp", None, None, None),
        P("layer", None, None),
        P("layer", None),
        P("dp", None, None, None),
    )
    out_specs = (
        P("layer", "dp", None, None, None),
        P("layer", "dp", None, None, None),
        P("layer", "dp", None, None, None),
        P("layer", "dp", None, None, None),
        P("layer", None, None),
    )
    return jax.shard_map(
        per_device, mesh=mesh, in_specs=in_specs, out_specs=out_specs, check_vma=False
    )
```
